128 devices in a mesh: dev: 128 (over x, z, y, core).
Axes of the slice: x: 4, y: 4, z: 4, core: 2. Of those that a mesh axis runs over, the one named last changes fastest.
Arguments:
- entity_table: float32 [131072, 400], P('dev'), may hold values from -2.1 to 2.1
- entity_state: float32 [131072], P('dev'), may hold values from 0.01 to 1
- relation_table: float32 [7424, 400], P('dev'), may hold values from -3.6 to 3.6
- relation_state: float32 [7424], P('dev'), may hold values from 0.01 to 1
- heads: int32 [262144], P('dev'), may hold values from 0 to 1023
- relations: int32 [262144], P('dev'), may hold values from 0 to 7423
- tails: int32 [262144], P('dev'), may hold values from 0 to 3071, as said below
- pull_lists: int32 [16384, 16], P('dev'), may hold values from 0 to 1023, as said below
- negatives: int32 [1024], P('dev'), may hold values from 0 to 1023
Outputs:
- new_entity_table: float32 [131072, 400], P('dev')
- new_entity_state: float32 [131072], P('dev')
- new_relation_table: float32 [7424, 400], P('dev')
- new_relation_state: float32 [7424], P('dev')
The draws below stay inside these ranges and needn't reach their ends.
Inputs may be any that keep to these rules, and one draw needn't show every extreme that they name: `pull_lists`: for partitions q != p, the first c entries of row q * 128 + p are distinct rows that q needs, 1 <= c <= 16; the last partition and a partition drawn from the seed (possibly the same one) are asked for exactly 16 rows by every other partition; row q * 128 + q asks for nothing; entries past c are valid rows that no edge names. `tails`: A value below 1024 is a row of the edge's own partition; a value 1024 + p * 16 + j names entry j of the edge's partition's pull list to partition p, only entries in its first c; every such entry is named by some edge of that partition.
All inputs are finite; a program needn't handle non-finite values.
Results may differ from the reference program's by a relative error of at most 0.0001.
Values sent between devices are 32-bit elements; how exact they have to be, the bound alone decides.
No kernel may reach another device: no remote copies, remote signals or barrier semaphores. Data moves between devices by JAX's collectives and lax.ppermute only.
A program may use at most 192 MiB of HBM per device.

```python
import math
import jax
import jax.numpy as jnp
from jax import lax

W = 400
ENT_DEV = 1024
E_DEV = 2048
NEG_DEV = 8
CAP = 16
ENT = 131072
EDGES = 262144
NEG = 1024
REL = 7424
N_DEV = 128


def layout(key):
    base = jax.random.fold_in(key, 11)
    keys = jax.random.split(base, 5)
    count_dev = N_DEV
    counts = jax.random.randint(keys[0], (count_dev, count_dev), max(CAP // 2 - 2, 1), CAP + 1)
    busiest = jax.random.randint(keys[1], (), 0, count_dev)
    column = jnp.arange(count_dev)[None, :]
    rowpos = jnp.arange(count_dev)[:, None]
    counts = jnp.where((column == busiest) | (column == count_dev - 1), CAP, counts)
    counts = jnp.where(rowpos == column, 0, counts)
    offset = jax.random.randint(keys[2], (count_dev, count_dev, 1), 0, ENT_DEV)
    stride = 2 * jax.random.randint(keys[3], (count_dev, count_dev, 1), 0, max(ENT_DEV // 2, 1)) + 1
    places = jnp.arange(CAP)[None, None, :]
    lists = (offset + places * stride) % ENT_DEV
    lists = lists.at[0, 0, 0].set(ENT_DEV - 1).at[0, 0, 1].set(0)
    return (counts, lists, keys[4])


def draw_pull_lists(key, part):
    counts, lists, spare = layout(key)
    return lists.reshape(N_DEV * N_DEV, CAP).astype(jnp.int32)


def draw_tails(key, part):
    counts, lists, spare = layout(key)
    count_dev = N_DEV
    total_slots = count_dev * CAP

    def one_device(dev_key, dev_counts):
        live = (jnp.arange(CAP)[None, :] < dev_counts[:, None]).reshape(total_slots)
        places = jnp.arange(total_slots)
        order = jnp.argsort(jnp.where(live, places, places + total_slots))
        live_count = jnp.sum(live.astype(jnp.int32))
        subkeys = jax.random.split(dev_key, 4)
        edge_pos = jnp.arange(E_DEV)
        pick = jax.random.randint(subkeys[0], (E_DEV,), 0, 1 << 20) % jnp.maximum(live_count, 1)
        extra = jax.random.randint(subkeys[1], (E_DEV,), 0, 4) == 0
        local_rows = jax.random.randint(subkeys[2], (E_DEV,), 0, ENT_DEV)
        local_rows = jnp.where(edge_pos == E_DEV - 1, 0, local_rows)
        chosen = jnp.where(edge_pos < live_count, order[jnp.minimum(edge_pos, total_slots - 1)], order[pick])
        remote = ((edge_pos < live_count) | extra) & (edge_pos != E_DEV - 1)
        tail_vals = jnp.where(remote, ENT_DEV + chosen, local_rows)
        shuffle = jax.random.permutation(subkeys[3], E_DEV)
        return tail_vals[shuffle]
    result = jax.vmap(one_device)(jax.random.split(spare, count_dev), counts)
    return result.reshape(count_dev * E_DEV).astype(jnp.int32)


def set_ends(values, own_key, low, largest):
    longest = values.shape.index(max(values.shape))
    spots = []
    for shift in (0, 1):
        where = [jax.random.randint(jax.random.fold_in(own_key, axis), (), 0, length) for axis, length in enumerate(values.shape)]
        where[longest] = (where[longest] + shift) % values.shape[longest]
        spots.append(tuple(where))
    return values.at[spots[0]].set(low).at[spots[1]].set(largest)


def levels(stream_key, dims, cuts, least, high):
    def one(position, parts):
        heights = jax.random.uniform(jax.random.fold_in(jax.random.fold_in(stream_key, 6), position), (parts,), jnp.float32, least / len(cuts), high / len(cuts))
        return jnp.repeat(jnp.exp(heights), dims[position] // parts).reshape((-1,) + (1,) * (len(dims) - position - 1))

    factor_of = one(*cuts[0])
    for cut in cuts[1:]:
        factor_of = factor_of * one(*cut)
    return factor_of


def centred(key, dims, spread, bound, cuts=(), kind=jnp.bfloat16):
    values = spread * jax.random.normal(key, dims, jnp.float32)
    if cuts:
        values = values * levels(key, dims, cuts, -0.22, 0.18)
    return jnp.clip(values, -bound, bound).astype(kind)


def setup_inputs(seed: int = 0) -> dict:
    splits = jax.random.split(jax.random.key(seed), 10)
    entity_table = centred(splits[0], (ENT, W), 0.35, 2.1, ((0, 128),), jnp.float32)
    entity_state = jnp.clip(jnp.exp(math.log(1.0) - 4.6051702 * jax.random.uniform(splits[1], (ENT,), jnp.float32) ** levels(splits[1], (ENT,), ((0, 128),), -0.2, 0.2)), 0.01, 1.0)
    relation_table = centred(splits[2], (REL, W), 0.6, 3.6, ((0, 128),), jnp.float32)
    relation_state = jnp.clip(jnp.exp(math.log(1.0) - 4.6051702 * jax.random.uniform(splits[3], (REL,), jnp.float32) ** levels(splits[3], (REL,), ((0, 128),), -0.2, 0.2)), 0.01, 1.0)
    heads = set_ends(jax.random.randint(splits[4], (EDGES,), 0, ENT_DEV), jax.random.fold_in(splits[4], 1), 0, ENT_DEV - 1).astype(jnp.int32)
    relations = set_ends(jax.random.randint(splits[5], (EDGES,), 0, REL), jax.random.fold_in(splits[5], 1), 0, REL - 1).astype(jnp.int32)
    tails = draw_tails(jax.random.fold_in(splits[9], 71), 0)
    pull_lists = draw_pull_lists(jax.random.fold_in(splits[9], 71), 0)
    negatives = set_ends(jax.random.randint(splits[8], (NEG,), 0, ENT_DEV), jax.random.fold_in(splits[8], 1), 0, ENT_DEV - 1).astype(jnp.int32)
    return {"entity_table": entity_table, "entity_state": entity_state, "relation_table": relation_table, "relation_state": relation_state, "heads": heads, "relations": relations, "tails": tails, "pull_lists": pull_lists, "negatives": negatives}


highest = lax.Precision.HIGHEST
rate = 0.1

def complex_product(left, right):
    half = left.shape[1] // 2
    left_re, left_im = (left[:, :half], left[:, half:])
    right_re, right_im = (right[:, :half], right[:, half:])
    return jnp.concatenate([left_re * right_re - left_im * right_im, left_re * right_im + left_im * right_re], axis=1)

def conj_product(grads, other):
    half = grads.shape[1] // 2
    grad_re, grad_im = (grads[:, :half], grads[:, half:])
    other_re, other_im = (other[:, :half], other[:, half:])
    return jnp.concatenate([grad_re * other_re + grad_im * other_im, grad_im * other_re - grad_re * other_im], axis=1)

def edge_terms(head_rows, rel_rows, tail_rows, neg_rows):
    query = complex_product(head_rows, rel_rows)
    positive = lax.optimization_barrier(jnp.sum(query * tail_rows, axis=1))
    negative = lax.dot_general(query, neg_rows, (((1,), (1,)), ((), ())), precision=highest, preferred_element_type=jnp.float32)
    pos_grad = jax.nn.sigmoid(positive) - 1.0
    neg_grad = jax.nn.sigmoid(negative) / neg_rows.shape[0]
    query_grad = pos_grad[:, None] * tail_rows + jnp.dot(neg_grad, neg_rows, precision=highest, preferred_element_type=jnp.float32)
    tail_grad = pos_grad[:, None] * query
    negs_grad = lax.dot_general(neg_grad, query, (((0,), (0,)), ((), ())), precision=highest, preferred_element_type=jnp.float32)
    head_grad = conj_product(query_grad, rel_rows)
    rel_grad = conj_product(query_grad, head_rows)
    return (head_grad, rel_grad, tail_grad, negs_grad)

def adagrad(rows, state, grads):
    new_state = state + lax.optimization_barrier(jnp.mean(grads * grads, axis=1))
    return (rows - rate * grads / (jnp.sqrt(new_state)[:, None] + 1e-10), new_state)

def reference(entity_table, entity_state, relation_table, relation_state, heads, relations, tails, pull_lists, negatives):
    count_dev = N_DEV
    owner = jnp.arange(E_DEV * count_dev, dtype=jnp.int32) // E_DEV
    head_ids = owner * ENT_DEV + heads
    is_local = tails < ENT_DEV
    slot = jnp.maximum(tails - ENT_DEV, 0)
    peer = slot // CAP
    pulled = pull_lists[owner * count_dev + peer, slot % CAP]
    tail_ids = jnp.where(is_local, owner * ENT_DEV + tails, peer * ENT_DEV + pulled).astype(jnp.int32)
    neg_ids = (jnp.arange(NEG, dtype=jnp.int32) // NEG_DEV * ENT_DEV + negatives).astype(jnp.int32)
    neg_rows = entity_table[neg_ids]

    def block(index, carry):
        entity_grad, relation_grad, negative_grad = carry
        start = (index * E_DEV).astype(jnp.int32)
        head_here = lax.dynamic_slice_in_dim(head_ids, start, E_DEV)
        tail_here = lax.dynamic_slice_in_dim(tail_ids, start, E_DEV)
        rel_here = lax.dynamic_slice_in_dim(relations, start, E_DEV)
        head_grad, rel_grad, tail_grad, negs_grad = edge_terms(entity_table[head_here], relation_table[rel_here], entity_table[tail_here], neg_rows)
        entity_grad = entity_grad.at[head_here].add(head_grad).at[tail_here].add(tail_grad)
        relation_grad = relation_grad.at[rel_here].add(rel_grad)
        return (entity_grad, relation_grad, negative_grad + negs_grad)
    start_carry = (jnp.zeros(entity_table.shape, jnp.float32), jnp.zeros(relation_table.shape, jnp.float32), jnp.zeros(neg_rows.shape, jnp.float32))
    entity_grad, relation_grad, negative_grad = lax.fori_loop(0, count_dev, block, start_carry)
    entity_grad = entity_grad.at[neg_ids].add(negative_grad)
    new_entity_table, new_entity_state = adagrad(entity_table, entity_state, entity_grad)
    new_relation_table, new_relation_state = adagrad(relation_table, relation_state, relation_grad)
    return (new_entity_table, new_entity_state, new_relation_table, new_relation_state)
```

```python
import jax
import jax.numpy as jnp
from jax import lax
from jax.sharding import Mesh, PartitionSpec as P

highest = lax.Precision.HIGHEST
rate = 0.1


def complex_product(left, right):
    half = left.shape[1] // 2
    left_re, left_im = (left[:, :half], left[:, half:])
    right_re, right_im = (right[:, :half], right[:, half:])
    return jnp.concatenate(
        [left_re * right_re - left_im * right_im, left_re * right_im + left_im * right_re], axis=1
    )


def conj_product(grads, other):
    half = grads.shape[1] // 2
    grad_re, grad_im = (grads[:, :half], grads[:, half:])
    other_re, other_im = (other[:, :half], other[:, half:])
    return jnp.concatenate(
        [grad_re * other_re + grad_im * other_im, grad_im * other_re - grad_re * other_im], axis=1
    )


def edge_terms(head_rows, rel_rows, tail_rows, neg_rows):
    query = complex_product(head_rows, rel_rows)
    positive = jnp.sum(query * tail_rows, axis=1)
    negative = lax.dot_general(
        query,
        neg_rows,
        (((1,), (1,)), ((), ())),
        precision=highest,
        preferred_element_type=jnp.float32,
    )
    pos_grad = jax.nn.sigmoid(positive) - 1.0
    neg_grad = jax.nn.sigmoid(negative) / neg_rows.shape[0]
    query_grad = pos_grad[:, None] * tail_rows + jnp.dot(
        neg_grad, neg_rows, precision=highest, preferred_element_type=jnp.float32
    )
    tail_grad = pos_grad[:, None] * query
    negs_grad = lax.dot_general(
        neg_grad,
        query,
        (((0,), (0,)), ((), ())),
        precision=highest,
        preferred_element_type=jnp.float32,
    )
    head_grad = conj_product(query_grad, rel_rows)
    rel_grad = conj_product(query_grad, head_rows)
    return (head_grad, rel_grad, tail_grad, negs_grad)


def adagrad(rows, state, grads):
    new_state = state + jnp.mean(grads * grads, axis=1)
    return (rows - rate * grads / (jnp.sqrt(new_state)[:, None] + 1e-10), new_state)


AXES = ("x", "z", "y", "c")


def local(
    entity_table,
    entity_state,
    relation_table,
    relation_state,
    heads,
    relations,
    tails,
    pull_lists,
    negatives,
):
    ent_rows, width = entity_table.shape
    rel_rows = relation_table.shape[0]
    neg_count = negatives.shape[0]
    per = rel_rows + neg_count
    neg_local = entity_table[negatives]
    shared = lax.all_gather(
        jnp.concatenate([relation_table, neg_local], axis=0), AXES, axis=0, tiled=False
    )
    n_dev = shared.shape[0]
    asked = lax.all_to_all(pull_lists, AXES, split_axis=0, concat_axis=0, tiled=True)
    rows_out = entity_table[asked]
    fetched = lax.all_to_all(rows_out, AXES, split_axis=0, concat_axis=0, tiled=True)
    slots_total = fetched.shape[0] * fetched.shape[1]
    extended = jnp.concatenate([entity_table, fetched.reshape(slots_total, width)], axis=0)
    neg_rows = shared[:, rel_rows:].reshape(n_dev * neg_count, width)
    rel_here = shared[relations // rel_rows, relations % rel_rows]
    head_grad, rel_grad, tail_grad, negs_grad = edge_terms(
        entity_table[heads], rel_here, extended[tails], neg_rows
    )
    extended_grad = jnp.zeros(extended.shape, jnp.float32).at[tails].add(tail_grad)
    local_grad = extended_grad[:ent_rows].at[heads].add(head_grad)
    outgoing = extended_grad[ent_rows:].reshape(fetched.shape)
    returned = lax.all_to_all(outgoing, AXES, split_axis=0, concat_axis=0, tiled=True)
    local_grad = local_grad.at[asked.reshape(slots_total)].add(returned.reshape(slots_total, width))
    owner = relations // rel_rows
    chips = n_dev // 2
    shared_grad = jnp.zeros((2, chips, per, width), jnp.float32)
    shared_grad = shared_grad.at[:, :, rel_rows:].set(
        negs_grad.reshape(chips, 2, neg_count, width).swapaxes(0, 1)
    )
    shared_grad = shared_grad.at[owner % 2, owner // 2, relations % rel_rows].add(rel_grad)
    core = lax.axis_index("c")
    other = lax.ppermute(
        lax.dynamic_index_in_dim(shared_grad, 1 - core, 0, keepdims=False), "c", [(0, 1), (1, 0)]
    )
    paired = lax.dynamic_index_in_dim(shared_grad, core, 0, keepdims=False) + other
    share = jnp.sum(lax.all_to_all(paired, AXES[:3], split_axis=0, concat_axis=0, tiled=True), axis=0)
    rel_share, neg_share = share[:rel_rows], share[rel_rows:]
    local_grad = local_grad.at[negatives].add(neg_share)
    new_entity_table, new_entity_state = adagrad(entity_table, entity_state, local_grad)
    new_relation_table, new_relation_state = adagrad(relation_table, relation_state, rel_share)
    return (new_entity_table, new_entity_state, new_relation_table, new_relation_state)


def solution(mesh):
    grid = Mesh(mesh.devices.reshape(4, 4, 4, 2), AXES)
    rows, flat = P(AXES, None), P(AXES)
    in_specs = (rows, flat, rows, flat, flat, flat, flat, rows, flat)
    out_specs = (rows, flat, rows, flat)
    return jax.shard_map(local, mesh=grid, in_specs=in_specs, out_specs=out_specs, check_vma=False)
```

```python
import jax
import jax.numpy as jnp
from jax import lax
from jax.experimental import pallas as pl
from jax.experimental.pallas import tpu as pltpu
from jax.sharding import Mesh, PartitionSpec as P

rate = 0.1
AXES = ("x", "z", "y", "c")
WIDTH = 400
HALF = 200
LANES = 128
CHUNKS = 4
SPANS = ((0, 128), (128, 72), (200, 128), (328, 72))
ENT_DEV = 1024
REL_DEV = 58
NEG_DEV = 8
E_DEV = 2048
N_DEV = 128
CAP = 16
NEG = N_DEV * NEG_DEV
SLOTS = N_DEV * CAP
CHIPS = N_DEV // 2
PER = CHUNKS * (REL_DEV + NEG_DEV)
REL4 = CHUNKS * REL_DEV
TILE = 256
UNROLL = 8

f32 = jnp.float32
bf16 = jnp.bfloat16
VMEM = pl.BlockSpec(memory_space=pltpu.VMEM)
SMEM = pl.BlockSpec(memory_space=pltpu.SMEM)
ANY = pl.BlockSpec(memory_space=pl.ANY)


def params(mib):
    return pltpu.CompilerParams(vmem_limit_bytes=mib * 1024 * 1024)


def cost(flops, moved):
    return pl.CostEstimate(flops=flops, bytes_accessed=moved, transcendentals=0)


def chunk_of(ref, c, n):
    return ref[pl.ds(c, n, stride=CHUNKS), :]


def row(i):
    return pl.ds(pl.multiple_of(i * CHUNKS, CHUNKS), CHUNKS)


def split(x):
    hi = x.astype(bf16)
    return hi, (x - hi.astype(f32)).astype(bf16)


def dot3(a, b, dims):
    (ah, al), (bh, bl) = a, b

    def one(p, q):
        return lax.dot_general(p, q, (dims, ((), ())), preferred_element_type=f32)

    return one(ah, bh) + (one(ah, bl) + one(al, bh))


def rows_loop(n, body):
    def step(s, carry):
        for u in range(UNROLL):
            body(s * UNROLL + u)
        return carry

    lax.fori_loop(0, n // UNROLL, step, 0)


def to_chunks(src, dst, n):
    for c, (start, size) in enumerate(SPANS):
        piece = src[start : start + size, :]
        if size < LANES:
            piece = jnp.concatenate([piece, jnp.zeros((LANES - size, n), f32)], axis=0)
        dst[pl.ds(c, n, stride=CHUNKS), :] = piece.T


def prep_kernel(negatives, table_t, rel_t, tab4, ag4, rel4):
    to_chunks(table_t, tab4, ENT_DEV)
    to_chunks(rel_t, rel4, LANES)
    ag4[0:REL4, :] = rel4[0:REL4, :]
    for i in range(NEG_DEV):
        ag4[REL4 + CHUNKS * i : REL4 + CHUNKS * (i + 1), :] = tab4[row(negatives[i]), :]


def prep(negatives, table_t, rel_t):
    return pl.pallas_call(
        prep_kernel,
        out_shape=(
            jax.ShapeDtypeStruct((ENT_DEV * CHUNKS, LANES), f32),
            jax.ShapeDtypeStruct((PER, LANES), f32),
        ),
        in_specs=[SMEM, VMEM, VMEM],
        out_specs=(VMEM, VMEM),
        scratch_shapes=[pltpu.VMEM((LANES * CHUNKS, LANES), f32)],
        compiler_params=params(24),
        cost_estimate=cost(0, 8 << 20),
        name="prep",
    )(negatives, table_t, rel_t)


def pull_kernel(asked, tab4, out):
    def body(i):
        out[row(i), :] = tab4[row(asked[i]), :]

    rows_loop(SLOTS, body)


def pull_rows(asked, tab4):
    return pl.pallas_call(
        pull_kernel,
        out_shape=jax.ShapeDtypeStruct((SLOTS * CHUNKS, LANES), f32),
        in_specs=[SMEM, VMEM],
        out_specs=VMEM,
        compiler_params=params(24),
        cost_estimate=cost(0, 8 << 20),
        name="pull_rows",
    )(asked, tab4)


def query_kernel(
    heads, rel_at, tails, tab4, fetched, shared,
    q_out, h_out, r_out, p_out, ext_grad_out,
    ext, rel, ext_grad, hb, rb, tb, sems,
):
    step = pl.program_id(0)
    local = ENT_DEV * CHUNKS

    @pl.when(step == 0)
    def _():
        loads = (
            pltpu.make_async_copy(tab4, ext.at[pl.ds(0, local)], sems.at[0]),
            pltpu.make_async_copy(fetched, ext.at[pl.ds(local, SLOTS * CHUNKS)], sems.at[1]),
            pltpu.make_async_copy(shared, rel, sems.at[2]),
        )
        for load in loads:
            load.start()
        ext_grad[...] = jnp.zeros_like(ext_grad)
        for load in loads:
            load.wait()

    base = step * TILE

    def gather(i):
        hb[row(i), :] = ext[row(heads[base + i]), :]
        rb[row(i), :] = rel[row(rel_at[base + i]), :]
        tb[row(i), :] = ext[row(tails[base + i]), :]

    rows_loop(TILE, gather)
    h = [chunk_of(hb, c, TILE) for c in range(CHUNKS)]
    r = [chunk_of(rb, c, TILE) for c in range(CHUNKS)]
    t = [chunk_of(tb, c, TILE) for c in range(CHUNKS)]
    q = [h[0] * r[0] - h[2] * r[2], h[1] * r[1] - h[3] * r[3], h[0] * r[2] + h[2] * r[0], h[1] * r[3] + h[3] * r[1]]
    score = (q[0] * t[0] + q[1] * t[1]) + (q[2] * t[2] + q[3] * t[3])
    pos_grad = jax.nn.sigmoid(jnp.sum(score, axis=1, keepdims=True)) - 1.0
    for c in range(CHUNKS):
        q_out[c] = q[c]
        h_out[c] = h[c]
        r_out[c] = r[c]
        p_out[c] = pos_grad * t[c]
        hb[pl.ds(c, TILE, stride=CHUNKS), :] = pos_grad * q[c]

    def scatter(i):
        at = row(tails[base + i])
        ext_grad[at, :] = ext_grad[at, :] + hb[row(i), :]

    rows_loop(TILE, scatter)

    @pl.when(step == E_DEV // TILE - 1)
    def _():
        store = pltpu.make_async_copy(ext_grad, ext_grad_out, sems.at[0])
        store.start()
        store.wait()


def queries(heads, rel_at, tails, tab4, fetched, shared):
    plane = jax.ShapeDtypeStruct((CHUNKS, E_DEV, LANES), f32)
    block = pl.BlockSpec((CHUNKS, TILE, LANES), lambda i: (0, i, 0))
    ext_rows = (ENT_DEV + SLOTS) * CHUNKS
    return pl.pallas_call(
        query_kernel,
        grid=(E_DEV // TILE,),
        out_shape=(plane, plane, plane, plane, jax.ShapeDtypeStruct((ext_rows, LANES), f32)),
        in_specs=[SMEM, SMEM, SMEM, ANY, ANY, ANY],
        out_specs=(block, block, block, block, ANY),
        scratch_shapes=[
            pltpu.VMEM((ext_rows, LANES), f32),
            pltpu.VMEM((N_DEV * PER, LANES), f32),
            pltpu.VMEM((ext_rows, LANES), f32),
            pltpu.VMEM((TILE * CHUNKS, LANES), f32),
            pltpu.VMEM((TILE * CHUNKS, LANES), f32),
            pltpu.VMEM((TILE * CHUNKS, LANES), f32),
            pltpu.SemaphoreType.DMA((3,)),
        ],
        compiler_params=params(44),
        cost_estimate=cost(0, 60 << 20),
        name="queries",
    )(heads, rel_at, tails, tab4, fetched, shared)


def grads_kernel(
    heads, grad_at, core, shared, local_grad, q_in, h_in, r_in, p_in,
    mine, other, head_grad,
    negs, n_hi, n_lo, t_hi, t_lo, neg_acc, rel_grad, hb, rb, sems,
):
    step = pl.program_id(0)

    @pl.when(step == 0)
    def _():
        load = pltpu.make_async_copy(shared.at[:, pl.ds(REL4, PER - REL4), :], negs, sems.at[0])
        load.start()
        start = pltpu.make_async_copy(local_grad.at[pl.ds(0, ENT_DEV * CHUNKS)], head_grad, sems.at[1])
        start.start()
        rel_grad[...] = jnp.zeros_like(rel_grad)
        neg_acc[...] = jnp.zeros_like(neg_acc)
        load.wait()
        flat = negs.reshape(NEG * CHUNKS, LANES)
        for c in range(CHUNKS):
            lanes = slice(c * LANES, (c + 1) * LANES)
            piece = chunk_of(flat, c, NEG)
            n_hi[:, lanes], n_lo[:, lanes] = split(piece)
            t_hi[lanes, :], t_lo[lanes, :] = split(piece.T)
        start.wait()

    base = step * TILE
    q = split(jnp.concatenate([q_in[c] for c in range(CHUNKS)], axis=1))
    negative = dot3(q, (t_hi[...], t_lo[...]), ((1,), (0,)))
    neg_grad = split(jax.nn.sigmoid(negative) * (1.0 / NEG))
    neg_acc[...] += dot3(neg_grad, q, ((0,), (0,)))
    back = dot3(neg_grad, (n_hi[...], n_lo[...]), ((1,), (0,)))
    g = [p_in[c] + back[:, c * LANES : (c + 1) * LANES] for c in range(CHUNKS)]
    for k in range(2):
        for buf, src in ((hb, r_in), (rb, h_in)):
            buf[pl.ds(k, TILE, stride=CHUNKS), :] = g[k] * src[k] + g[k + 2] * src[k + 2]
            buf[pl.ds(k + 2, TILE, stride=CHUNKS), :] = g[k + 2] * src[k] - g[k] * src[k + 2]

    def scatter(i):
        at = row(heads[base + i])
        rel = row(grad_at[base + i])
        head_grad[at, :] = head_grad[at, :] + hb[row(i), :]
        rel_grad[rel, :] = rel_grad[rel, :] + rb[row(i), :]

    rows_loop(TILE, scatter)

    @pl.when(step == E_DEV // TILE - 1)
    def _():
        def place(d, carry):
            spot = ((d % 2) * CHIPS + d // 2) * PER + REL4
            rows = pl.ds(pl.multiple_of(d * NEG_DEV, NEG_DEV), NEG_DEV)
            for c in range(CHUNKS):
                rel_grad[pl.ds(spot + c, NEG_DEV, stride=CHUNKS), :] = neg_acc[rows, c * LANES : (c + 1) * LANES]
            return carry

        lax.fori_loop(0, N_DEV, place, 0)
        side = core[0]
        half = CHIPS * PER
        stores = (
            pltpu.make_async_copy(rel_grad.at[pl.ds(pl.multiple_of((1 - side) * half, 8), half)], other, sems.at[0]),
            pltpu.make_async_copy(rel_grad.at[pl.ds(pl.multiple_of(side * half, 8), half)], mine, sems.at[1]),
        )
        for store in stores:
            store.start()
        for store in stores:
            store.wait()


def gradients(heads, grad_at, core, shared, ext_grad, q, h, r, p):
    block = pl.BlockSpec((CHUNKS, TILE, LANES), lambda i: (0, i, 0))
    half = jax.ShapeDtypeStruct((CHIPS * PER, LANES), f32)
    whole = pl.BlockSpec((ENT_DEV * CHUNKS, LANES), lambda i: (0, 0))
    return pl.pallas_call(
        grads_kernel,
        grid=(E_DEV // TILE,),
        out_shape=(half, half, jax.ShapeDtypeStruct((ENT_DEV * CHUNKS, LANES), f32)),
        in_specs=[SMEM, SMEM, SMEM, ANY, ANY, block, block, block, block],
        out_specs=(ANY, ANY, whole),
        scratch_shapes=[
            pltpu.VMEM((N_DEV, PER - REL4, LANES), f32),
            pltpu.VMEM((NEG, CHUNKS * LANES), bf16),
            pltpu.VMEM((NEG, CHUNKS * LANES), bf16),
            pltpu.VMEM((CHUNKS * LANES, NEG), bf16),
            pltpu.VMEM((CHUNKS * LANES, NEG), bf16),
            pltpu.VMEM((NEG, CHUNKS * LANES), f32),
            pltpu.VMEM((N_DEV * PER, LANES), f32),
            pltpu.VMEM((TILE * CHUNKS, LANES), f32),
            pltpu.VMEM((TILE * CHUNKS, LANES), f32),
            pltpu.SemaphoreType.DMA((2,)),
        ],
        compiler_params=params(52),
        cost_estimate=cost(36_000_000_000, 60 << 20),
        name="gradients",
    )(heads, grad_at, core, shared, ext_grad, q, h, r, p)


def returned_kernel(asked, returned, head_grad, out):
    out[...] = head_grad[...]

    def body(i):
        at = row(asked[i])
        out[at, :] = out[at, :] + returned[row(i), :]

    rows_loop(SLOTS, body)


def add_returned(asked, returned, head_grad):
    return pl.pallas_call(
        returned_kernel,
        out_shape=jax.ShapeDtypeStruct((ENT_DEV * CHUNKS, LANES), f32),
        in_specs=[SMEM, VMEM, VMEM],
        out_specs=VMEM,
        compiler_params=params(24),
        cost_estimate=cost(0, 10 << 20),
        name="add_returned",
    )(asked, returned, head_grad)


def adagrad(grad, n, table_t, state, new_table_t, new_state):
    g = [chunk_of(grad, c, n).T for c in range(CHUNKS)]
    squares = (g[0] * g[0] + g[1] * g[1]) + (g[2] * g[2] + g[3] * g[3])
    state_now = state[...] + jnp.sum(squares, axis=0, keepdims=True) * (1.0 / WIDTH)
    new_state[...] = state_now
    below = jnp.sqrt(state_now) + 1e-10
    for c, (start, size) in enumerate(SPANS):
        spot = slice(start, start + size)
        new_table_t[spot, :] = table_t[spot, :] - rate * g[c][:size] / below


def step_kernel(
    negatives, local_grad, parts, table_t, state, rel_t, rel_state,
    new_table_t, new_state, new_rel_t, new_rel_state,
    grad, share,
):
    grad[...] = local_grad[...]
    share[...] = jnp.zeros_like(share)
    share[0:PER, :] = jnp.sum(parts[...], axis=0)
    for i in range(NEG_DEV):
        at = row(negatives[i])
        grad[at, :] = grad[at, :] + share[REL4 + CHUNKS * i : REL4 + CHUNKS * (i + 1), :]
    adagrad(grad, ENT_DEV, table_t, state, new_table_t, new_state)
    adagrad(share, LANES, rel_t, rel_state, new_rel_t, new_rel_state)


def adagrad_step(negatives, local_grad, parts, table_t, state, rel_t, rel_state):
    def like(*shape):
        return jax.ShapeDtypeStruct(shape, f32)

    return pl.pallas_call(
        step_kernel,
        out_shape=(like(WIDTH, ENT_DEV), like(1, ENT_DEV), like(WIDTH, LANES), like(1, LANES)),
        in_specs=[SMEM] + [VMEM] * 6,
        out_specs=(VMEM,) * 4,
        scratch_shapes=[
            pltpu.VMEM((ENT_DEV * CHUNKS, LANES), f32),
            pltpu.VMEM((CHUNKS * LANES, LANES), f32),
        ],
        compiler_params=params(40),
        cost_estimate=cost(0, 16 << 20),
        name="adagrad_step",
    )(negatives, local_grad, parts, table_t, state, rel_t, rel_state)


def local(
    entity_table,
    entity_state,
    relation_table,
    relation_state,
    heads,
    relations,
    tails,
    pull_lists,
    negatives,
):
    table_t = entity_table.T
    rel_t = jnp.pad(relation_table, ((0, LANES - REL_DEV), (0, 0))).T
    owner, place = relations // REL_DEV, relations % REL_DEV
    rel_at = owner * (REL_DEV + NEG_DEV) + place
    grad_at = ((owner % 2) * CHIPS + owner // 2) * (REL_DEV + NEG_DEV) + place
    core = lax.axis_index("c")

    tab4, ag4 = prep(negatives, table_t, rel_t)
    shared = lax.all_gather(ag4, AXES, axis=0, tiled=True)
    asked = lax.all_to_all(pull_lists, AXES, split_axis=0, concat_axis=0, tiled=True).reshape(SLOTS)
    rows_out = pull_rows(asked, tab4)

    def exchange(rows):
        rows = rows.reshape(N_DEV, CAP * CHUNKS, LANES)
        return lax.all_to_all(rows, AXES, split_axis=0, concat_axis=0, tiled=True).reshape(SLOTS * CHUNKS, LANES)

    fetched = exchange(rows_out)
    q, h, r, p, ext_grad = queries(heads, rel_at, tails, tab4, fetched, shared)
    returned = exchange(ext_grad[ENT_DEV * CHUNKS :])
    mine, other, head_grad = gradients(
        heads, grad_at, core.reshape(1), shared.reshape(N_DEV, PER, LANES), ext_grad, q, h, r, p
    )
    paired = mine + lax.ppermute(other, "c", [(0, 1), (1, 0)])
    parts = lax.all_to_all(
        paired.reshape(CHIPS, PER, LANES), AXES[:3], split_axis=0, concat_axis=0, tiled=True
    )
    local_grad = add_returned(asked, returned, head_grad)
    new_table_t, new_state, new_rel_t, new_rel_state = adagrad_step(
        negatives,
        local_grad,
        parts,
        table_t,
        entity_state.reshape(1, ENT_DEV),
        rel_t,
        jnp.pad(relation_state, (0, LANES - REL_DEV)).reshape(1, LANES),
    )
    return (
        new_table_t.T,
        new_state.reshape(ENT_DEV),
        new_rel_t.T[:REL_DEV],
        new_rel_state.reshape(LANES)[:REL_DEV],
    )


def solution(mesh):
    grid = Mesh(mesh.devices.reshape(4, 4, 4, 2), AXES)
    rows, flat = P(AXES, None), P(AXES)
    in_specs = (rows, flat, rows, flat, flat, flat, flat, rows, flat)
    out_specs = (rows, flat, rows, flat)
    return jax.shard_map(local, mesh=grid, in_specs=in_specs, out_specs=out_specs, check_vma=False)
```

```python
import jax
import jax.numpy as jnp
from jax import lax
from jax.experimental import pallas as pl
from jax.experimental.pallas import tpu as pltpu
from jax.sharding import Mesh, PartitionSpec as P

rate = 0.1
AXES = ("x", "z", "y", "c")
WIDTH = 400
HALF = 200
LANES = 128
CHUNKS = 4
SPANS = ((0, 128), (128, 72), (200, 128), (328, 72))
ENT_DEV = 1024
REL_DEV = 58
NEG_DEV = 8
E_DEV = 2048
N_DEV = 128
CAP = 16
NEG = N_DEV * NEG_DEV
SLOTS = N_DEV * CAP
CHIPS = N_DEV // 2
PER = CHUNKS * (REL_DEV + NEG_DEV)
REL4 = CHUNKS * REL_DEV
TILE = 256
UNROLL = 8

f32 = jnp.float32
bf16 = jnp.bfloat16
VMEM = pl.BlockSpec(memory_space=pltpu.VMEM)
SMEM = pl.BlockSpec(memory_space=pltpu.SMEM)
ANY = pl.BlockSpec(memory_space=pl.ANY)


def params(mib):
    return pltpu.CompilerParams(vmem_limit_bytes=mib * 1024 * 1024)


def cost(flops, moved):
    return pl.CostEstimate(flops=flops, bytes_accessed=moved, transcendentals=0)


def chunk_of(ref, c, n):
    return ref[pl.ds(c, n, stride=CHUNKS), :]


def row(i):
    return pl.ds(pl.multiple_of(i * CHUNKS, CHUNKS), CHUNKS)


def split(x):
    hi = x.astype(bf16)
    return hi, (x - hi.astype(f32)).astype(bf16)


def dot3(a, b, dims):
    (ah, al), (bh, bl) = a, b

    def one(p, q):
        return lax.dot_general(p, q, (dims, ((), ())), preferred_element_type=f32)

    return one(ah, bh) + (one(ah, bl) + one(al, bh))


def rows_loop(n, body):
    def step(s, carry):
        for u in range(UNROLL):
            body(s * UNROLL + u)
        return carry

    lax.fori_loop(0, n // UNROLL, step, 0)


def to_chunks(src, dst, n):
    for c, (start, size) in enumerate(SPANS):
        piece = src[start : start + size, :]
        if size < LANES:
            piece = jnp.concatenate([piece, jnp.zeros((LANES - size, n), f32)], axis=0)
        dst[pl.ds(c, n, stride=CHUNKS), :] = piece.T


def prep_kernel(negatives, table_t, rel_t, tab4, ag4, rel4):
    to_chunks(table_t, tab4, ENT_DEV)
    to_chunks(rel_t, rel4, LANES)
    ag4[0:REL4, :] = rel4[0:REL4, :]
    for i in range(NEG_DEV):
        ag4[REL4 + CHUNKS * i : REL4 + CHUNKS * (i + 1), :] = tab4[row(negatives[i]), :]


def prep(negatives, table_t, rel_t):
    return pl.pallas_call(
        prep_kernel,
        out_shape=(
            jax.ShapeDtypeStruct((ENT_DEV * CHUNKS, LANES), f32),
            jax.ShapeDtypeStruct((PER, LANES), f32),
        ),
        in_specs=[SMEM, VMEM, VMEM],
        out_specs=(VMEM, VMEM),
        scratch_shapes=[pltpu.VMEM((LANES * CHUNKS, LANES), f32)],
        compiler_params=params(24),
        cost_estimate=cost(0, 8 << 20),
        name="prep",
    )(negatives, table_t, rel_t)


def pull_kernel(asked, tab4, out):
    def body(i):
        out[row(i), :] = tab4[row(asked[i]), :]

    rows_loop(SLOTS, body)


def pull_rows(asked, tab4):
    return pl.pallas_call(
        pull_kernel,
        out_shape=jax.ShapeDtypeStruct((SLOTS * CHUNKS, LANES), f32),
        in_specs=[SMEM, VMEM],
        out_specs=VMEM,
        compiler_params=params(24),
        cost_estimate=cost(0, 8 << 20),
        name="pull_rows",
    )(asked, tab4)


def ends_kernel(heads, tails, tab4, fetched, h_out, t_out, ext, hb, tb, sems):
    step = pl.program_id(0)
    local = ENT_DEV * CHUNKS

    @pl.when(step == 0)
    def _():
        loads = (
            pltpu.make_async_copy(tab4, ext.at[pl.ds(0, local)], sems.at[0]),
            pltpu.make_async_copy(fetched, ext.at[pl.ds(local, SLOTS * CHUNKS)], sems.at[1]),
        )
        for load in loads:
            load.start()
        for load in loads:
            load.wait()

    base = step * TILE

    def gather(i):
        hb[row(i), :] = ext[row(heads[base + i]), :]
        tb[row(i), :] = ext[row(tails[base + i]), :]

    rows_loop(TILE, gather)
    for c in range(CHUNKS):
        h_out[c] = chunk_of(hb, c, TILE)
        t_out[c] = chunk_of(tb, c, TILE)


def ends(heads, tails, tab4, fetched):
    plane = jax.ShapeDtypeStruct((CHUNKS, E_DEV, LANES), f32)
    block = pl.BlockSpec((CHUNKS, TILE, LANES), lambda i: (0, i, 0))
    return pl.pallas_call(
        ends_kernel,
        grid=(E_DEV // TILE,),
        out_shape=(plane, plane),
        in_specs=[SMEM, SMEM, ANY, ANY],
        out_specs=(block, block),
        scratch_shapes=[
            pltpu.VMEM(((ENT_DEV + SLOTS) * CHUNKS, LANES), f32),
            pltpu.VMEM((TILE * CHUNKS, LANES), f32),
            pltpu.VMEM((TILE * CHUNKS, LANES), f32),
            pltpu.SemaphoreType.DMA((2,)),
        ],
        compiler_params=params(24),
        cost_estimate=cost(0, 30 << 20),
        name="ends",
    )(heads, tails, tab4, fetched)


def query_kernel(
    rel_at, tails, shared, h_in, t_in,
    q_out, r_out, p_out, tail_local, outgoing,
    rel, ext_grad, hb, rb, sems,
):
    step = pl.program_id(0)

    @pl.when(step == 0)
    def _():
        load = pltpu.make_async_copy(shared, rel, sems.at[0])
        load.start()
        ext_grad[...] = jnp.zeros_like(ext_grad)
        load.wait()

    base = step * TILE

    def gather(i):
        rb[row(i), :] = rel[row(rel_at[base + i]), :]

    rows_loop(TILE, gather)
    h = [h_in[c] for c in range(CHUNKS)]
    r = [chunk_of(rb, c, TILE) for c in range(CHUNKS)]
    t = [t_in[c] for c in range(CHUNKS)]
    q = [h[0] * r[0] - h[2] * r[2], h[1] * r[1] - h[3] * r[3], h[0] * r[2] + h[2] * r[0], h[1] * r[3] + h[3] * r[1]]
    score = (q[0] * t[0] + q[1] * t[1]) + (q[2] * t[2] + q[3] * t[3])
    pos_grad = jax.nn.sigmoid(jnp.sum(score, axis=1, keepdims=True)) - 1.0
    for c in range(CHUNKS):
        q_out[c] = q[c]
        r_out[c] = r[c]
        p_out[c] = pos_grad * t[c]
        hb[pl.ds(c, TILE, stride=CHUNKS), :] = pos_grad * q[c]

    def scatter(i):
        at = row(tails[base + i])
        ext_grad[at, :] = ext_grad[at, :] + hb[row(i), :]

    rows_loop(TILE, scatter)

    @pl.when(step == E_DEV // TILE - 1)
    def _():
        local = ENT_DEV * CHUNKS
        stores = (
            pltpu.make_async_copy(ext_grad.at[pl.ds(0, local)], tail_local, sems.at[0]),
            pltpu.make_async_copy(ext_grad.at[pl.ds(local, SLOTS * CHUNKS)], outgoing, sems.at[1]),
        )
        for store in stores:
            store.start()
        for store in stores:
            store.wait()


def queries(rel_at, tails, shared, h, t):
    plane = jax.ShapeDtypeStruct((CHUNKS, E_DEV, LANES), f32)
    block = pl.BlockSpec((CHUNKS, TILE, LANES), lambda i: (0, i, 0))
    return pl.pallas_call(
        query_kernel,
        grid=(E_DEV // TILE,),
        out_shape=(
            plane,
            plane,
            plane,
            jax.ShapeDtypeStruct((ENT_DEV * CHUNKS, LANES), f32),
            jax.ShapeDtypeStruct((SLOTS * CHUNKS, LANES), f32),
        ),
        in_specs=[SMEM, SMEM, ANY, block, block],
        out_specs=(block, block, block, ANY, ANY),
        scratch_shapes=[
            pltpu.VMEM((N_DEV * PER, LANES), f32),
            pltpu.VMEM(((ENT_DEV + SLOTS) * CHUNKS, LANES), f32),
            pltpu.VMEM((TILE * CHUNKS, LANES), f32),
            pltpu.VMEM((TILE * CHUNKS, LANES), f32),
            pltpu.SemaphoreType.DMA((2,)),
        ],
        compiler_params=params(40),
        cost_estimate=cost(0, 60 << 20),
        name="queries",
    )(rel_at, tails, shared, h, t)


def grads_kernel(
    heads, grad_at, core, shared, local_grad, q_in, h_in, r_in, p_in,
    mine, other, head_grad,
    negs, n_hi, n_lo, t_hi, t_lo, neg_acc, rel_grad, hb, rb, sems,
):
    step = pl.program_id(0)

    @pl.when(step == 0)
    def _():
        load = pltpu.make_async_copy(shared.at[:, pl.ds(REL4, PER - REL4), :], negs, sems.at[0])
        load.start()
        start = pltpu.make_async_copy(local_grad, head_grad, sems.at[1])
        start.start()
        rel_grad[...] = jnp.zeros_like(rel_grad)
        neg_acc[...] = jnp.zeros_like(neg_acc)
        load.wait()
        flat = negs.reshape(NEG * CHUNKS, LANES)
        for c in range(CHUNKS):
            lanes = slice(c * LANES, (c + 1) * LANES)
            piece = chunk_of(flat, c, NEG)
            n_hi[:, lanes], n_lo[:, lanes] = split(piece)
            t_hi[lanes, :], t_lo[lanes, :] = split(piece.T)
        start.wait()

    base = step * TILE
    q = split(jnp.concatenate([q_in[c] for c in range(CHUNKS)], axis=1))
    negative = dot3(q, (t_hi[...], t_lo[...]), ((1,), (0,)))
    neg_grad = split(jax.nn.sigmoid(negative) * (1.0 / NEG))
    neg_acc[...] += dot3(neg_grad, q, ((0,), (0,)))
    back = dot3(neg_grad, (n_hi[...], n_lo[...]), ((1,), (0,)))
    g = [p_in[c] + back[:, c * LANES : (c + 1) * LANES] for c in range(CHUNKS)]
    for k in range(2):
        for buf, src in ((hb, r_in), (rb, h_in)):
            buf[pl.ds(k, TILE, stride=CHUNKS), :] = g[k] * src[k] + g[k + 2] * src[k + 2]
            buf[pl.ds(k + 2, TILE, stride=CHUNKS), :] = g[k + 2] * src[k] - g[k] * src[k + 2]

    def scatter(i):
        at = row(heads[base + i])
        rel = row(grad_at[base + i])
        head_grad[at, :] = head_grad[at, :] + hb[row(i), :]
        rel_grad[rel, :] = rel_grad[rel, :] + rb[row(i), :]

    rows_loop(TILE, scatter)

    @pl.when(step == E_DEV // TILE - 1)
    def _():
        def place(d, carry):
            spot = ((d % 2) * CHIPS + d // 2) * PER + REL4
            rows = pl.ds(pl.multiple_of(d * NEG_DEV, NEG_DEV), NEG_DEV)
            for c in range(CHUNKS):
                rel_grad[pl.ds(spot + c, NEG_DEV, stride=CHUNKS), :] = neg_acc[rows, c * LANES : (c + 1) * LANES]
            return carry

        lax.fori_loop(0, N_DEV, place, 0)
        side = core[0]
        half = CHIPS * PER
        stores = (
            pltpu.make_async_copy(rel_grad.at[pl.ds(pl.multiple_of((1 - side) * half, 8), half)], other, sems.at[0]),
            pltpu.make_async_copy(rel_grad.at[pl.ds(pl.multiple_of(side * half, 8), half)], mine, sems.at[1]),
        )
        for store in stores:
            store.start()
        for store in stores:
            store.wait()


def gradients(heads, grad_at, core, shared, tail_local, q, h, r, p):
    block = pl.BlockSpec((CHUNKS, TILE, LANES), lambda i: (0, i, 0))
    half = jax.ShapeDtypeStruct((CHIPS * PER, LANES), f32)
    whole = pl.BlockSpec((ENT_DEV * CHUNKS, LANES), lambda i: (0, 0))
    return pl.pallas_call(
        grads_kernel,
        grid=(E_DEV // TILE,),
        out_shape=(half, half, jax.ShapeDtypeStruct((ENT_DEV * CHUNKS, LANES), f32)),
        in_specs=[SMEM, SMEM, SMEM, ANY, ANY, block, block, block, block],
        out_specs=(ANY, ANY, whole),
        scratch_shapes=[
            pltpu.VMEM((N_DEV, PER - REL4, LANES), f32),
            pltpu.VMEM((NEG, CHUNKS * LANES), bf16),
            pltpu.VMEM((NEG, CHUNKS * LANES), bf16),
            pltpu.VMEM((CHUNKS * LANES, NEG), bf16),
            pltpu.VMEM((CHUNKS * LANES, NEG), bf16),
            pltpu.VMEM((NEG, CHUNKS * LANES), f32),
            pltpu.VMEM((N_DEV * PER, LANES), f32),
            pltpu.VMEM((TILE * CHUNKS, LANES), f32),
            pltpu.VMEM((TILE * CHUNKS, LANES), f32),
            pltpu.SemaphoreType.DMA((2,)),
        ],
        compiler_params=params(52),
        cost_estimate=cost(36_000_000_000, 60 << 20),
        name="gradients",
    )(heads, grad_at, core, shared, tail_local, q, h, r, p)


def returned_kernel(asked, returned, head_grad, out):
    out[...] = head_grad[...]

    def body(i):
        at = row(asked[i])
        out[at, :] = out[at, :] + returned[row(i), :]

    rows_loop(SLOTS, body)


def add_returned(asked, returned, head_grad):
    return pl.pallas_call(
        returned_kernel,
        out_shape=jax.ShapeDtypeStruct((ENT_DEV * CHUNKS, LANES), f32),
        in_specs=[SMEM, VMEM, VMEM],
        out_specs=VMEM,
        compiler_params=params(24),
        cost_estimate=cost(0, 10 << 20),
        name="add_returned",
    )(asked, returned, head_grad)


def adagrad(grad, n, table_t, state, new_table_t, new_state):
    g = [chunk_of(grad, c, n).T for c in range(CHUNKS)]
    squares = (g[0] * g[0] + g[1] * g[1]) + (g[2] * g[2] + g[3] * g[3])
    state_now = state[...] + jnp.sum(squares, axis=0, keepdims=True) * (1.0 / WIDTH)
    new_state[...] = state_now
    below = jnp.sqrt(state_now) + 1e-10
    for c, (start, size) in enumerate(SPANS):
        spot = slice(start, start + size)
        new_table_t[spot, :] = table_t[spot, :] - rate * g[c][:size] / below


def step_kernel(
    negatives, local_grad, parts, table_t, state, rel_t, rel_state,
    new_table_t, new_state, new_rel_t, new_rel_state,
    grad, share,
):
    grad[...] = local_grad[...]
    share[...] = jnp.zeros_like(share)
    share[0:PER, :] = jnp.sum(parts[...], axis=0)
    for i in range(NEG_DEV):
        at = row(negatives[i])
        grad[at, :] = grad[at, :] + share[REL4 + CHUNKS * i : REL4 + CHUNKS * (i + 1), :]
    adagrad(grad, ENT_DEV, table_t, state, new_table_t, new_state)
    adagrad(share, LANES, rel_t, rel_state, new_rel_t, new_rel_state)


def adagrad_step(negatives, local_grad, parts, table_t, state, rel_t, rel_state):
    def like(*shape):
        return jax.ShapeDtypeStruct(shape, f32)

    return pl.pallas_call(
        step_kernel,
        out_shape=(like(WIDTH, ENT_DEV), like(1, ENT_DEV), like(WIDTH, LANES), like(1, LANES)),
        in_specs=[SMEM] + [VMEM] * 6,
        out_specs=(VMEM,) * 4,
        scratch_shapes=[
            pltpu.VMEM((ENT_DEV * CHUNKS, LANES), f32),
            pltpu.VMEM((CHUNKS * LANES, LANES), f32),
        ],
        compiler_params=params(40),
        cost_estimate=cost(0, 16 << 20),
        name="adagrad_step",
    )(negatives, local_grad, parts, table_t, state, rel_t, rel_state)


def local(
    entity_table,
    entity_state,
    relation_table,
    relation_state,
    heads,
    relations,
    tails,
    pull_lists,
    negatives,
):
    table_t = entity_table.T
    rel_t = jnp.pad(relation_table, ((0, LANES - REL_DEV), (0, 0))).T
    owner, place = relations // REL_DEV, relations % REL_DEV
    rel_at = owner * (REL_DEV + NEG_DEV) + place
    grad_at = ((owner % 2) * CHIPS + owner // 2) * (REL_DEV + NEG_DEV) + place
    core = lax.axis_index("c")

    tab4, ag4 = prep(negatives, table_t, rel_t)
    shared = lax.all_gather(ag4, AXES, axis=0, tiled=True)
    asked = lax.all_to_all(pull_lists, AXES, split_axis=0, concat_axis=0, tiled=True).reshape(SLOTS)
    rows_out = pull_rows(asked, tab4)

    def exchange(rows):
        rows = rows.reshape(N_DEV, CAP * CHUNKS, LANES)
        return lax.all_to_all(rows, AXES, split_axis=0, concat_axis=0, tiled=True).reshape(SLOTS * CHUNKS, LANES)

    fetched = exchange(rows_out)
    h, t = ends(heads, tails, tab4, fetched)
    q, r, p, tail_local, outgoing = queries(rel_at, tails, shared, h, t)
    returned = exchange(outgoing)
    mine, other, head_grad = gradients(
        heads, grad_at, core.reshape(1), shared.reshape(N_DEV, PER, LANES), tail_local, q, h, r, p
    )
    other, returned = lax.optimization_barrier((other, returned))
    paired = mine + lax.ppermute(other, "c", [(0, 1), (1, 0)])
    parts = lax.all_to_all(
        paired.reshape(CHIPS, PER, LANES), AXES[:3], split_axis=0, concat_axis=0, tiled=True
    )
    local_grad = add_returned(asked, returned, head_grad)
    new_table_t, new_state, new_rel_t, new_rel_state = adagrad_step(
        negatives,
        local_grad,
        parts,
        table_t,
        entity_state.reshape(1, ENT_DEV),
        rel_t,
        jnp.pad(relation_state, (0, LANES - REL_DEV)).reshape(1, LANES),
    )
    return (
        new_table_t.T,
        new_state.reshape(ENT_DEV),
        new_rel_t.T[:REL_DEV],
        new_rel_state.reshape(LANES)[:REL_DEV],
    )


def solution(mesh):
    grid = Mesh(mesh.devices.reshape(4, 4, 4, 2), AXES)
    rows, flat = P(AXES, None), P(AXES)
    in_specs = (rows, flat, rows, flat, flat, flat, flat, rows, flat)
    out_specs = (rows, flat, rows, flat)
    return jax.shard_map(local, mesh=grid, in_specs=in_specs, out_specs=out_specs, check_vma=False)
```

```python
import jax
import jax.numpy as jnp
from jax import lax
from jax.experimental import pallas as pl
from jax.experimental.pallas import tpu as pltpu
from jax.sharding import Mesh, PartitionSpec as P

rate = 0.1
AXES = ("x", "z", "y", "c")
WIDTH = 400
HALF = 200
LANES = 128
CHUNKS = 4
SPANS = ((0, 128), (128, 72), (200, 128), (328, 72))
ENT_DEV = 1024
REL_DEV = 58
NEG_DEV = 8
E_DEV = 2048
N_DEV = 128
CAP = 16
NEG = N_DEV * NEG_DEV
SLOTS = N_DEV * CAP
CHIPS = N_DEV // 2
PER = CHUNKS * (REL_DEV + NEG_DEV)
REL4 = CHUNKS * REL_DEV
TILE = 256
PACK16 = 56
PACK66 = 208
UNROLL = 8

f32 = jnp.float32
bf16 = jnp.bfloat16
VMEM = pl.BlockSpec(memory_space=pltpu.VMEM)
SMEM = pl.BlockSpec(memory_space=pltpu.SMEM)
ANY = pl.BlockSpec(memory_space=pl.ANY)
HBM = pl.BlockSpec(memory_space=pltpu.HBM)


def params(mib):
    return pltpu.CompilerParams(vmem_limit_bytes=mib * 1024 * 1024)


def cost(flops, moved):
    return pl.CostEstimate(flops=flops, bytes_accessed=moved, transcendentals=0)


def chunk_of(ref, c, n):
    return ref[pl.ds(c, n, stride=CHUNKS), :]


def row(i):
    return pl.ds(pl.multiple_of(i * CHUNKS, CHUNKS), CHUNKS)


def split(x):
    hi = x.astype(bf16)
    return hi, (x - hi.astype(f32)).astype(bf16)


def dot3(a, b, dims):
    (ah, al), (bh, bl) = a, b

    def one(p, q):
        return lax.dot_general(p, q, (dims, ((), ())), preferred_element_type=f32)

    return one(ah, bh) + (one(ah, bl) + one(al, bh))


def rows_loop(n, body):
    def step(s, carry):
        for u in range(UNROLL):
            body(s * UNROLL + u)
        return carry

    lax.fori_loop(0, n // UNROLL, step, 0)


def lane(n):
    return lax.broadcasted_iota(jnp.int32, (n, LANES), 1)


def join(c1, c3):
    return jnp.where(lane(c1.shape[0]) < 72, c1, pltpu.roll(c3, 72, 1))


def rest(c3, k):
    return pltpu.roll(c3, (72 + 16 * k) % LANES, 1)


def part(joined, rem, k):
    at = lane(joined.shape[0])
    c1 = jnp.where(at < 72, joined, 0.0)
    tail = jnp.where(at < 72, pltpu.roll(rem, (56 - 16 * k) % LANES, 1), 0.0)
    return c1, jnp.where(at < 56, pltpu.roll(joined, 56, 1), tail)


def four(ref, base, n):
    return [ref[pl.ds(base + c, n, stride=CHUNKS), :] for c in range(CHUNKS)]


def pack16(src, src_base, dst, dst_base):
    rem = None
    for k in range(2):
        c0, c1, c2, c3 = four(src, src_base + 32 * k, 8)
        dst[pl.ds(dst_base + 8 * k, 8), :] = c0
        dst[pl.ds(dst_base + 16 + 8 * k, 8), :] = c2
        dst[pl.ds(dst_base + 32 + 8 * k, 8), :] = join(c1, c3)
        rem = rest(c3, 0) if k == 0 else jnp.where(lane(8) < 16, rem, rest(c3, 1))
    dst[pl.ds(dst_base + 48, 8), :] = rem


def unpack16(src, src_base, dst, dst_base):
    rem = src[pl.ds(src_base + 48, 8), :]
    for k in range(2):
        c1, c3 = part(src[pl.ds(src_base + 32 + 8 * k, 8), :], rem, k)
        c0 = src[pl.ds(src_base + 8 * k, 8), :]
        c2 = src[pl.ds(src_base + 16 + 8 * k, 8), :]
        for c, piece in enumerate((c0, c1, c2, c3)):
            dst[pl.ds(dst_base + 32 * k + c, 8, stride=CHUNKS), :] = piece


def blocks_loop(n, unroll, body):
    def step(s, carry):
        for u in range(unroll):
            body(s * unroll + u)
        return carry

    lax.fori_loop(0, n // unroll, step, 0)


def pack_slots(src, src_base, dst):
    blocks_loop(N_DEV, 4, lambda d: pack16(src, src_base + d * CAP * CHUNKS, dst, d * PACK16))


def unpack_slots(src, dst, dst_base):
    blocks_loop(N_DEV, 4, lambda d: unpack16(src, d * PACK16, dst, dst_base + d * CAP * CHUNKS))


def pack66(src, src_base, dst, dst_base):
    rows = REL_DEV + NEG_DEV
    rem = None
    for k in range(9):
        n = 8 if k < 8 else 2
        c0, c1, c2, c3 = four(src, src_base + 32 * k, n)
        dst[pl.ds(dst_base + 8 * k, n), :] = c0
        dst[pl.ds(dst_base + rows + 8 * k, n), :] = c2
        dst[pl.ds(dst_base + 2 * rows + 8 * k, n), :] = join(c1, c3)
        if k == 8:
            dst[pl.ds(dst_base + 3 * rows + 8, 2), :] = rest(c3, 0)
        else:
            rem = rest(c3, k) if k == 0 else jnp.where(lane(8) < 16 * k, rem, rest(c3, k))
    dst[pl.ds(dst_base + 3 * rows, 8), :] = rem


def unpack66(src, dst):
    rows = REL_DEV + NEG_DEV
    for k in range(9):
        n = 8 if k < 8 else 2
        rem = src[pl.ds(3 * rows, 8), :] if k < 8 else src[pl.ds(3 * rows + 8, 2), :]
        c1, c3 = part(src[pl.ds(2 * rows + 8 * k, n), :], rem, k % 8)
        c0 = src[pl.ds(8 * k, n), :]
        c2 = src[pl.ds(rows + 8 * k, n), :]
        for c, piece in enumerate((c0, c1, c2, c3)):
            dst[pl.ds(32 * k + c, n, stride=CHUNKS), :] = piece


def to_chunks(src, dst, n):
    for c, (start, size) in enumerate(SPANS):
        piece = src[start : start + size, :]
        if size < LANES:
            piece = jnp.concatenate([piece, jnp.zeros((LANES - size, n), f32)], axis=0)
        dst[pl.ds(c, n, stride=CHUNKS), :] = piece.T


def prep_kernel(negatives, table_t, rel_t, tab4, ag4, rel4):
    to_chunks(table_t, tab4, ENT_DEV)
    to_chunks(rel_t, rel4, LANES)
    ag4[0:REL4, :] = rel4[0:REL4, :]
    for i in range(NEG_DEV):
        ag4[REL4 + CHUNKS * i : REL4 + CHUNKS * (i + 1), :] = tab4[row(negatives[i]), :]


def prep(negatives, table_t, rel_t):
    return pl.pallas_call(
        prep_kernel,
        out_shape=(
            jax.ShapeDtypeStruct((ENT_DEV * CHUNKS, LANES), f32),
            jax.ShapeDtypeStruct((PER, LANES), f32),
        ),
        in_specs=[SMEM, VMEM, VMEM],
        out_specs=(VMEM, VMEM),
        scratch_shapes=[pltpu.VMEM((LANES * CHUNKS, LANES), f32)],
        compiler_params=params(58),
        cost_estimate=cost(0, 8 << 20),
        name="prep",
    )(negatives, table_t, rel_t)


def pull_kernel(asked, tab4, out, picked, packed, sem):
    def body(i):
        picked[row(i), :] = tab4[row(asked[i]), :]

    rows_loop(SLOTS, body)
    pack_slots(picked, 0, packed)
    store = pltpu.make_async_copy(packed, out, sem)
    store.start()
    store.wait()


def pull_rows(asked, tab4):
    return pl.pallas_call(
        pull_kernel,
        out_shape=jax.ShapeDtypeStruct((N_DEV * PACK16, LANES), f32),
        in_specs=[SMEM, VMEM],
        out_specs=HBM,
        scratch_shapes=[
            pltpu.VMEM((SLOTS * CHUNKS, LANES), f32),
            pltpu.VMEM((N_DEV * PACK16, LANES), f32),
            pltpu.SemaphoreType.DMA,
        ],
        compiler_params=params(58),
        cost_estimate=cost(0, 8 << 20),
        name="pull_rows",
    )(asked, tab4)


def ends_kernel(heads, tails, tab4, fetched, h_out, t_out, ext, packed, hb, tb, sems):
    step = pl.program_id(0)
    local = ENT_DEV * CHUNKS

    @pl.when(step == 0)
    def _():
        loads = (
            pltpu.make_async_copy(tab4, ext.at[pl.ds(0, local)], sems.at[0]),
            pltpu.make_async_copy(fetched, packed, sems.at[1]),
        )
        for load in loads:
            load.start()
        for load in loads:
            load.wait()
        unpack_slots(packed, ext, local)

    base = step * TILE

    def gather(i):
        hb[row(i), :] = ext[row(heads[base + i]), :]
        tb[row(i), :] = ext[row(tails[base + i]), :]

    rows_loop(TILE, gather)
    for c in range(CHUNKS):
        h_out[c] = chunk_of(hb, c, TILE)
        t_out[c] = chunk_of(tb, c, TILE)


def ends(heads, tails, tab4, fetched):
    plane = jax.ShapeDtypeStruct((CHUNKS, E_DEV, LANES), f32)
    block = pl.BlockSpec((CHUNKS, TILE, LANES), lambda i: (0, i, 0))
    return pl.pallas_call(
        ends_kernel,
        grid=(E_DEV // TILE,),
        out_shape=(plane, plane),
        in_specs=[SMEM, SMEM, ANY, ANY],
        out_specs=(block, block),
        scratch_shapes=[
            pltpu.VMEM(((ENT_DEV + SLOTS) * CHUNKS, LANES), f32),
            pltpu.VMEM((N_DEV * PACK16, LANES), f32),
            pltpu.VMEM((TILE * CHUNKS, LANES), f32),
            pltpu.VMEM((TILE * CHUNKS, LANES), f32),
            pltpu.SemaphoreType.DMA((2,)),
        ],
        compiler_params=params(58),
        cost_estimate=cost(0, 30 << 20),
        name="ends",
    )(heads, tails, tab4, fetched)


def query_kernel(
    rel_at, tails, shared, h_in, t_in,
    q_out, r_out, p_out, tail_local, outgoing,
    rel, ext_grad, packed, hb, rb, sems,
):
    step = pl.program_id(0)

    @pl.when(step == 0)
    def _():
        load = pltpu.make_async_copy(shared, rel, sems.at[0])
        load.start()
        ext_grad[...] = jnp.zeros_like(ext_grad)
        load.wait()

    base = step * TILE

    def gather(i):
        rb[row(i), :] = rel[row(rel_at[base + i]), :]

    rows_loop(TILE, gather)
    h = [h_in[c] for c in range(CHUNKS)]
    r = [chunk_of(rb, c, TILE) for c in range(CHUNKS)]
    t = [t_in[c] for c in range(CHUNKS)]
    q = [h[0] * r[0] - h[2] * r[2], h[1] * r[1] - h[3] * r[3], h[0] * r[2] + h[2] * r[0], h[1] * r[3] + h[3] * r[1]]
    score = (q[0] * t[0] + q[1] * t[1]) + (q[2] * t[2] + q[3] * t[3])
    pos_grad = jax.nn.sigmoid(jnp.sum(score, axis=1, keepdims=True)) - 1.0
    for c in range(CHUNKS):
        q_out[c] = q[c]
        r_out[c] = r[c]
        p_out[c] = pos_grad * t[c]
        hb[pl.ds(c, TILE, stride=CHUNKS), :] = pos_grad * q[c]

    def scatter(i):
        at = row(tails[base + i])
        ext_grad[at, :] = ext_grad[at, :] + hb[row(i), :]

    rows_loop(TILE, scatter)

    @pl.when(step == E_DEV // TILE - 1)
    def _():
        local = ENT_DEV * CHUNKS
        stores = (
            pltpu.make_async_copy(ext_grad.at[pl.ds(0, local)], tail_local, sems.at[0]),
            pltpu.make_async_copy(packed, outgoing, sems.at[1]),
        )
        stores[0].start()
        pack_slots(ext_grad, local, packed)
        stores[1].start()
        for store in stores:
            store.wait()


def queries(rel_at, tails, shared, h, t):
    plane = jax.ShapeDtypeStruct((CHUNKS, E_DEV, LANES), f32)
    block = pl.BlockSpec((CHUNKS, TILE, LANES), lambda i: (0, i, 0))
    return pl.pallas_call(
        query_kernel,
        grid=(E_DEV // TILE,),
        out_shape=(
            plane,
            plane,
            plane,
            jax.ShapeDtypeStruct((ENT_DEV * CHUNKS, LANES), f32),
            jax.ShapeDtypeStruct((N_DEV * PACK16, LANES), f32),
        ),
        in_specs=[SMEM, SMEM, ANY, block, block],
        out_specs=(block, block, block, HBM, HBM),
        scratch_shapes=[
            pltpu.VMEM((N_DEV * PER, LANES), f32),
            pltpu.VMEM(((ENT_DEV + SLOTS) * CHUNKS, LANES), f32),
            pltpu.VMEM((N_DEV * PACK16, LANES), f32),
            pltpu.VMEM((TILE * CHUNKS, LANES), f32),
            pltpu.VMEM((TILE * CHUNKS, LANES), f32),
            pltpu.SemaphoreType.DMA((2,)),
        ],
        compiler_params=params(58),
        cost_estimate=cost(0, 60 << 20),
        name="queries",
    )(rel_at, tails, shared, h, t)


def grads_kernel(
    heads, grad_at, core, shared, local_grad, q_in, h_in, r_in, p_in,
    mine, other, head_grad,
    negs, n_hi, n_lo, t_hi, t_lo, neg_acc, rel_grad, packed, hb, rb, sems,
):
    step = pl.program_id(0)

    @pl.when(step == 0)
    def _():
        load = pltpu.make_async_copy(shared.at[:, pl.ds(REL4, PER - REL4), :], negs, sems.at[0])
        load.start()
        start = pltpu.make_async_copy(local_grad, head_grad, sems.at[1])
        start.start()
        rel_grad[...] = jnp.zeros_like(rel_grad)
        neg_acc[...] = jnp.zeros_like(neg_acc)
        load.wait()
        flat = negs.reshape(NEG * CHUNKS, LANES)
        for c in range(CHUNKS):
            lanes = slice(c * LANES, (c + 1) * LANES)
            piece = chunk_of(flat, c, NEG)
            n_hi[:, lanes], n_lo[:, lanes] = split(piece)
            t_hi[lanes, :], t_lo[lanes, :] = split(piece.T)
        start.wait()

    base = step * TILE
    q = split(jnp.concatenate([q_in[c] for c in range(CHUNKS)], axis=1))
    negative = dot3(q, (t_hi[...], t_lo[...]), ((1,), (0,)))
    neg_grad = split(jax.nn.sigmoid(negative) * (1.0 / NEG))
    neg_acc[...] += dot3(neg_grad, q, ((0,), (0,)))
    back = dot3(neg_grad, (n_hi[...], n_lo[...]), ((1,), (0,)))
    g = [p_in[c] + back[:, c * LANES : (c + 1) * LANES] for c in range(CHUNKS)]
    for k in range(2):
        for buf, src in ((hb, r_in), (rb, h_in)):
            buf[pl.ds(k, TILE, stride=CHUNKS), :] = g[k] * src[k] + g[k + 2] * src[k + 2]
            buf[pl.ds(k + 2, TILE, stride=CHUNKS), :] = g[k + 2] * src[k] - g[k] * src[k + 2]

    def scatter(i):
        at = row(heads[base + i])
        rel = row(grad_at[base + i])
        head_grad[at, :] = head_grad[at, :] + hb[row(i), :]
        rel_grad[rel, :] = rel_grad[rel, :] + rb[row(i), :]

    rows_loop(TILE, scatter)

    @pl.when(step == E_DEV // TILE - 1)
    def _():
        def place(d, carry):
            spot = ((d % 2) * CHIPS + d // 2) * PER + REL4
            rows = pl.ds(pl.multiple_of(d * NEG_DEV, NEG_DEV), NEG_DEV)
            for c in range(CHUNKS):
                rel_grad[pl.ds(spot + c, NEG_DEV, stride=CHUNKS), :] = neg_acc[rows, c * LANES : (c + 1) * LANES]
            return carry

        lax.fori_loop(0, N_DEV, place, 0)
        side = core[0]
        half = CHIPS * PACK66
        stores = (
            pltpu.make_async_copy(packed.at[pl.ds(0, half)], other, sems.at[0]),
            pltpu.make_async_copy(packed.at[pl.ds(half, half)], mine, sems.at[1]),
        )
        for i, owner in enumerate((1 - side, side)):

            def pack(d, i=i, owner=owner):
                pack66(rel_grad, (owner * CHIPS + d) * PER, packed, (i * CHIPS + d) * PACK66)

            blocks_loop(CHIPS, 2, pack)
            stores[i].start()
        for store in stores:
            store.wait()


def gradients(heads, grad_at, core, shared, tail_local, q, h, r, p):
    block = pl.BlockSpec((CHUNKS, TILE, LANES), lambda i: (0, i, 0))
    half = jax.ShapeDtypeStruct((CHIPS * PACK66, LANES), f32)
    whole = pl.BlockSpec((ENT_DEV * CHUNKS, LANES), lambda i: (0, 0))
    return pl.pallas_call(
        grads_kernel,
        grid=(E_DEV // TILE,),
        out_shape=(half, half, jax.ShapeDtypeStruct((ENT_DEV * CHUNKS, LANES), f32)),
        in_specs=[SMEM, SMEM, SMEM, ANY, ANY, block, block, block, block],
        out_specs=(HBM, HBM, whole),
        scratch_shapes=[
            pltpu.VMEM((N_DEV, PER - REL4, LANES), f32),
            pltpu.VMEM((NEG, CHUNKS * LANES), bf16),
            pltpu.VMEM((NEG, CHUNKS * LANES), bf16),
            pltpu.VMEM((CHUNKS * LANES, NEG), bf16),
            pltpu.VMEM((CHUNKS * LANES, NEG), bf16),
            pltpu.VMEM((NEG, CHUNKS * LANES), f32),
            pltpu.VMEM((N_DEV * PER, LANES), f32),
            pltpu.VMEM((N_DEV * PACK66, LANES), f32),
            pltpu.VMEM((TILE * CHUNKS, LANES), f32),
            pltpu.VMEM((TILE * CHUNKS, LANES), f32),
            pltpu.SemaphoreType.DMA((2,)),
        ],
        compiler_params=params(58),
        cost_estimate=cost(36_000_000_000, 60 << 20),
        name="gradients",
    )(heads, grad_at, core, shared, tail_local, q, h, r, p)


def returned_kernel(asked, packed, head_grad, out, returned):
    out[...] = head_grad[...]
    unpack_slots(packed, returned, 0)

    def body(i):
        at = row(asked[i])
        out[at, :] = out[at, :] + returned[row(i), :]

    rows_loop(SLOTS, body)


def add_returned(asked, returned, head_grad):
    return pl.pallas_call(
        returned_kernel,
        out_shape=jax.ShapeDtypeStruct((ENT_DEV * CHUNKS, LANES), f32),
        in_specs=[SMEM, VMEM, VMEM],
        out_specs=VMEM,
        scratch_shapes=[pltpu.VMEM((SLOTS * CHUNKS, LANES), f32)],
        compiler_params=params(24),
        cost_estimate=cost(0, 10 << 20),
        name="add_returned",
    )(asked, returned, head_grad)


def adagrad(grad, n, table_t, state, new_table_t, new_state):
    g = [chunk_of(grad, c, n).T for c in range(CHUNKS)]
    squares = (g[0] * g[0] + g[1] * g[1]) + (g[2] * g[2] + g[3] * g[3])
    state_now = state[...] + jnp.sum(squares, axis=0, keepdims=True) * (1.0 / WIDTH)
    new_state[...] = state_now
    below = jnp.sqrt(state_now) + 1e-10
    for c, (start, size) in enumerate(SPANS):
        spot = slice(start, start + size)
        new_table_t[spot, :] = table_t[spot, :] - rate * g[c][:size] / below


def step_kernel(
    negatives, local_grad, parts, table_t, state, rel_t, rel_state,
    new_table_t, new_state, new_rel_t, new_rel_state,
    grad, share, packed,
):
    grad[...] = local_grad[...]
    share[...] = jnp.zeros_like(share)
    packed[...] = jnp.sum(parts[...], axis=0)
    unpack66(packed, share)
    for i in range(NEG_DEV):
        at = row(negatives[i])
        grad[at, :] = grad[at, :] + share[REL4 + CHUNKS * i : REL4 + CHUNKS * (i + 1), :]
    adagrad(grad, ENT_DEV, table_t, state, new_table_t, new_state)
    adagrad(share, LANES, rel_t, rel_state, new_rel_t, new_rel_state)


def adagrad_step(negatives, local_grad, parts, table_t, state, rel_t, rel_state):
    def like(*shape):
        return jax.ShapeDtypeStruct(shape, f32)

    return pl.pallas_call(
        step_kernel,
        out_shape=(like(WIDTH, ENT_DEV), like(1, ENT_DEV), like(WIDTH, LANES), like(1, LANES)),
        in_specs=[SMEM] + [VMEM] * 6,
        out_specs=(VMEM,) * 4,
        scratch_shapes=[
            pltpu.VMEM((ENT_DEV * CHUNKS, LANES), f32),
            pltpu.VMEM((CHUNKS * LANES, LANES), f32),
            pltpu.VMEM((PACK66, LANES), f32),
        ],
        compiler_params=params(40),
        cost_estimate=cost(0, 16 << 20),
        name="adagrad_step",
    )(negatives, local_grad, parts, table_t, state, rel_t, rel_state)


def local(
    entity_table,
    entity_state,
    relation_table,
    relation_state,
    heads,
    relations,
    tails,
    pull_lists,
    negatives,
):
    table_t = entity_table.T
    rel_t = jnp.pad(relation_table, ((0, LANES - REL_DEV), (0, 0))).T
    owner, place = relations // REL_DEV, relations % REL_DEV
    rel_at = owner * (REL_DEV + NEG_DEV) + place
    grad_at = ((owner % 2) * CHIPS + owner // 2) * (REL_DEV + NEG_DEV) + place
    core = lax.axis_index("c")

    tab4, ag4 = prep(negatives, table_t, rel_t)
    shared = lax.all_gather(ag4, AXES, axis=0, tiled=True)
    asked = lax.all_to_all(pull_lists, AXES, split_axis=0, concat_axis=0, tiled=True).reshape(SLOTS)
    rows_out = pull_rows(asked, tab4)

    def exchange(rows):
        rows = rows.reshape(N_DEV, PACK16, LANES)
        return lax.all_to_all(rows, AXES, split_axis=0, concat_axis=0, tiled=True).reshape(N_DEV * PACK16, LANES)

    fetched = exchange(rows_out)
    h, t = ends(heads, tails, tab4, fetched)
    q, r, p, tail_local, outgoing = queries(rel_at, tails, shared, h, t)
    returned = exchange(outgoing)
    mine, other, head_grad = gradients(
        heads, grad_at, core.reshape(1), shared.reshape(N_DEV, PER, LANES), tail_local, q, h, r, p
    )
    other, returned = lax.optimization_barrier((other, returned))
    paired = mine + lax.ppermute(other, "c", [(0, 1), (1, 0)])
    parts = lax.all_to_all(
        paired.reshape(CHIPS, PACK66, LANES), AXES[:3], split_axis=0, concat_axis=0, tiled=True
    )
    local_grad = add_returned(asked, returned, head_grad)
    new_table_t, new_state, new_rel_t, new_rel_state = adagrad_step(
        negatives,
        local_grad,
        parts,
        table_t,
        entity_state.reshape(1, ENT_DEV),
        rel_t,
        jnp.pad(relation_state, (0, LANES - REL_DEV)).reshape(1, LANES),
    )
    return (
        new_table_t.T,
        new_state.reshape(ENT_DEV),
        new_rel_t.T[:REL_DEV],
        new_rel_state.reshape(LANES)[:REL_DEV],
    )


def solution(mesh):
    grid = Mesh(mesh.devices.reshape(4, 4, 4, 2), AXES)
    rows, flat = P(AXES, None), P(AXES)
    in_specs = (rows, flat, rows, flat, flat, flat, flat, rows, flat)
    out_specs = (rows, flat, rows, flat)
    return jax.shard_map(local, mesh=grid, in_specs=in_specs, out_specs=out_specs, check_vma=False)
```

```python
import jax
import jax.numpy as jnp
from jax import lax
from jax.experimental import pallas as pl
from jax.experimental.pallas import tpu as pltpu
from jax.sharding import Mesh, PartitionSpec as P

rate = 0.1
AXES = ("x", "z", "y", "c")
WIDTH = 400
HALF = 200
LANES = 128
CHUNKS = 4
SPANS = ((0, 128), (128, 72), (200, 128), (328, 72))
ENT_DEV = 1024
REL_DEV = 58
NEG_DEV = 8
E_DEV = 2048
N_DEV = 128
CAP = 16
NEG = N_DEV * NEG_DEV
SLOTS = N_DEV * CAP
CHIPS = N_DEV // 2
PER = CHUNKS * (REL_DEV + NEG_DEV)
REL4 = CHUNKS * REL_DEV
TILE = 256
PACK16 = 56
PACK66 = 208
UNROLL = 8

f32 = jnp.float32
bf16 = jnp.bfloat16
VMEM = pl.BlockSpec(memory_space=pltpu.VMEM)
SMEM = pl.BlockSpec(memory_space=pltpu.SMEM)
ANY = pl.BlockSpec(memory_space=pl.ANY)
HBM = pl.BlockSpec(memory_space=pltpu.HBM)


def params(mib):
    return pltpu.CompilerParams(vmem_limit_bytes=mib * 1024 * 1024)


def cost(flops, moved):
    return pl.CostEstimate(flops=flops, bytes_accessed=moved, transcendentals=0)


def chunk_of(ref, c, n):
    return ref[pl.ds(c, n, stride=CHUNKS), :]


def row(i):
    return pl.ds(pl.multiple_of(i * CHUNKS, CHUNKS), CHUNKS)


def split(x):
    hi = x.astype(bf16)
    return hi, (x - hi.astype(f32)).astype(bf16)


def dot3(a, b, dims):
    (ah, al), (bh, bl) = a, b

    def one(p, q):
        return lax.dot_general(p, q, (dims, ((), ())), preferred_element_type=f32)

    return one(ah, bh) + (one(ah, bl) + one(al, bh))


def rows_loop(n, body):
    def step(s, carry):
        for u in range(UNROLL):
            body(s * UNROLL + u)
        return carry

    lax.fori_loop(0, n // UNROLL, step, 0)


def lane(n):
    return lax.broadcasted_iota(jnp.int32, (n, LANES), 1)


def join(c1, c3):
    return jnp.where(lane(c1.shape[0]) < 72, c1, pltpu.roll(c3, 72, 1))


def rest(c3, k):
    return pltpu.roll(c3, (72 + 16 * k) % LANES, 1)


def part(joined, rem, k):
    at = lane(joined.shape[0])
    c1 = jnp.where(at < 72, joined, 0.0)
    tail = jnp.where(at < 72, pltpu.roll(rem, (56 - 16 * k) % LANES, 1), 0.0)
    return c1, jnp.where(at < 56, pltpu.roll(joined, 56, 1), tail)


def four(ref, base, n):
    return [ref[pl.ds(base + c, n, stride=CHUNKS), :] for c in range(CHUNKS)]


def pack16(src, src_base, dst, dst_base):
    rem = None
    for k in range(2):
        c0, c1, c2, c3 = four(src, src_base + 32 * k, 8)
        dst[pl.ds(dst_base + 8 * k, 8), :] = c0
        dst[pl.ds(dst_base + 16 + 8 * k, 8), :] = c2
        dst[pl.ds(dst_base + 32 + 8 * k, 8), :] = join(c1, c3)
        rem = rest(c3, 0) if k == 0 else jnp.where(lane(8) < 16, rem, rest(c3, 1))
    dst[pl.ds(dst_base + 48, 8), :] = rem


def unpack16(src, src_base, dst, dst_base):
    rem = src[pl.ds(src_base + 48, 8), :]
    for k in range(2):
        c1, c3 = part(src[pl.ds(src_base + 32 + 8 * k, 8), :], rem, k)
        c0 = src[pl.ds(src_base + 8 * k, 8), :]
        c2 = src[pl.ds(src_base + 16 + 8 * k, 8), :]
        for c, piece in enumerate((c0, c1, c2, c3)):
            dst[pl.ds(dst_base + 32 * k + c, 8, stride=CHUNKS), :] = piece


def blocks_loop(n, unroll, body):
    def step(s, carry):
        for u in range(unroll):
            body(s * unroll + u)
        return carry

    lax.fori_loop(0, n // unroll, step, 0)


def pack_slots(src, src_base, dst):
    blocks_loop(N_DEV, 4, lambda d: pack16(src, src_base + d * CAP * CHUNKS, dst, d * PACK16))


def unpack_slots(src, dst, dst_base):
    blocks_loop(N_DEV, 4, lambda d: unpack16(src, d * PACK16, dst, dst_base + d * CAP * CHUNKS))


def pack66(src, src_base, dst, dst_base):
    rows = REL_DEV + NEG_DEV
    rem = None
    for k in range(9):
        n = 8 if k < 8 else 2
        c0, c1, c2, c3 = four(src, src_base + 32 * k, n)
        dst[pl.ds(dst_base + 8 * k, n), :] = c0
        dst[pl.ds(dst_base + rows + 8 * k, n), :] = c2
        dst[pl.ds(dst_base + 2 * rows + 8 * k, n), :] = join(c1, c3)
        if k == 8:
            dst[pl.ds(dst_base + 3 * rows + 8, 2), :] = rest(c3, 0)
        else:
            rem = rest(c3, k) if k == 0 else jnp.where(lane(8) < 16 * k, rem, rest(c3, k))
    dst[pl.ds(dst_base + 3 * rows, 8), :] = rem


def unpack66(src, dst):
    rows = REL_DEV + NEG_DEV
    for k in range(9):
        n = 8 if k < 8 else 2
        rem = src[pl.ds(3 * rows, 8), :] if k < 8 else src[pl.ds(3 * rows + 8, 2), :]
        c1, c3 = part(src[pl.ds(2 * rows + 8 * k, n), :], rem, k % 8)
        c0 = src[pl.ds(8 * k, n), :]
        c2 = src[pl.ds(rows + 8 * k, n), :]
        for c, piece in enumerate((c0, c1, c2, c3)):
            dst[pl.ds(32 * k + c, n, stride=CHUNKS), :] = piece


def to_chunks(src, dst, n):
    for c, (start, size) in enumerate(SPANS):
        piece = src[start : start + size, :]
        if size < LANES:
            piece = jnp.concatenate([piece, jnp.zeros((LANES - size, n), f32)], axis=0)
        dst[pl.ds(c, n, stride=CHUNKS), :] = piece.T


def prep_kernel(negatives, table_t, rel_t, tab4, ag4, rel4):
    to_chunks(table_t, tab4, ENT_DEV)
    to_chunks(rel_t, rel4, LANES)
    ag4[0:REL4, :] = rel4[0:REL4, :]
    for i in range(NEG_DEV):
        ag4[REL4 + CHUNKS * i : REL4 + CHUNKS * (i + 1), :] = tab4[row(negatives[i]), :]


def prep(negatives, table_t, rel_t):
    return pl.pallas_call(
        prep_kernel,
        out_shape=(
            jax.ShapeDtypeStruct((ENT_DEV * CHUNKS, LANES), f32),
            jax.ShapeDtypeStruct((PER, LANES), f32),
        ),
        in_specs=[SMEM, VMEM, VMEM],
        out_specs=(VMEM, VMEM),
        scratch_shapes=[pltpu.VMEM((LANES * CHUNKS, LANES), f32)],
        compiler_params=params(58),
        cost_estimate=cost(0, 8 << 20),
        name="prep",
    )(negatives, table_t, rel_t)


def pull_kernel(asked, tab4, out, picked, packed, sem):
    def body(i):
        picked[row(i), :] = tab4[row(asked[i]), :]

    rows_loop(SLOTS, body)
    pack_slots(picked, 0, packed)
    store = pltpu.make_async_copy(packed, out, sem)
    store.start()
    store.wait()


def pull_rows(asked, tab4):
    return pl.pallas_call(
        pull_kernel,
        out_shape=jax.ShapeDtypeStruct((N_DEV * PACK16, LANES), f32),
        in_specs=[SMEM, VMEM],
        out_specs=HBM,
        scratch_shapes=[
            pltpu.VMEM((SLOTS * CHUNKS, LANES), f32),
            pltpu.VMEM((N_DEV * PACK16, LANES), f32),
            pltpu.SemaphoreType.DMA,
        ],
        compiler_params=params(58),
        cost_estimate=cost(0, 8 << 20),
        name="pull_rows",
    )(asked, tab4)


def query_kernel(
    heads, rel_at, tab4, shared,
    q_out, h_out, r_out, back_out, neg_acc,
    tab, rel, n_hi, n_lo, t_hi, t_lo, hb, rb, sems,
):
    step = pl.program_id(0)

    @pl.when(step == 0)
    def _():
        loads = (
            pltpu.make_async_copy(tab4, tab, sems.at[0]),
            pltpu.make_async_copy(shared, rel, sems.at[1]),
        )
        for load in loads:
            load.start()
        neg_acc[...] = jnp.zeros_like(neg_acc)
        for load in loads:
            load.wait()

        for c in range(CHUNKS):
            lanes = slice(c * LANES, (c + 1) * LANES)

            def place(d, carry, c=c):
                rows = pl.ds(pl.multiple_of(d * NEG_DEV, NEG_DEV), NEG_DEV)
                hb[rows, :] = rel[pl.ds(d * PER + REL4 + c, NEG_DEV, stride=CHUNKS), :]
                return carry

            lax.fori_loop(0, N_DEV, place, 0)
            piece = hb[...]
            n_hi[:, lanes], n_lo[:, lanes] = split(piece)
            t_hi[lanes, :], t_lo[lanes, :] = split(piece.T)

    base = step * TILE

    def gather(i):
        hb[row(i), :] = tab[row(heads[base + i]), :]
        rb[row(i), :] = rel[row(rel_at[base + i]), :]

    rows_loop(TILE, gather)
    h = [chunk_of(hb, c, TILE) for c in range(CHUNKS)]
    r = [chunk_of(rb, c, TILE) for c in range(CHUNKS)]
    q = [h[0] * r[0] - h[2] * r[2], h[1] * r[1] - h[3] * r[3], h[0] * r[2] + h[2] * r[0], h[1] * r[3] + h[3] * r[1]]
    for c in range(CHUNKS):
        q_out[c] = q[c]
        h_out[c] = h[c]
        r_out[c] = r[c]
    q = split(jnp.concatenate(q, axis=1))
    negative = dot3(q, (t_hi[...], t_lo[...]), ((1,), (0,)))
    neg_grad = split(jax.nn.sigmoid(negative) * (1.0 / NEG))
    neg_acc[...] += dot3(neg_grad, q, ((0,), (0,)))
    back = dot3(neg_grad, (n_hi[...], n_lo[...]), ((1,), (0,)))
    for c in range(CHUNKS):
        back_out[c] = back[:, c * LANES : (c + 1) * LANES]


PLANE = jax.ShapeDtypeStruct((CHUNKS, E_DEV, LANES), f32)
BLOCK = pl.BlockSpec((CHUNKS, TILE, LANES), lambda i: (0, i, 0))


def queries(heads, rel_at, tab4, shared):
    rows = pltpu.VMEM((TILE * CHUNKS, LANES), f32)
    wide = pltpu.VMEM((NEG, CHUNKS * LANES), bf16)
    tall = pltpu.VMEM((CHUNKS * LANES, NEG), bf16)
    return pl.pallas_call(
        query_kernel,
        grid=(E_DEV // TILE,),
        out_shape=(PLANE, PLANE, PLANE, PLANE, jax.ShapeDtypeStruct((NEG, CHUNKS * LANES), f32)),
        in_specs=[SMEM, SMEM, ANY, ANY],
        out_specs=(BLOCK, BLOCK, BLOCK, BLOCK, pl.BlockSpec((NEG, CHUNKS * LANES), lambda i: (0, 0))),
        scratch_shapes=[
            pltpu.VMEM((ENT_DEV * CHUNKS, LANES), f32),
            pltpu.VMEM((N_DEV * PER, LANES), f32),
            wide,
            wide,
            tall,
            tall,
            rows,
            rows,
            pltpu.SemaphoreType.DMA((2,)),
        ],
        compiler_params=params(58),
        cost_estimate=cost(36_000_000_000, 60 << 20),
        name="queries",
    )(heads, rel_at, tab4, shared)


def tail_kernel(
    tails, tab4, fetched, q_in,
    p_out, tail_local, outgoing,
    ext, ext_grad, packed, tb, sems,
):
    step = pl.program_id(0)
    local = ENT_DEV * CHUNKS

    @pl.when(step == 0)
    def _():
        loads = (
            pltpu.make_async_copy(fetched, packed, sems.at[1]),
            pltpu.make_async_copy(tab4, ext.at[pl.ds(0, local)], sems.at[0]),
        )
        for load in loads:
            load.start()
        ext_grad[...] = jnp.zeros_like(ext_grad)
        for load in loads:
            load.wait()
        unpack_slots(packed, ext, local)

    base = step * TILE

    def gather(i):
        tb[row(i), :] = ext[row(tails[base + i]), :]

    rows_loop(TILE, gather)
    t = [chunk_of(tb, c, TILE) for c in range(CHUNKS)]
    q = [q_in[c] for c in range(CHUNKS)]
    score = (q[0] * t[0] + q[1] * t[1]) + (q[2] * t[2] + q[3] * t[3])
    pos_grad = jax.nn.sigmoid(jnp.sum(score, axis=1, keepdims=True)) - 1.0
    for c in range(CHUNKS):
        p_out[c] = pos_grad * t[c]
        tb[pl.ds(c, TILE, stride=CHUNKS), :] = pos_grad * q[c]

    def scatter(i):
        at = row(tails[base + i])
        ext_grad[at, :] = ext_grad[at, :] + tb[row(i), :]

    rows_loop(TILE, scatter)

    @pl.when(step == E_DEV // TILE - 1)
    def _():
        stores = (
            pltpu.make_async_copy(ext_grad.at[pl.ds(0, local)], tail_local, sems.at[0]),
            pltpu.make_async_copy(packed, outgoing, sems.at[1]),
        )
        stores[0].start()
        pack_slots(ext_grad, local, packed)
        stores[1].start()
        for store in stores:
            store.wait()


def tail_terms(tails, tab4, fetched, q):
    return pl.pallas_call(
        tail_kernel,
        grid=(E_DEV // TILE,),
        out_shape=(
            PLANE,
            jax.ShapeDtypeStruct((ENT_DEV * CHUNKS, LANES), f32),
            jax.ShapeDtypeStruct((N_DEV * PACK16, LANES), f32),
        ),
        in_specs=[SMEM, ANY, ANY, BLOCK],
        out_specs=(BLOCK, HBM, HBM),
        scratch_shapes=[
            pltpu.VMEM(((ENT_DEV + SLOTS) * CHUNKS, LANES), f32),
            pltpu.VMEM(((ENT_DEV + SLOTS) * CHUNKS, LANES), f32),
            pltpu.VMEM((N_DEV * PACK16, LANES), f32),
            pltpu.VMEM((TILE * CHUNKS, LANES), f32),
            pltpu.SemaphoreType.DMA((2,)),
        ],
        compiler_params=params(58),
        cost_estimate=cost(0, 30 << 20),
        name="tail_terms",
    )(tails, tab4, fetched, q)


def edge_kernel(
    heads, grad_at, core, tail_local, neg_acc, h_in, r_in, p_in, back_in,
    mine, other, head_grad,
    rel_grad, packed, hb, rb, sems,
):
    step = pl.program_id(0)

    @pl.when(step == 0)
    def _():
        start = pltpu.make_async_copy(tail_local, head_grad, sems.at[0])
        start.start()
        rel_grad[...] = jnp.zeros_like(rel_grad)
        start.wait()

    base = step * TILE
    g = [p_in[c] + back_in[c] for c in range(CHUNKS)]
    for k in range(2):
        for buf, src in ((hb, r_in), (rb, h_in)):
            buf[pl.ds(k, TILE, stride=CHUNKS), :] = g[k] * src[k] + g[k + 2] * src[k + 2]
            buf[pl.ds(k + 2, TILE, stride=CHUNKS), :] = g[k + 2] * src[k] - g[k] * src[k + 2]

    def scatter(i):
        at = row(heads[base + i])
        rel = row(grad_at[base + i])
        head_grad[at, :] = head_grad[at, :] + hb[row(i), :]
        rel_grad[rel, :] = rel_grad[rel, :] + rb[row(i), :]

    rows_loop(TILE, scatter)

    @pl.when(step == E_DEV // TILE - 1)
    def _():
        def place(d, carry):
            spot = ((d % 2) * CHIPS + d // 2) * PER + REL4
            rows = pl.ds(pl.multiple_of(d * NEG_DEV, NEG_DEV), NEG_DEV)
            for c in range(CHUNKS):
                rel_grad[pl.ds(spot + c, NEG_DEV, stride=CHUNKS), :] = neg_acc[rows, c * LANES : (c + 1) * LANES]
            return carry

        lax.fori_loop(0, N_DEV, place, 0)
        side = core[0]
        half = CHIPS * PACK66
        stores = (
            pltpu.make_async_copy(packed.at[pl.ds(0, half)], other, sems.at[0]),
            pltpu.make_async_copy(packed.at[pl.ds(half, half)], mine, sems.at[1]),
        )
        for i, owner in enumerate((1 - side, side)):

            def pack(d, i=i, owner=owner):
                pack66(rel_grad, (owner * CHIPS + d) * PER, packed, (i * CHIPS + d) * PACK66)

            blocks_loop(CHIPS, 2, pack)
            stores[i].start()
        for store in stores:
            store.wait()


def gradients(heads, grad_at, core, tail_local, neg_acc, h, r, p, back):
    half = jax.ShapeDtypeStruct((CHIPS * PACK66, LANES), f32)
    whole = pl.BlockSpec((ENT_DEV * CHUNKS, LANES), lambda i: (0, 0))
    return pl.pallas_call(
        edge_kernel,
        grid=(E_DEV // TILE,),
        out_shape=(half, half, jax.ShapeDtypeStruct((ENT_DEV * CHUNKS, LANES), f32)),
        in_specs=[SMEM, SMEM, SMEM, ANY, pl.BlockSpec((NEG, CHUNKS * LANES), lambda i: (0, 0)), BLOCK, BLOCK, BLOCK, BLOCK],
        out_specs=(HBM, HBM, whole),
        scratch_shapes=[
            pltpu.VMEM((N_DEV * PER, LANES), f32),
            pltpu.VMEM((N_DEV * PACK66, LANES), f32),
            pltpu.VMEM((TILE * CHUNKS, LANES), f32),
            pltpu.VMEM((TILE * CHUNKS, LANES), f32),
            pltpu.SemaphoreType.DMA((2,)),
        ],
        compiler_params=params(58),
        cost_estimate=cost(0, 1 << 20),
        name="gradients",
    )(heads, grad_at, core, tail_local, neg_acc, h, r, p, back)


def returned_kernel(asked, packed, head_grad, out, returned):
    out[...] = head_grad[...]
    unpack_slots(packed, returned, 0)

    def body(i):
        at = row(asked[i])
        out[at, :] = out[at, :] + returned[row(i), :]

    rows_loop(SLOTS, body)


def add_returned(asked, returned, head_grad):
    return pl.pallas_call(
        returned_kernel,
        out_shape=jax.ShapeDtypeStruct((ENT_DEV * CHUNKS, LANES), f32),
        in_specs=[SMEM, VMEM, VMEM],
        out_specs=VMEM,
        scratch_shapes=[pltpu.VMEM((SLOTS * CHUNKS, LANES), f32)],
        compiler_params=params(24),
        cost_estimate=cost(0, 10 << 20),
        name="add_returned",
    )(asked, returned, head_grad)


def adagrad(grad, n, table_t, state, new_table_t, new_state):
    g = [chunk_of(grad, c, n).T for c in range(CHUNKS)]
    squares = (g[0] * g[0] + g[1] * g[1]) + (g[2] * g[2] + g[3] * g[3])
    state_now = state[...] + jnp.sum(squares, axis=0, keepdims=True) * (1.0 / WIDTH)
    new_state[...] = state_now
    below = jnp.sqrt(state_now) + 1e-10
    for c, (start, size) in enumerate(SPANS):
        spot = slice(start, start + size)
        new_table_t[spot, :] = table_t[spot, :] - rate * g[c][:size] / below


def step_kernel(
    negatives, local_grad, parts, table_t, state, rel_t, rel_state,
    new_table_t, new_state, new_rel_t, new_rel_state,
    grad, share, packed,
):
    grad[...] = local_grad[...]
    share[...] = jnp.zeros_like(share)
    packed[...] = jnp.sum(parts[...], axis=0)
    unpack66(packed, share)
    for i in range(NEG_DEV):
        at = row(negatives[i])
        grad[at, :] = grad[at, :] + share[REL4 + CHUNKS * i : REL4 + CHUNKS * (i + 1), :]
    adagrad(grad, ENT_DEV, table_t, state, new_table_t, new_state)
    adagrad(share, LANES, rel_t, rel_state, new_rel_t, new_rel_state)


def adagrad_step(negatives, local_grad, parts, table_t, state, rel_t, rel_state):
    def like(*shape):
        return jax.ShapeDtypeStruct(shape, f32)

    return pl.pallas_call(
        step_kernel,
        out_shape=(like(WIDTH, ENT_DEV), like(1, ENT_DEV), like(WIDTH, LANES), like(1, LANES)),
        in_specs=[SMEM] + [VMEM] * 6,
        out_specs=(VMEM,) * 4,
        scratch_shapes=[
            pltpu.VMEM((ENT_DEV * CHUNKS, LANES), f32),
            pltpu.VMEM((CHUNKS * LANES, LANES), f32),
            pltpu.VMEM((PACK66, LANES), f32),
        ],
        compiler_params=params(40),
        cost_estimate=cost(0, 16 << 20),
        name="adagrad_step",
    )(negatives, local_grad, parts, table_t, state, rel_t, rel_state)


def local(
    entity_table,
    entity_state,
    relation_table,
    relation_state,
    heads,
    relations,
    tails,
    pull_lists,
    negatives,
):
    table_t = entity_table.T
    rel_t = jnp.pad(relation_table, ((0, LANES - REL_DEV), (0, 0))).T
    owner, place = relations // REL_DEV, relations % REL_DEV
    rel_at = owner * (REL_DEV + NEG_DEV) + place
    grad_at = ((owner % 2) * CHIPS + owner // 2) * (REL_DEV + NEG_DEV) + place
    core = lax.axis_index("c")

    tab4, ag4 = prep(negatives, table_t, rel_t)
    shared = lax.all_gather(ag4, AXES, axis=0, tiled=True)
    asked = lax.all_to_all(pull_lists, AXES, split_axis=0, concat_axis=0, tiled=True).reshape(SLOTS)
    rows_out, shared = lax.optimization_barrier((pull_rows(asked, tab4), shared))

    def exchange(rows):
        rows = rows.reshape(N_DEV, PACK16, LANES)
        return lax.all_to_all(rows, AXES, split_axis=0, concat_axis=0, tiled=True).reshape(N_DEV * PACK16, LANES)

    fetched = exchange(rows_out)
    q, h, r, back, neg_acc = queries(heads, rel_at, tab4, shared)
    p, tail_local, outgoing = tail_terms(tails, tab4, fetched, q)
    returned = exchange(outgoing)
    mine, other, head_grad = gradients(
        heads, grad_at, core.reshape(1), tail_local, neg_acc, h, r, p, back
    )
    other, returned = lax.optimization_barrier((other, returned))
    paired = mine + lax.ppermute(other, "c", [(0, 1), (1, 0)])
    parts = lax.all_to_all(
        paired.reshape(CHIPS, PACK66, LANES), AXES[:3], split_axis=0, concat_axis=0, tiled=True
    )
    local_grad = add_returned(asked, returned, head_grad)
    new_table_t, new_state, new_rel_t, new_rel_state = adagrad_step(
        negatives,
        local_grad,
        parts,
        table_t,
        entity_state.reshape(1, ENT_DEV),
        rel_t,
        jnp.pad(relation_state, (0, LANES - REL_DEV)).reshape(1, LANES),
    )
    return (
        new_table_t.T,
        new_state.reshape(ENT_DEV),
        new_rel_t.T[:REL_DEV],
        new_rel_state.reshape(LANES)[:REL_DEV],
    )


def solution(mesh):
    grid = Mesh(mesh.devices.reshape(4, 4, 4, 2), AXES)
    rows, flat = P(AXES, None), P(AXES)
    in_specs = (rows, flat, rows, flat, flat, flat, flat, rows, flat)
    out_specs = (rows, flat, rows, flat)
    return jax.shard_map(local, mesh=grid, in_specs=in_specs, out_specs=out_specs, check_vma=False)
```

```python
import jax
import jax.numpy as jnp
from jax import lax
from jax.experimental import pallas as pl
from jax.experimental.pallas import tpu as pltpu
from jax.sharding import Mesh, PartitionSpec as P

rate = 0.1
AXES = ("x", "z", "y", "c")
WIDTH = 400
HALF = 200
LANES = 128
CHUNKS = 4
SPANS = ((0, 128), (128, 72), (200, 128), (328, 72))
ENT_DEV = 1024
REL_DEV = 58
NEG_DEV = 8
E_DEV = 2048
N_DEV = 128
CAP = 16
NEG = N_DEV * NEG_DEV
SLOTS = N_DEV * CAP
CHIPS = N_DEV // 2
PER = CHUNKS * (REL_DEV + NEG_DEV)
REL4 = CHUNKS * REL_DEV
TILE = 256
PACK16 = 56
PACK66 = 208
PIECES = 4
UNROLL = 8

f32 = jnp.float32
bf16 = jnp.bfloat16
VMEM = pl.BlockSpec(memory_space=pltpu.VMEM)
SMEM = pl.BlockSpec(memory_space=pltpu.SMEM)
ANY = pl.BlockSpec(memory_space=pl.ANY)
HBM = pl.BlockSpec(memory_space=pltpu.HBM)


def params(mib):
    return pltpu.CompilerParams(vmem_limit_bytes=mib * 1024 * 1024)


def cost(flops, moved):
    return pl.CostEstimate(flops=flops, bytes_accessed=moved, transcendentals=0)


def chunk_of(ref, c, n):
    return ref[pl.ds(c, n, stride=CHUNKS), :]


def row(i):
    return pl.ds(pl.multiple_of(i * CHUNKS, CHUNKS), CHUNKS)


def split(x):
    hi = x.astype(bf16)
    return hi, (x - hi.astype(f32)).astype(bf16)


def dot3(a, b, dims):
    (ah, al), (bh, bl) = a, b

    def one(p, q):
        return lax.dot_general(p, q, (dims, ((), ())), preferred_element_type=f32)

    return one(ah, bh) + (one(ah, bl) + one(al, bh))


def rows_loop(n, body):
    def step(s, carry):
        for u in range(UNROLL):
            body(s * UNROLL + u)
        return carry

    lax.fori_loop(0, n // UNROLL, step, 0)


def lane(n):
    return lax.broadcasted_iota(jnp.int32, (n, LANES), 1)


def join(c1, c3):
    return jnp.where(lane(c1.shape[0]) < 72, c1, pltpu.roll(c3, 72, 1))


def rest(c3, k):
    return pltpu.roll(c3, (72 + 16 * k) % LANES, 1)


def part(joined, rem, k):
    at = lane(joined.shape[0])
    c1 = jnp.where(at < 72, joined, 0.0)
    tail = jnp.where(at < 72, pltpu.roll(rem, (56 - 16 * k) % LANES, 1), 0.0)
    return c1, jnp.where(at < 56, pltpu.roll(joined, 56, 1), tail)


def four(ref, base, n):
    return [ref[pl.ds(base + c, n, stride=CHUNKS), :] for c in range(CHUNKS)]


def pack16(src, src_base, dst, dst_base):
    rem = None
    for k in range(2):
        c0, c1, c2, c3 = four(src, src_base + 32 * k, 8)
        dst[pl.ds(dst_base + 8 * k, 8), :] = c0
        dst[pl.ds(dst_base + 16 + 8 * k, 8), :] = c2
        dst[pl.ds(dst_base + 32 + 8 * k, 8), :] = join(c1, c3)
        rem = rest(c3, 0) if k == 0 else jnp.where(lane(8) < 16, rem, rest(c3, 1))
    dst[pl.ds(dst_base + 48, 8), :] = rem


def unpack16(src, src_base, dst, dst_base):
    rem = src[pl.ds(src_base + 48, 8), :]
    for k in range(2):
        c1, c3 = part(src[pl.ds(src_base + 32 + 8 * k, 8), :], rem, k)
        c0 = src[pl.ds(src_base + 8 * k, 8), :]
        c2 = src[pl.ds(src_base + 16 + 8 * k, 8), :]
        for c, piece in enumerate((c0, c1, c2, c3)):
            dst[pl.ds(dst_base + 32 * k + c, 8, stride=CHUNKS), :] = piece


def blocks_loop(n, unroll, body):
    def step(s, carry):
        for u in range(unroll):
            body(s * unroll + u)
        return carry

    lax.fori_loop(0, n // unroll, step, 0)


def pack_slots(src, src_base, dst):
    blocks_loop(N_DEV, 4, lambda d: pack16(src, src_base + d * CAP * CHUNKS, dst, d * PACK16))


def unpack_slots(src, dst, dst_base):
    blocks_loop(N_DEV, 4, lambda d: unpack16(src, d * PACK16, dst, dst_base + d * CAP * CHUNKS))


def pack66(src, src_base, dst, dst_base):
    rows = REL_DEV + NEG_DEV
    rem = None
    for k in range(9):
        n = 8 if k < 8 else 2
        c0, c1, c2, c3 = four(src, src_base + 32 * k, n)
        dst[pl.ds(dst_base + 8 * k, n), :] = c0
        dst[pl.ds(dst_base + rows + 8 * k, n), :] = c2
        dst[pl.ds(dst_base + 2 * rows + 8 * k, n), :] = join(c1, c3)
        if k == 8:
            dst[pl.ds(dst_base + 3 * rows + 8, 2), :] = rest(c3, 0)
        else:
            rem = rest(c3, k) if k == 0 else jnp.where(lane(8) < 16 * k, rem, rest(c3, k))
    dst[pl.ds(dst_base + 3 * rows, 8), :] = rem


def unpack66(src, src_base, dst, dst_base):
    rows = REL_DEV + NEG_DEV
    for k in range(9):
        n = 8 if k < 8 else 2
        rem = src[pl.ds(src_base + 3 * rows + (0 if k < 8 else 8), n), :]
        c1, c3 = part(src[pl.ds(src_base + 2 * rows + 8 * k, n), :], rem, k % 8)
        c0 = src[pl.ds(src_base + 8 * k, n), :]
        c2 = src[pl.ds(src_base + rows + 8 * k, n), :]
        for c, piece in enumerate((c0, c1, c2, c3)):
            dst[pl.ds(dst_base + 32 * k + c, n, stride=CHUNKS), :] = piece


def to_chunks(src, dst, n):
    for c, (start, size) in enumerate(SPANS):
        piece = src[start : start + size, :]
        if size < LANES:
            piece = jnp.concatenate([piece, jnp.zeros((LANES - size, n), f32)], axis=0)
        dst[pl.ds(c, n, stride=CHUNKS), :] = piece.T


def prep_kernel(negatives, table_t, rel_t, tab4, send, rel4):
    to_chunks(table_t, tab4, ENT_DEV)
    to_chunks(rel_t, rel4, LANES)
    for i in range(NEG_DEV):
        rel4[REL4 + CHUNKS * i : REL4 + CHUNKS * (i + 1), :] = tab4[row(negatives[i]), :]
    pack66(rel4, 0, send, 0)


def prep(negatives, table_t, rel_t):
    return pl.pallas_call(
        prep_kernel,
        out_shape=(
            jax.ShapeDtypeStruct((ENT_DEV * CHUNKS, LANES), f32),
            jax.ShapeDtypeStruct((PACK66, LANES), f32),
        ),
        in_specs=[SMEM, VMEM, VMEM],
        out_specs=(VMEM, VMEM),
        scratch_shapes=[pltpu.VMEM((LANES * CHUNKS, LANES), f32)],
        compiler_params=params(58),
        cost_estimate=cost(0, 8 << 20),
        name="prep",
    )(negatives, table_t, rel_t)


def pull_kernel(asked, tab4, out, picked, packed, sem):
    def body(i):
        picked[row(i), :] = tab4[row(asked[i]), :]

    rows_loop(SLOTS, body)
    pack_slots(picked, 0, packed)
    store = pltpu.make_async_copy(packed, out, sem)
    store.start()
    store.wait()


def pull_rows(asked, tab4):
    return pl.pallas_call(
        pull_kernel,
        out_shape=jax.ShapeDtypeStruct((N_DEV * PACK16, LANES), f32),
        in_specs=[SMEM, VMEM],
        out_specs=HBM,
        scratch_shapes=[
            pltpu.VMEM((SLOTS * CHUNKS, LANES), f32),
            pltpu.VMEM((N_DEV * PACK16, LANES), f32),
            pltpu.SemaphoreType.DMA,
        ],
        compiler_params=params(58),
        cost_estimate=cost(0, 8 << 20),
        name="pull_rows",
    )(asked, tab4)


def query_kernel(
    heads, rel_at, tab4, shared,
    q_out, h_out, r_out, back_out, neg_acc,
    tab, rel, packed, n_hi, n_lo, t_hi, t_lo, hb, rb, sems,
):
    step = pl.program_id(0)

    @pl.when(step == 0)
    def _():
        size = N_DEV * PACK66 // PIECES
        loads = [
            pltpu.make_async_copy(shared.at[pl.ds(i * size, size)], packed.at[pl.ds(i * size, size)], sems.at[i])
            for i in range(PIECES)
        ]
        loads.append(pltpu.make_async_copy(tab4, tab, sems.at[PIECES]))
        for load in loads:
            load.start()
        neg_acc[...] = jnp.zeros_like(neg_acc)
        each = N_DEV // PIECES
        for i in range(PIECES):
            loads[i].wait()
            blocks_loop(each, 2, lambda d, i=i: unpack66(packed, (i * each + d) * PACK66, rel, (i * each + d) * PER))
        loads[PIECES].wait()

        for c in range(CHUNKS):
            lanes = slice(c * LANES, (c + 1) * LANES)

            def place(d, carry, c=c):
                rows = pl.ds(pl.multiple_of(d * NEG_DEV, NEG_DEV), NEG_DEV)
                hb[rows, :] = rel[pl.ds(d * PER + REL4 + c, NEG_DEV, stride=CHUNKS), :]
                return carry

            lax.fori_loop(0, N_DEV, place, 0)
            piece = hb[...]
            n_hi[:, lanes], n_lo[:, lanes] = split(piece)
            t_hi[lanes, :], t_lo[lanes, :] = split(piece.T)

    base = step * TILE

    def gather(i):
        hb[row(i), :] = tab[row(heads[base + i]), :]
        rb[row(i), :] = rel[row(rel_at[base + i]), :]

    rows_loop(TILE, gather)
    h = [chunk_of(hb, c, TILE) for c in range(CHUNKS)]
    r = [chunk_of(rb, c, TILE) for c in range(CHUNKS)]
    q = [h[0] * r[0] - h[2] * r[2], h[1] * r[1] - h[3] * r[3], h[0] * r[2] + h[2] * r[0], h[1] * r[3] + h[3] * r[1]]
    for c in range(CHUNKS):
        q_out[c] = q[c]
        h_out[c] = h[c]
        r_out[c] = r[c]
    q = split(jnp.concatenate(q, axis=1))
    negative = dot3(q, (t_hi[...], t_lo[...]), ((1,), (0,)))
    neg_grad = split(jax.nn.sigmoid(negative) * (1.0 / NEG))
    neg_acc[...] += dot3(neg_grad, q, ((0,), (0,)))
    back = dot3(neg_grad, (n_hi[...], n_lo[...]), ((1,), (0,)))
    for c in range(CHUNKS):
        back_out[c] = back[:, c * LANES : (c + 1) * LANES]


PLANE = jax.ShapeDtypeStruct((CHUNKS, E_DEV, LANES), f32)
BLOCK = pl.BlockSpec((CHUNKS, TILE, LANES), lambda i: (0, i, 0))


def queries(heads, rel_at, tab4, shared):
    rows = pltpu.VMEM((TILE * CHUNKS, LANES), f32)
    wide = pltpu.VMEM((NEG, CHUNKS * LANES), bf16)
    tall = pltpu.VMEM((CHUNKS * LANES, NEG), bf16)
    return pl.pallas_call(
        query_kernel,
        grid=(E_DEV // TILE,),
        out_shape=(PLANE, PLANE, PLANE, PLANE, jax.ShapeDtypeStruct((NEG, CHUNKS * LANES), f32)),
        in_specs=[SMEM, SMEM, ANY, ANY],
        out_specs=(BLOCK, BLOCK, BLOCK, BLOCK, pl.BlockSpec((NEG, CHUNKS * LANES), lambda i: (0, 0))),
        scratch_shapes=[
            pltpu.VMEM((ENT_DEV * CHUNKS, LANES), f32),
            pltpu.VMEM((N_DEV * PER, LANES), f32),
            pltpu.VMEM((N_DEV * PACK66, LANES), f32),
            wide,
            wide,
            tall,
            tall,
            rows,
            rows,
            pltpu.SemaphoreType.DMA((PIECES + 1,)),
        ],
        compiler_params=params(58),
        cost_estimate=cost(36_000_000_000, 60 << 20),
        name="queries",
    )(heads, rel_at, tab4, shared)


def tail_kernel(
    tails, tab4, fetched, q_in,
    p_out, tail_local, outgoing,
    ext, ext_grad, packed, tb, sems,
):
    step = pl.program_id(0)
    local = ENT_DEV * CHUNKS

    @pl.when(step == 0)
    def _():
        loads = (
            pltpu.make_async_copy(fetched, packed, sems.at[1]),
            pltpu.make_async_copy(tab4, ext.at[pl.ds(0, local)], sems.at[0]),
        )
        for load in loads:
            load.start()
        ext_grad[...] = jnp.zeros_like(ext_grad)
        for load in loads:
            load.wait()
        unpack_slots(packed, ext, local)

    base = step * TILE

    def gather(i):
        tb[row(i), :] = ext[row(tails[base + i]), :]

    rows_loop(TILE, gather)
    t = [chunk_of(tb, c, TILE) for c in range(CHUNKS)]
    q = [q_in[c] for c in range(CHUNKS)]
    score = (q[0] * t[0] + q[1] * t[1]) + (q[2] * t[2] + q[3] * t[3])
    pos_grad = jax.nn.sigmoid(jnp.sum(score, axis=1, keepdims=True)) - 1.0
    for c in range(CHUNKS):
        p_out[c] = pos_grad * t[c]
        tb[pl.ds(c, TILE, stride=CHUNKS), :] = pos_grad * q[c]

    def scatter(i):
        at = row(tails[base + i])
        ext_grad[at, :] = ext_grad[at, :] + tb[row(i), :]

    rows_loop(TILE, scatter)

    @pl.when(step == E_DEV // TILE - 1)
    def _():
        stores = (
            pltpu.make_async_copy(ext_grad.at[pl.ds(0, local)], tail_local, sems.at[0]),
            pltpu.make_async_copy(packed, outgoing, sems.at[1]),
        )
        stores[0].start()
        pack_slots(ext_grad, local, packed)
        stores[1].start()
        for store in stores:
            store.wait()


def tail_terms(tails, tab4, fetched, q):
    return pl.pallas_call(
        tail_kernel,
        grid=(E_DEV // TILE,),
        out_shape=(
            PLANE,
            jax.ShapeDtypeStruct((ENT_DEV * CHUNKS, LANES), f32),
            jax.ShapeDtypeStruct((N_DEV * PACK16, LANES), f32),
        ),
        in_specs=[SMEM, ANY, ANY, BLOCK],
        out_specs=(BLOCK, HBM, HBM),
        scratch_shapes=[
            pltpu.VMEM(((ENT_DEV + SLOTS) * CHUNKS, LANES), f32),
            pltpu.VMEM(((ENT_DEV + SLOTS) * CHUNKS, LANES), f32),
            pltpu.VMEM((N_DEV * PACK16, LANES), f32),
            pltpu.VMEM((TILE * CHUNKS, LANES), f32),
            pltpu.SemaphoreType.DMA((2,)),
        ],
        compiler_params=params(58),
        cost_estimate=cost(0, 30 << 20),
        name="tail_terms",
    )(tails, tab4, fetched, q)


def edge_kernel(
    heads, grad_at, core, tail_local, neg_acc, h_in, r_in, p_in, back_in,
    mine, other0, other1, other2, other3, head_grad,
    rel_grad, packed, hb, rb, sems,
):
    step = pl.program_id(0)

    @pl.when(step == 0)
    def _():
        start = pltpu.make_async_copy(tail_local, head_grad, sems.at[0])
        start.start()
        rel_grad[...] = jnp.zeros_like(rel_grad)
        start.wait()

    base = step * TILE
    g = [p_in[c] + back_in[c] for c in range(CHUNKS)]
    for k in range(2):
        for buf, src in ((hb, r_in), (rb, h_in)):
            buf[pl.ds(k, TILE, stride=CHUNKS), :] = g[k] * src[k] + g[k + 2] * src[k + 2]
            buf[pl.ds(k + 2, TILE, stride=CHUNKS), :] = g[k + 2] * src[k] - g[k] * src[k + 2]

    def scatter(i):
        at = row(heads[base + i])
        rel = row(grad_at[base + i])
        head_grad[at, :] = head_grad[at, :] + hb[row(i), :]
        rel_grad[rel, :] = rel_grad[rel, :] + rb[row(i), :]

    rows_loop(TILE, scatter)

    @pl.when(step == E_DEV // TILE - 1)
    def _():
        def place(d, carry):
            spot = ((d % 2) * CHIPS + d // 2) * PER + REL4
            rows = pl.ds(pl.multiple_of(d * NEG_DEV, NEG_DEV), NEG_DEV)
            for c in range(CHUNKS):
                rel_grad[pl.ds(spot + c, NEG_DEV, stride=CHUNKS), :] = neg_acc[rows, c * LANES : (c + 1) * LANES]
            return carry

        lax.fori_loop(0, N_DEV, place, 0)
        side = core[0]
        size = CHIPS * PACK66 // PIECES
        stores = [
            pltpu.make_async_copy(packed.at[pl.ds(i * size, size)], other, sems.at[i])
            for i, other in enumerate((other0, other1, other2, other3))
        ]
        stores.append(pltpu.make_async_copy(packed.at[pl.ds(PIECES * size, PIECES * size)], mine, sems.at[PIECES]))

        def pack(d, owner, first):
            pack66(rel_grad, (owner * CHIPS + d) * PER, packed, (first + d) * PACK66)

        chips = CHIPS // PIECES
        for i in range(PIECES):
            blocks_loop(chips, 2, lambda d, i=i: pack(i * chips + d, 1 - side, 0))
            stores[i].start()
        blocks_loop(CHIPS, 2, lambda d: pack(d, side, CHIPS))
        stores[PIECES].start()
        for store in stores:
            store.wait()


def gradients(heads, grad_at, core, tail_local, neg_acc, h, r, p, back):
    half = jax.ShapeDtypeStruct((CHIPS * PACK66, LANES), f32)
    piece = jax.ShapeDtypeStruct((CHIPS * PACK66 // PIECES, LANES), f32)
    whole = pl.BlockSpec((ENT_DEV * CHUNKS, LANES), lambda i: (0, 0))
    return pl.pallas_call(
        edge_kernel,
        grid=(E_DEV // TILE,),
        out_shape=(half, piece, piece, piece, piece, jax.ShapeDtypeStruct((ENT_DEV * CHUNKS, LANES), f32)),
        in_specs=[SMEM, SMEM, SMEM, ANY, pl.BlockSpec((NEG, CHUNKS * LANES), lambda i: (0, 0)), BLOCK, BLOCK, BLOCK, BLOCK],
        out_specs=(HBM,) * 5 + (whole,),
        scratch_shapes=[
            pltpu.VMEM((N_DEV * PER, LANES), f32),
            pltpu.VMEM((N_DEV * PACK66, LANES), f32),
            pltpu.VMEM((TILE * CHUNKS, LANES), f32),
            pltpu.VMEM((TILE * CHUNKS, LANES), f32),
            pltpu.SemaphoreType.DMA((PIECES + 1,)),
        ],
        compiler_params=params(58),
        cost_estimate=cost(0, 1 << 20),
        name="gradients",
    )(heads, grad_at, core, tail_local, neg_acc, h, r, p, back)


def merge_kernel(mine, got0, got1, got2, got3, out):
    part = pl.program_id(0) // (MERGE_STEPS // PIECES)
    for i, got in enumerate((got0, got1, got2, got3)):

        @pl.when(part == i)
        def _(got=got):
            out[...] = mine[...] + got[...]


MERGE_STEPS = 16


def merge(mine, got):
    size = CHIPS * PACK66 // MERGE_STEPS
    each = MERGE_STEPS // PIECES
    block = pl.BlockSpec((size, LANES), lambda s: (s, 0))
    pieces = [
        pl.BlockSpec((size, LANES), lambda s, i=i: (jnp.clip(s - i * each, 0, each - 1), 0)) for i in range(PIECES)
    ]
    return pl.pallas_call(
        merge_kernel,
        grid=(MERGE_STEPS,),
        out_shape=jax.ShapeDtypeStruct((CHIPS * PACK66, LANES), f32),
        in_specs=[block] + pieces,
        out_specs=block,
        compiler_params=params(58),
        cost_estimate=cost(0, 1 << 16),
        name="merge",
    )(mine, *got)


def returned_kernel(asked, packed, head_grad, out, returned):
    out[...] = head_grad[...]
    unpack_slots(packed, returned, 0)

    def body(i):
        at = row(asked[i])
        out[at, :] = out[at, :] + returned[row(i), :]

    rows_loop(SLOTS, body)


def add_returned(asked, returned, head_grad):
    return pl.pallas_call(
        returned_kernel,
        out_shape=jax.ShapeDtypeStruct((ENT_DEV * CHUNKS, LANES), f32),
        in_specs=[SMEM, VMEM, VMEM],
        out_specs=VMEM,
        scratch_shapes=[pltpu.VMEM((SLOTS * CHUNKS, LANES), f32)],
        compiler_params=params(24),
        cost_estimate=cost(0, 10 << 20),
        name="add_returned",
    )(asked, returned, head_grad)


def adagrad(grad, n, table_t, state, new_table_t, new_state):
    g = [chunk_of(grad, c, n).T for c in range(CHUNKS)]
    squares = (g[0] * g[0] + g[1] * g[1]) + (g[2] * g[2] + g[3] * g[3])
    state_now = state[...] + jnp.sum(squares, axis=0, keepdims=True) * (1.0 / WIDTH)
    new_state[...] = state_now
    below = jnp.sqrt(state_now) + 1e-10
    for c, (start, size) in enumerate(SPANS):
        spot = slice(start, start + size)
        new_table_t[spot, :] = table_t[spot, :] - rate * g[c][:size] / below


def step_kernel(
    negatives, local_grad, parts, table_t, state, rel_t, rel_state,
    new_table_t, new_state, new_rel_t, new_rel_state,
    grad, share, packed,
):
    grad[...] = local_grad[...]
    share[...] = jnp.zeros_like(share)
    packed[...] = jnp.sum(parts[...], axis=0)
    unpack66(packed, 0, share, 0)
    for i in range(NEG_DEV):
        at = row(negatives[i])
        grad[at, :] = grad[at, :] + share[REL4 + CHUNKS * i : REL4 + CHUNKS * (i + 1), :]
    adagrad(grad, ENT_DEV, table_t, state, new_table_t, new_state)
    adagrad(share, LANES, rel_t, rel_state, new_rel_t, new_rel_state)


def adagrad_step(negatives, local_grad, parts, table_t, state, rel_t, rel_state):
    def like(*shape):
        return jax.ShapeDtypeStruct(shape, f32)

    return pl.pallas_call(
        step_kernel,
        out_shape=(like(WIDTH, ENT_DEV), like(1, ENT_DEV), like(WIDTH, LANES), like(1, LANES)),
        in_specs=[SMEM] + [VMEM] * 6,
        out_specs=(VMEM,) * 4,
        scratch_shapes=[
            pltpu.VMEM((ENT_DEV * CHUNKS, LANES), f32),
            pltpu.VMEM((CHUNKS * LANES, LANES), f32),
            pltpu.VMEM((PACK66, LANES), f32),
        ],
        compiler_params=params(40),
        cost_estimate=cost(0, 16 << 20),
        name="adagrad_step",
    )(negatives, local_grad, parts, table_t, state, rel_t, rel_state)


def local(
    entity_table,
    entity_state,
    relation_table,
    relation_state,
    heads,
    relations,
    tails,
    pull_lists,
    negatives,
):
    table_t = entity_table.T
    rel_t = jnp.pad(relation_table, ((0, LANES - REL_DEV), (0, 0))).T
    owner, place = relations // REL_DEV, relations % REL_DEV
    rel_at = owner * (REL_DEV + NEG_DEV) + place
    grad_at = ((owner % 2) * CHIPS + owner // 2) * (REL_DEV + NEG_DEV) + place
    core = lax.axis_index("c")

    tab4, send = prep(negatives, table_t, rel_t)
    shared = lax.all_gather(send, AXES, axis=0, tiled=True)
    asked = lax.all_to_all(pull_lists, AXES, split_axis=0, concat_axis=0, tiled=True).reshape(SLOTS)
    rows_out, shared = lax.optimization_barrier((pull_rows(asked, tab4), shared))

    def exchange(rows):
        rows = rows.reshape(N_DEV, PACK16, LANES)
        return lax.all_to_all(rows, AXES, split_axis=0, concat_axis=0, tiled=True).reshape(N_DEV * PACK16, LANES)

    fetched = exchange(rows_out)
    q, h, r, back, neg_acc = queries(heads, rel_at, tab4, shared)
    p, tail_local, outgoing = tail_terms(tails, tab4, fetched, q)
    returned = exchange(outgoing)
    mine, *others, head_grad = gradients(
        heads, grad_at, core.reshape(1), tail_local, neg_acc, h, r, p, back
    )
    paired = merge(mine, [lax.ppermute(other, "c", [(0, 1), (1, 0)]) for other in others])
    paired, returned = lax.optimization_barrier((paired, returned))
    parts = lax.all_to_all(
        paired.reshape(CHIPS, PACK66, LANES), AXES[:3], split_axis=0, concat_axis=0, tiled=True
    )
    local_grad = add_returned(asked, returned, head_grad)
    new_table_t, new_state, new_rel_t, new_rel_state = adagrad_step(
        negatives,
        local_grad,
        parts,
        table_t,
        entity_state.reshape(1, ENT_DEV),
        rel_t,
        jnp.pad(relation_state, (0, LANES - REL_DEV)).reshape(1, LANES),
    )
    return (
        new_table_t.T,
        new_state.reshape(ENT_DEV),
        new_rel_t.T[:REL_DEV],
        new_rel_state.reshape(LANES)[:REL_DEV],
    )


def solution(mesh):
    grid = Mesh(mesh.devices.reshape(4, 4, 4, 2), AXES)
    rows, flat = P(AXES, None), P(AXES)
    in_specs = (rows, flat, rows, flat, flat, flat, flat, rows, flat)
    out_specs = (rows, flat, rows, flat)
    return jax.shard_map(local, mesh=grid, in_specs=in_specs, out_specs=out_specs, check_vma=False)
```

```python
import jax
import jax.numpy as jnp
from jax import lax
from jax.experimental import pallas as pl
from jax.experimental.pallas import tpu as pltpu
from jax.sharding import Mesh, PartitionSpec as P

rate = 0.1
AXES = ("x", "z", "y", "c")
WIDTH = 400
HALF = 200
LANES = 128
CHUNKS = 4
SPANS = ((0, 128), (128, 72), (200, 128), (328, 72))
ENT_DEV = 1024
REL_DEV = 58
NEG_DEV = 8
E_DEV = 2048
N_DEV = 128
CAP = 16
NEG = N_DEV * NEG_DEV
SLOTS = N_DEV * CAP
CHIPS = N_DEV // 2
PER = CHUNKS * (REL_DEV + NEG_DEV)
REL4 = CHUNKS * REL_DEV
TILE = 256
PACK16 = 56
PACK66 = 208
PIECES = 4
KEPT = PACK66 // 2
GROUPS = (0, 11, 22, 33, 44, 54, 64)
UNROLL = 8

f32 = jnp.float32
bf16 = jnp.bfloat16
VMEM = pl.BlockSpec(memory_space=pltpu.VMEM)
SMEM = pl.BlockSpec(memory_space=pltpu.SMEM)
ANY = pl.BlockSpec(memory_space=pl.ANY)
HBM = pl.BlockSpec(memory_space=pltpu.HBM)


def params(mib):
    return pltpu.CompilerParams(vmem_limit_bytes=mib * 1024 * 1024)


def cost(flops, moved):
    return pl.CostEstimate(flops=flops, bytes_accessed=moved, transcendentals=0)


def chunk_of(ref, c, n):
    return ref[pl.ds(c, n, stride=CHUNKS), :]


def row(i):
    return pl.ds(pl.multiple_of(i * CHUNKS, CHUNKS), CHUNKS)


def split(x):
    hi = x.astype(bf16)
    return hi, (x - hi.astype(f32)).astype(bf16)


def dot3(a, b, dims):
    (ah, al), (bh, bl) = a, b

    def one(p, q):
        return lax.dot_general(p, q, (dims, ((), ())), preferred_element_type=f32)

    return one(ah, bh) + (one(ah, bl) + one(al, bh))


def rows_loop(n, body):
    def step(s, carry):
        for u in range(UNROLL):
            body(s * UNROLL + u)
        return carry

    lax.fori_loop(0, n // UNROLL, step, 0)


def lane(n):
    return lax.broadcasted_iota(jnp.int32, (n, LANES), 1)


def join(c1, c3):
    return jnp.where(lane(c1.shape[0]) < 72, c1, pltpu.roll(c3, 72, 1))


def rest(c3, k):
    return pltpu.roll(c3, (72 + 16 * k) % LANES, 1)


def part(joined, rem, k):
    at = lane(joined.shape[0])
    c1 = jnp.where(at < 72, joined, 0.0)
    tail = jnp.where(at < 72, pltpu.roll(rem, (56 - 16 * k) % LANES, 1), 0.0)
    return c1, jnp.where(at < 56, pltpu.roll(joined, 56, 1), tail)


def four(ref, base, n):
    return [ref[pl.ds(base + c, n, stride=CHUNKS), :] for c in range(CHUNKS)]


def pack16(src, src_base, dst, dst_base):
    rem = None
    for k in range(2):
        c0, c1, c2, c3 = four(src, src_base + 32 * k, 8)
        dst[pl.ds(dst_base + 8 * k, 8), :] = c0
        dst[pl.ds(dst_base + 16 + 8 * k, 8), :] = c2
        dst[pl.ds(dst_base + 32 + 8 * k, 8), :] = join(c1, c3)
        rem = rest(c3, 0) if k == 0 else jnp.where(lane(8) < 16, rem, rest(c3, 1))
    dst[pl.ds(dst_base + 48, 8), :] = rem


def unpack16(src, src_base, dst, dst_base):
    rem = src[pl.ds(src_base + 48, 8), :]
    for k in range(2):
        c1, c3 = part(src[pl.ds(src_base + 32 + 8 * k, 8), :], rem, k)
        c0 = src[pl.ds(src_base + 8 * k, 8), :]
        c2 = src[pl.ds(src_base + 16 + 8 * k, 8), :]
        for c, piece in enumerate((c0, c1, c2, c3)):
            dst[pl.ds(dst_base + 32 * k + c, 8, stride=CHUNKS), :] = piece


def blocks_loop(n, unroll, body):
    def step(s, carry):
        for u in range(unroll):
            body(s * unroll + u)
        return carry

    lax.fori_loop(0, n // unroll, step, 0)


def pack_slots(src, src_base, dst):
    blocks_loop(N_DEV, 4, lambda d: pack16(src, src_base + d * CAP * CHUNKS, dst, d * PACK16))


def unpack_slots(src, dst, dst_base):
    blocks_loop(N_DEV, 4, lambda d: unpack16(src, d * PACK16, dst, dst_base + d * CAP * CHUNKS))


def pack66(src, src_base, dst, dst_base):
    rows = REL_DEV + NEG_DEV
    rem = None
    for k in range(9):
        n = 8 if k < 8 else 2
        c0, c1, c2, c3 = four(src, src_base + 32 * k, n)
        dst[pl.ds(dst_base + 8 * k, n), :] = c0
        dst[pl.ds(dst_base + rows + 8 * k, n), :] = c2
        dst[pl.ds(dst_base + 2 * rows + 8 * k, n), :] = join(c1, c3)
        if k == 8:
            dst[pl.ds(dst_base + 3 * rows + 8, 2), :] = rest(c3, 0)
        else:
            rem = rest(c3, k) if k == 0 else jnp.where(lane(8) < 16 * k, rem, rest(c3, k))
    dst[pl.ds(dst_base + 3 * rows, 8), :] = rem


def unpack66(src, src_base, dst, dst_base):
    rows = REL_DEV + NEG_DEV
    for k in range(9):
        n = 8 if k < 8 else 2
        rem = src[pl.ds(src_base + 3 * rows + (0 if k < 8 else 8), n), :]
        c1, c3 = part(src[pl.ds(src_base + 2 * rows + 8 * k, n), :], rem, k % 8)
        c0 = src[pl.ds(src_base + 8 * k, n), :]
        c2 = src[pl.ds(src_base + rows + 8 * k, n), :]
        for c, piece in enumerate((c0, c1, c2, c3)):
            dst[pl.ds(dst_base + 32 * k + c, n, stride=CHUNKS), :] = piece


def to_chunks(src, dst, n):
    for c, (start, size) in enumerate(SPANS):
        piece = src[start : start + size, :]
        if size < LANES:
            piece = jnp.concatenate([piece, jnp.zeros((LANES - size, n), f32)], axis=0)
        dst[pl.ds(c, n, stride=CHUNKS), :] = piece.T


def prep_kernel(negatives, table_t, rel_t, tab4, send, rel4):
    to_chunks(table_t, tab4, ENT_DEV)
    to_chunks(rel_t, rel4, LANES)
    for i in range(NEG_DEV):
        rel4[REL4 + CHUNKS * i : REL4 + CHUNKS * (i + 1), :] = tab4[row(negatives[i]), :]
    pack66(rel4, 0, send, 0)


def prep(negatives, table_t, rel_t):
    return pl.pallas_call(
        prep_kernel,
        out_shape=(
            jax.ShapeDtypeStruct((ENT_DEV * CHUNKS, LANES), f32),
            jax.ShapeDtypeStruct((PACK66, LANES), f32),
        ),
        in_specs=[SMEM, VMEM, VMEM],
        out_specs=(VMEM, VMEM),
        scratch_shapes=[pltpu.VMEM((LANES * CHUNKS, LANES), f32)],
        compiler_params=params(58),
        cost_estimate=cost(0, 8 << 20),
        name="prep",
    )(negatives, table_t, rel_t)


def pull_kernel(asked, tab4, out, picked, packed, sem):
    def body(i):
        picked[row(i), :] = tab4[row(asked[i]), :]

    rows_loop(SLOTS, body)
    pack_slots(picked, 0, packed)
    store = pltpu.make_async_copy(packed, out, sem)
    store.start()
    store.wait()


def pull_rows(asked, tab4):
    return pl.pallas_call(
        pull_kernel,
        out_shape=jax.ShapeDtypeStruct((N_DEV * PACK16, LANES), f32),
        in_specs=[SMEM, VMEM],
        out_specs=HBM,
        scratch_shapes=[
            pltpu.VMEM((SLOTS * CHUNKS, LANES), f32),
            pltpu.VMEM((N_DEV * PACK16, LANES), f32),
            pltpu.SemaphoreType.DMA,
        ],
        compiler_params=params(58),
        cost_estimate=cost(0, 8 << 20),
        name="pull_rows",
    )(asked, tab4)


def query_kernel(
    heads, rel_at, tab4, shared,
    q_out, h_out, r_out, back_out, neg_acc,
    tab, rel, packed, n_hi, n_lo, t_hi, t_lo, hb, rb, sems,
):
    step = pl.program_id(0)

    @pl.when(step == 0)
    def _():
        size = N_DEV * PACK66 // PIECES
        loads = [
            pltpu.make_async_copy(shared.at[pl.ds(i * size, size)], packed.at[pl.ds(i * size, size)], sems.at[i])
            for i in range(PIECES)
        ]
        loads.append(pltpu.make_async_copy(tab4, tab, sems.at[PIECES]))
        for load in loads:
            load.start()
        neg_acc[...] = jnp.zeros_like(neg_acc)
        each = N_DEV // PIECES
        for i in range(PIECES):
            loads[i].wait()
            blocks_loop(each, 2, lambda d, i=i: unpack66(packed, (i * each + d) * PACK66, rel, (i * each + d) * PER))
        loads[PIECES].wait()

        for c in range(CHUNKS):
            lanes = slice(c * LANES, (c + 1) * LANES)

            def place(d, carry, c=c):
                rows = pl.ds(pl.multiple_of(d * NEG_DEV, NEG_DEV), NEG_DEV)
                hb[rows, :] = rel[pl.ds(d * PER + REL4 + c, NEG_DEV, stride=CHUNKS), :]
                return carry

            lax.fori_loop(0, N_DEV, place, 0)
            piece = hb[...]
            n_hi[:, lanes], n_lo[:, lanes] = split(piece)
            t_hi[lanes, :], t_lo[lanes, :] = split(piece.T)

    base = step * TILE

    def gather(i):
        hb[row(i), :] = tab[row(heads[base + i]), :]
        rb[row(i), :] = rel[row(rel_at[base + i]), :]

    rows_loop(TILE, gather)
    h = [chunk_of(hb, c, TILE) for c in range(CHUNKS)]
    r = [chunk_of(rb, c, TILE) for c in range(CHUNKS)]
    q = [h[0] * r[0] - h[2] * r[2], h[1] * r[1] - h[3] * r[3], h[0] * r[2] + h[2] * r[0], h[1] * r[3] + h[3] * r[1]]
    for c in range(CHUNKS):
        q_out[c] = q[c]
        h_out[c] = h[c]
        r_out[c] = r[c]
    q = split(jnp.concatenate(q, axis=1))
    negative = dot3(q, (t_hi[...], t_lo[...]), ((1,), (0,)))
    neg_grad = split(jax.nn.sigmoid(negative) * (1.0 / NEG))
    neg_acc[...] += dot3(neg_grad, q, ((0,), (0,)))
    back = dot3(neg_grad, (n_hi[...], n_lo[...]), ((1,), (0,)))
    for c in range(CHUNKS):
        back_out[c] = back[:, c * LANES : (c + 1) * LANES]


PLANE = jax.ShapeDtypeStruct((CHUNKS, E_DEV, LANES), f32)
BLOCK = pl.BlockSpec((CHUNKS, TILE, LANES), lambda i: (0, i, 0))


def queries(heads, rel_at, tab4, shared):
    rows = pltpu.VMEM((TILE * CHUNKS, LANES), f32)
    wide = pltpu.VMEM((NEG, CHUNKS * LANES), bf16)
    tall = pltpu.VMEM((CHUNKS * LANES, NEG), bf16)
    return pl.pallas_call(
        query_kernel,
        grid=(E_DEV // TILE,),
        out_shape=(PLANE, PLANE, PLANE, PLANE, jax.ShapeDtypeStruct((NEG, CHUNKS * LANES), f32)),
        in_specs=[SMEM, SMEM, ANY, ANY],
        out_specs=(BLOCK, BLOCK, BLOCK, BLOCK, pl.BlockSpec((NEG, CHUNKS * LANES), lambda i: (0, 0))),
        scratch_shapes=[
            pltpu.VMEM((ENT_DEV * CHUNKS, LANES), f32),
            pltpu.VMEM((N_DEV * PER, LANES), f32),
            pltpu.VMEM((N_DEV * PACK66, LANES), f32),
            wide,
            wide,
            tall,
            tall,
            rows,
            rows,
            pltpu.SemaphoreType.DMA((PIECES + 1,)),
        ],
        compiler_params=params(58),
        cost_estimate=cost(36_000_000_000, 60 << 20),
        name="queries",
    )(heads, rel_at, tab4, shared)


def tail_kernel(
    tails, tab4, fetched, q_in,
    p_out, tail_local, outgoing,
    ext, ext_grad, packed, tb, sems,
):
    step = pl.program_id(0)
    local = ENT_DEV * CHUNKS

    @pl.when(step == 0)
    def _():
        loads = (
            pltpu.make_async_copy(fetched, packed, sems.at[1]),
            pltpu.make_async_copy(tab4, ext.at[pl.ds(0, local)], sems.at[0]),
        )
        for load in loads:
            load.start()
        ext_grad[...] = jnp.zeros_like(ext_grad)
        for load in loads:
            load.wait()
        unpack_slots(packed, ext, local)

    base = step * TILE

    def gather(i):
        tb[row(i), :] = ext[row(tails[base + i]), :]

    rows_loop(TILE, gather)
    t = [chunk_of(tb, c, TILE) for c in range(CHUNKS)]
    q = [q_in[c] for c in range(CHUNKS)]
    score = (q[0] * t[0] + q[1] * t[1]) + (q[2] * t[2] + q[3] * t[3])
    pos_grad = jax.nn.sigmoid(jnp.sum(score, axis=1, keepdims=True)) - 1.0
    for c in range(CHUNKS):
        p_out[c] = pos_grad * t[c]
        tb[pl.ds(c, TILE, stride=CHUNKS), :] = pos_grad * q[c]

    def scatter(i):
        at = row(tails[base + i])
        ext_grad[at, :] = ext_grad[at, :] + tb[row(i), :]

    rows_loop(TILE, scatter)

    @pl.when(step == E_DEV // TILE - 1)
    def _():
        stores = (
            pltpu.make_async_copy(ext_grad.at[pl.ds(0, local)], tail_local, sems.at[0]),
            pltpu.make_async_copy(packed, outgoing, sems.at[1]),
        )
        stores[0].start()
        pack_slots(ext_grad, local, packed)
        stores[1].start()
        for store in stores:
            store.wait()


def tail_terms(tails, tab4, fetched, q):
    return pl.pallas_call(
        tail_kernel,
        grid=(E_DEV // TILE,),
        out_shape=(
            PLANE,
            jax.ShapeDtypeStruct((ENT_DEV * CHUNKS, LANES), f32),
            jax.ShapeDtypeStruct((N_DEV * PACK16, LANES), f32),
        ),
        in_specs=[SMEM, ANY, ANY, BLOCK],
        out_specs=(BLOCK, HBM, HBM),
        scratch_shapes=[
            pltpu.VMEM(((ENT_DEV + SLOTS) * CHUNKS, LANES), f32),
            pltpu.VMEM(((ENT_DEV + SLOTS) * CHUNKS, LANES), f32),
            pltpu.VMEM((N_DEV * PACK16, LANES), f32),
            pltpu.VMEM((TILE * CHUNKS, LANES), f32),
            pltpu.SemaphoreType.DMA((2,)),
        ],
        compiler_params=params(58),
        cost_estimate=cost(0, 30 << 20),
        name="tail_terms",
    )(tails, tab4, fetched, q)


def edge_kernel(
    heads, grad_at, core, tail_local, neg_acc, h_in, r_in, p_in, back_in,
    mine, other0, other1, other2, other3, head_grad,
    rel_grad, packed, hb, rb, sems,
):
    step = pl.program_id(0)

    @pl.when(step == 0)
    def _():
        start = pltpu.make_async_copy(tail_local, head_grad, sems.at[0])
        start.start()
        rel_grad[...] = jnp.zeros_like(rel_grad)
        start.wait()

    base = step * TILE
    g = [p_in[c] + back_in[c] for c in range(CHUNKS)]
    for k in range(2):
        for buf, src in ((hb, r_in), (rb, h_in)):
            buf[pl.ds(k, TILE, stride=CHUNKS), :] = g[k] * src[k] + g[k + 2] * src[k + 2]
            buf[pl.ds(k + 2, TILE, stride=CHUNKS), :] = g[k + 2] * src[k] - g[k] * src[k + 2]

    def scatter(i):
        at = row(heads[base + i])
        rel = row(grad_at[base + i])
        head_grad[at, :] = head_grad[at, :] + hb[row(i), :]
        rel_grad[rel, :] = rel_grad[rel, :] + rb[row(i), :]

    rows_loop(TILE, scatter)

    @pl.when(step == E_DEV // TILE - 1)
    def _():
        def place(d, carry):
            spot = ((d % 2) * CHIPS + d // 2) * PER + REL4
            rows = pl.ds(pl.multiple_of(d * NEG_DEV, NEG_DEV), NEG_DEV)
            for c in range(CHUNKS):
                rel_grad[pl.ds(spot + c, NEG_DEV, stride=CHUNKS), :] = neg_acc[rows, c * LANES : (c + 1) * LANES]
            return carry

        lax.fori_loop(0, N_DEV, place, 0)
        side = core[0]
        size = CHIPS * PACK66 // PIECES
        stores = [
            pltpu.make_async_copy(packed.at[pl.ds(i * size, size)], other, sems.at[i])
            for i, other in enumerate((other0, other1, other2, other3))
        ]
        stores.append(pltpu.make_async_copy(packed.at[pl.ds(PIECES * size, PIECES * size)], mine, sems.at[PIECES]))

        def pack(d, owner, first):
            pack66(rel_grad, (owner * CHIPS + d) * PER, packed, (first + d) * PACK66)

        chips = CHIPS // PIECES
        for i in range(PIECES):
            blocks_loop(chips, 2, lambda d, i=i: pack(i * chips + d, 1 - side, 0))
            stores[i].start()
        blocks_loop(CHIPS, 2, lambda d: pack(d, side, CHIPS))
        stores[PIECES].start()
        for store in stores:
            store.wait()


def gradients(heads, grad_at, core, tail_local, neg_acc, h, r, p, back):
    half = jax.ShapeDtypeStruct((CHIPS * PACK66, LANES), f32)
    piece = jax.ShapeDtypeStruct((CHIPS * PACK66 // PIECES, LANES), f32)
    whole = pl.BlockSpec((ENT_DEV * CHUNKS, LANES), lambda i: (0, 0))
    return pl.pallas_call(
        edge_kernel,
        grid=(E_DEV // TILE,),
        out_shape=(half, piece, piece, piece, piece, jax.ShapeDtypeStruct((ENT_DEV * CHUNKS, LANES), f32)),
        in_specs=[SMEM, SMEM, SMEM, ANY, pl.BlockSpec((NEG, CHUNKS * LANES), lambda i: (0, 0)), BLOCK, BLOCK, BLOCK, BLOCK],
        out_specs=(HBM,) * 5 + (whole,),
        scratch_shapes=[
            pltpu.VMEM((N_DEV * PER, LANES), f32),
            pltpu.VMEM((N_DEV * PACK66, LANES), f32),
            pltpu.VMEM((TILE * CHUNKS, LANES), f32),
            pltpu.VMEM((TILE * CHUNKS, LANES), f32),
            pltpu.SemaphoreType.DMA((PIECES + 1,)),
        ],
        compiler_params=params(58),
        cost_estimate=cost(0, 1 << 20),
        name="gradients",
    )(heads, grad_at, core, tail_local, neg_acc, h, r, p, back)


def merge_kernel(
    color, mine, got0, got1, got2, got3,
    keep, send0, send1, send2, send3, send4, send5,
    total, came, sems, came_sems,
):
    each = CHIPS // PIECES
    loads, arrivals = [], []
    for i, got in enumerate((got0, got1, got2, got3)):
        here = pl.ds(i * each, each)
        loads.append(pltpu.make_async_copy(mine.at[here], total.at[here], sems.at[i]))
        arrivals.append(pltpu.make_async_copy(got, came.at[here], came_sems.at[i]))
        loads[i].start()
        arrivals[i].start()
    own = pl.ds(pl.multiple_of(color[0] * KEPT, 8), KEPT)
    theirs = pl.ds(pl.multiple_of((1 - color[0]) * KEPT, 8), KEPT)
    stores = [
        pltpu.make_async_copy(total.at[pl.ds(first, last - first), theirs], send, sems.at[PIECES + i])
        for i, (first, last, send) in enumerate(
            zip(GROUPS[:-1], GROUPS[1:], (send0, send1, send2, send3, send4, send5), strict=True)
        )
    ]
    stores.append(pltpu.make_async_copy(total.at[:, own], keep, sems.at[PIECES + 6]))
    started = 0
    for i in range(PIECES):
        loads[i].wait()
        arrivals[i].wait()

        def add(d, carry, i=i):
            total[i * each + d] = total[i * each + d] + came[i * each + d]
            return carry

        lax.fori_loop(0, each, add, 0)
        while started < 6 and GROUPS[started + 1] <= (i + 1) * each:
            stores[started].start()
            started += 1
    stores[6].start()
    for store in stores:
        store.wait()


def merge(color, mine, got):
    def blocks(n, rows):
        return jax.ShapeDtypeStruct((n, rows, LANES), f32)

    return pl.pallas_call(
        merge_kernel,
        out_shape=(blocks(CHIPS, KEPT),) + tuple(blocks(b - a, KEPT) for a, b in zip(GROUPS[:-1], GROUPS[1:], strict=True)),
        in_specs=[SMEM, ANY] + [ANY] * PIECES,
        out_specs=(HBM,) * 7,
        scratch_shapes=[
            pltpu.VMEM((CHIPS, PACK66, LANES), f32),
            pltpu.VMEM((CHIPS, PACK66, LANES), f32),
            pltpu.SemaphoreType.DMA((PIECES + 7,)),
            pltpu.SemaphoreType.DMA((PIECES,)),
        ],
        compiler_params=params(58),
        cost_estimate=cost(0, 1 << 16),
        name="merge",
    )(color, mine.reshape(CHIPS, PACK66, LANES), *[x.reshape(CHIPS // PIECES, PACK66, LANES) for x in got])


def meet_kernel(keep, got0, got1, got2, got3, got4, got5, out, total, came, sems, came_sems):
    spans = list(zip(GROUPS[:-1], GROUPS[1:], (got0, got1, got2, got3, got4, got5), strict=True))
    loads, arrivals, stores = [], [], []
    for i, (first, last, got) in enumerate(spans):
        here = pl.ds(first, last - first)
        loads.append(pltpu.make_async_copy(keep.at[here], total.at[here], sems.at[i]))
        stores.append(pltpu.make_async_copy(total.at[here], out.at[here], sems.at[6 + i]))
        arrivals.append(pltpu.make_async_copy(got, came.at[here], came_sems.at[i]))
        loads[i].start()
        arrivals[i].start()
    for i, (first, last, _) in enumerate(spans):
        loads[i].wait()
        arrivals[i].wait()

        def add(d, carry, first=first):
            total[first + d] = total[first + d] + came[first + d]
            return carry

        lax.fori_loop(0, last - first, add, 0)
        stores[i].start()
    for store in stores:
        store.wait()


def meet(keep, got):
    return pl.pallas_call(
        meet_kernel,
        out_shape=jax.ShapeDtypeStruct((CHIPS, KEPT, LANES), f32),
        in_specs=[ANY] * 7,
        out_specs=HBM,
        scratch_shapes=[
            pltpu.VMEM((CHIPS, KEPT, LANES), f32),
            pltpu.VMEM((CHIPS, KEPT, LANES), f32),
            pltpu.SemaphoreType.DMA((12,)),
            pltpu.SemaphoreType.DMA((6,)),
        ],
        compiler_params=params(58),
        cost_estimate=cost(0, 1 << 16),
        name="meet",
    )(keep, *got)


def color_of(chip):
    return (chip // 16 + chip // 4 + chip) % 2


def matching(k):
    pairs = []
    for chip in range(CHIPS):
        if color_of(chip) == 0:
            at = [chip // 16, chip // 4 % 4, chip % 4]
            at[k // 2] = (at[k // 2] + (1 if k % 2 == 0 else 3)) % 4
            mate = (at[0] * 4 + at[1]) * 4 + at[2]
            pairs += [(chip, mate), (mate, chip)]
    return pairs


def returned_kernel(asked, packed, head_grad, out, returned):
    out[...] = head_grad[...]
    unpack_slots(packed, returned, 0)

    def body(i):
        at = row(asked[i])
        out[at, :] = out[at, :] + returned[row(i), :]

    rows_loop(SLOTS, body)


def add_returned(asked, returned, head_grad):
    return pl.pallas_call(
        returned_kernel,
        out_shape=jax.ShapeDtypeStruct((ENT_DEV * CHUNKS, LANES), f32),
        in_specs=[SMEM, VMEM, VMEM],
        out_specs=VMEM,
        scratch_shapes=[pltpu.VMEM((SLOTS * CHUNKS, LANES), f32)],
        compiler_params=params(24),
        cost_estimate=cost(0, 10 << 20),
        name="add_returned",
    )(asked, returned, head_grad)


def adagrad(grad, n, table_t, state, new_table_t, new_state):
    g = [chunk_of(grad, c, n).T for c in range(CHUNKS)]
    squares = (g[0] * g[0] + g[1] * g[1]) + (g[2] * g[2] + g[3] * g[3])
    state_now = state[...] + jnp.sum(squares, axis=0, keepdims=True) * (1.0 / WIDTH)
    new_state[...] = state_now
    below = jnp.sqrt(state_now) + 1e-10
    for c, (start, size) in enumerate(SPANS):
        spot = slice(start, start + size)
        new_table_t[spot, :] = table_t[spot, :] - rate * g[c][:size] / below


def step_kernel(
    negatives, local_grad, parts, table_t, state, rel_t, rel_state,
    new_table_t, new_state, new_rel_t, new_rel_state,
    grad, share, packed,
):
    grad[...] = local_grad[...]
    share[...] = jnp.zeros_like(share)
    for half in range(2):
        total = None
        for chip in range(CHIPS):
            if color_of(chip) == half:
                total = parts[chip] if total is None else total + parts[chip]
        packed[half * KEPT : (half + 1) * KEPT, :] = total
    unpack66(packed, 0, share, 0)
    for i in range(NEG_DEV):
        at = row(negatives[i])
        grad[at, :] = grad[at, :] + share[REL4 + CHUNKS * i : REL4 + CHUNKS * (i + 1), :]
    adagrad(grad, ENT_DEV, table_t, state, new_table_t, new_state)
    adagrad(share, LANES, rel_t, rel_state, new_rel_t, new_rel_state)


def adagrad_step(negatives, local_grad, parts, table_t, state, rel_t, rel_state):
    def like(*shape):
        return jax.ShapeDtypeStruct(shape, f32)

    return pl.pallas_call(
        step_kernel,
        out_shape=(like(WIDTH, ENT_DEV), like(1, ENT_DEV), like(WIDTH, LANES), like(1, LANES)),
        in_specs=[SMEM] + [VMEM] * 6,
        out_specs=(VMEM,) * 4,
        scratch_shapes=[
            pltpu.VMEM((ENT_DEV * CHUNKS, LANES), f32),
            pltpu.VMEM((CHUNKS * LANES, LANES), f32),
            pltpu.VMEM((PACK66, LANES), f32),
        ],
        compiler_params=params(40),
        cost_estimate=cost(0, 16 << 20),
        name="adagrad_step",
    )(negatives, local_grad, parts, table_t, state, rel_t, rel_state)


def local(
    entity_table,
    entity_state,
    relation_table,
    relation_state,
    heads,
    relations,
    tails,
    pull_lists,
    negatives,
):
    table_t = entity_table.T
    rel_t = jnp.pad(relation_table, ((0, LANES - REL_DEV), (0, 0))).T
    owner, place = relations // REL_DEV, relations % REL_DEV
    rel_at = owner * (REL_DEV + NEG_DEV) + place
    grad_at = ((owner % 2) * CHIPS + owner // 2) * (REL_DEV + NEG_DEV) + place
    core = lax.axis_index("c")

    tab4, send = prep(negatives, table_t, rel_t)
    shared = lax.all_gather(send, AXES, axis=0, tiled=True)
    asked = lax.all_to_all(pull_lists, AXES, split_axis=0, concat_axis=0, tiled=True).reshape(SLOTS)
    rows_out, shared = lax.optimization_barrier((pull_rows(asked, tab4), shared))

    def exchange(rows):
        rows = rows.reshape(N_DEV, PACK16, LANES)
        return lax.all_to_all(rows, AXES, split_axis=0, concat_axis=0, tiled=True).reshape(N_DEV * PACK16, LANES)

    fetched = exchange(rows_out)
    q, h, r, back, neg_acc = queries(heads, rel_at, tab4, shared)
    p, tail_local, outgoing = tail_terms(tails, tab4, fetched, q)
    returned = exchange(outgoing)
    mine, *others, head_grad = gradients(
        heads, grad_at, core.reshape(1), tail_local, neg_acc, h, r, p, back
    )
    color = (lax.axis_index("x") + lax.axis_index("z") + lax.axis_index("y")) % 2
    got = [lax.ppermute(other, "c", [(0, 1), (1, 0)]) for other in others]
    merged = merge(color.reshape(1), mine, got)
    (keep, *sends), returned = lax.optimization_barrier((merged, returned))
    met = meet(keep, [lax.ppermute(send, AXES[:3], matching(k)) for k, send in enumerate(sends)])
    parts = lax.all_to_all(met, AXES[:3], split_axis=0, concat_axis=0, tiled=True)
    local_grad = add_returned(asked, returned, head_grad)
    new_table_t, new_state, new_rel_t, new_rel_state = adagrad_step(
        negatives,
        local_grad,
        parts,
        table_t,
        entity_state.reshape(1, ENT_DEV),
        rel_t,
        jnp.pad(relation_state, (0, LANES - REL_DEV)).reshape(1, LANES),
    )
    return (
        new_table_t.T,
        new_state.reshape(ENT_DEV),
        new_rel_t.T[:REL_DEV],
        new_rel_state.reshape(LANES)[:REL_DEV],
    )


def solution(mesh):
    grid = Mesh(mesh.devices.reshape(4, 4, 4, 2), AXES)
    rows, flat = P(AXES, None), P(AXES)
    in_specs = (rows, flat, rows, flat, flat, flat, flat, rows, flat)
    out_specs = (rows, flat, rows, flat)
    return jax.shard_map(local, mesh=grid, in_specs=in_specs, out_specs=out_specs, check_vma=False)
```

```python
import jax
import jax.numpy as jnp
from jax import lax
from jax.experimental import pallas as pl
from jax.experimental.pallas import tpu as pltpu
from jax.sharding import Mesh, PartitionSpec as P

rate = 0.1
AXES = ("x", "z", "y", "c")
WIDTH = 400
HALF = 200
LANES = 128
CHUNKS = 4
SPANS = ((0, 128), (128, 72), (200, 128), (328, 72))
ENT_DEV = 1024
REL_DEV = 58
NEG_DEV = 8
E_DEV = 2048
N_DEV = 128
CAP = 16
NEG = N_DEV * NEG_DEV
SLOTS = N_DEV * CAP
CHIPS = N_DEV // 2
PER = CHUNKS * (REL_DEV + NEG_DEV)
REL4 = CHUNKS * REL_DEV
TILE = 256
PACK16 = 56
PACK66 = 208
PIECES = 4
KEPT = PACK66 // 2
GROUPS = (0, 13, 26, 39, 52, 64)
WAYS = len(GROUPS) - 1
UNROLL = 8

f32 = jnp.float32
bf16 = jnp.bfloat16
VMEM = pl.BlockSpec(memory_space=pltpu.VMEM)
SMEM = pl.BlockSpec(memory_space=pltpu.SMEM)
ANY = pl.BlockSpec(memory_space=pl.ANY)
HBM = pl.BlockSpec(memory_space=pltpu.HBM)


def params(mib):
    return pltpu.CompilerParams(vmem_limit_bytes=mib * 1024 * 1024)


def cost(flops, moved):
    return pl.CostEstimate(flops=flops, bytes_accessed=moved, transcendentals=0)


def chunk_of(ref, c, n):
    return ref[pl.ds(c, n, stride=CHUNKS), :]


def row(i):
    return pl.ds(pl.multiple_of(i * CHUNKS, CHUNKS), CHUNKS)


def split(x):
    hi = x.astype(bf16)
    return hi, (x - hi.astype(f32)).astype(bf16)


def dot3(a, b, dims):
    (ah, al), (bh, bl) = a, b

    def one(p, q):
        return lax.dot_general(p, q, (dims, ((), ())), preferred_element_type=f32)

    return one(ah, bh) + (one(ah, bl) + one(al, bh))


def rows_loop(n, body):
    def step(s, carry):
        for u in range(UNROLL):
            body(s * UNROLL + u)
        return carry

    lax.fori_loop(0, n // UNROLL, step, 0)


def lane(n):
    return lax.broadcasted_iota(jnp.int32, (n, LANES), 1)


def join(c1, c3):
    return jnp.where(lane(c1.shape[0]) < 72, c1, pltpu.roll(c3, 72, 1))


def rest(c3, k):
    return pltpu.roll(c3, (72 + 16 * k) % LANES, 1)


def part(joined, rem, k):
    at = lane(joined.shape[0])
    c1 = jnp.where(at < 72, joined, 0.0)
    tail = jnp.where(at < 72, pltpu.roll(rem, (56 - 16 * k) % LANES, 1), 0.0)
    return c1, jnp.where(at < 56, pltpu.roll(joined, 56, 1), tail)


def four(ref, base, n):
    return [ref[pl.ds(base + c, n, stride=CHUNKS), :] for c in range(CHUNKS)]


def pack16(src, src_base, dst, dst_base):
    rem = None
    for k in range(2):
        c0, c1, c2, c3 = four(src, src_base + 32 * k, 8)
        dst[pl.ds(dst_base + 8 * k, 8), :] = c0
        dst[pl.ds(dst_base + 16 + 8 * k, 8), :] = c2
        dst[pl.ds(dst_base + 32 + 8 * k, 8), :] = join(c1, c3)
        rem = rest(c3, 0) if k == 0 else jnp.where(lane(8) < 16, rem, rest(c3, 1))
    dst[pl.ds(dst_base + 48, 8), :] = rem


def unpack16(src, src_base, dst, dst_base):
    rem = src[pl.ds(src_base + 48, 8), :]
    for k in range(2):
        c1, c3 = part(src[pl.ds(src_base + 32 + 8 * k, 8), :], rem, k)
        c0 = src[pl.ds(src_base + 8 * k, 8), :]
        c2 = src[pl.ds(src_base + 16 + 8 * k, 8), :]
        for c, piece in enumerate((c0, c1, c2, c3)):
            dst[pl.ds(dst_base + 32 * k + c, 8, stride=CHUNKS), :] = piece


def blocks_loop(n, unroll, body):
    def step(s, carry):
        for u in range(unroll):
            body(s * unroll + u)
        return carry

    lax.fori_loop(0, n // unroll, step, 0)


def pack_slots(src, src_base, dst):
    blocks_loop(N_DEV, 4, lambda d: pack16(src, src_base + d * CAP * CHUNKS, dst, d * PACK16))


def unpack_slots(src, dst, dst_base):
    blocks_loop(N_DEV, 4, lambda d: unpack16(src, d * PACK16, dst, dst_base + d * CAP * CHUNKS))


def pack66(src, src_base, dst, dst_base):
    rows = REL_DEV + NEG_DEV
    rem = None
    for k in range(9):
        n = 8 if k < 8 else 2
        c0, c1, c2, c3 = four(src, src_base + 32 * k, n)
        dst[pl.ds(dst_base + 8 * k, n), :] = c0
        dst[pl.ds(dst_base + rows + 8 * k, n), :] = c2
        dst[pl.ds(dst_base + 2 * rows + 8 * k, n), :] = join(c1, c3)
        if k == 8:
            dst[pl.ds(dst_base + 3 * rows + 8, 2), :] = rest(c3, 0)
        else:
            rem = rest(c3, k) if k == 0 else jnp.where(lane(8) < 16 * k, rem, rest(c3, k))
    dst[pl.ds(dst_base + 3 * rows, 8), :] = rem


def unpack66(src, src_base, dst, dst_base):
    rows = REL_DEV + NEG_DEV
    for k in range(9):
        n = 8 if k < 8 else 2
        rem = src[pl.ds(src_base + 3 * rows + (0 if k < 8 else 8), n), :]
        c1, c3 = part(src[pl.ds(src_base + 2 * rows + 8 * k, n), :], rem, k % 8)
        c0 = src[pl.ds(src_base + 8 * k, n), :]
        c2 = src[pl.ds(src_base + rows + 8 * k, n), :]
        for c, piece in enumerate((c0, c1, c2, c3)):
            dst[pl.ds(dst_base + 32 * k + c, n, stride=CHUNKS), :] = piece


def to_chunks(src, dst, n):
    for c, (start, size) in enumerate(SPANS):
        piece = src[start : start + size, :]
        if size < LANES:
            piece = jnp.concatenate([piece, jnp.zeros((LANES - size, n), f32)], axis=0)
        dst[pl.ds(c, n, stride=CHUNKS), :] = piece.T


def prep_kernel(negatives, table_t, rel_t, tab4, send, rel4):
    to_chunks(table_t, tab4, ENT_DEV)
    to_chunks(rel_t, rel4, LANES)
    for i in range(NEG_DEV):
        rel4[REL4 + CHUNKS * i : REL4 + CHUNKS * (i + 1), :] = tab4[row(negatives[i]), :]
    pack66(rel4, 0, send, 0)


def prep(negatives, table_t, rel_t):
    return pl.pallas_call(
        prep_kernel,
        out_shape=(
            jax.ShapeDtypeStruct((ENT_DEV * CHUNKS, LANES), f32),
            jax.ShapeDtypeStruct((PACK66, LANES), f32),
        ),
        in_specs=[SMEM, VMEM, VMEM],
        out_specs=(VMEM, VMEM),
        scratch_shapes=[pltpu.VMEM((LANES * CHUNKS, LANES), f32)],
        compiler_params=params(58),
        cost_estimate=cost(0, 8 << 20),
        name="prep",
    )(negatives, table_t, rel_t)


def pull_kernel(asked, tab4, out, picked, packed, sem):
    def body(i):
        picked[row(i), :] = tab4[row(asked[i]), :]

    rows_loop(SLOTS, body)
    pack_slots(picked, 0, packed)
    store = pltpu.make_async_copy(packed, out, sem)
    store.start()
    store.wait()


def pull_rows(asked, tab4):
    return pl.pallas_call(
        pull_kernel,
        out_shape=jax.ShapeDtypeStruct((N_DEV * PACK16, LANES), f32),
        in_specs=[SMEM, VMEM],
        out_specs=HBM,
        scratch_shapes=[
            pltpu.VMEM((SLOTS * CHUNKS, LANES), f32),
            pltpu.VMEM((N_DEV * PACK16, LANES), f32),
            pltpu.SemaphoreType.DMA,
        ],
        compiler_params=params(58),
        cost_estimate=cost(0, 8 << 20),
        name="pull_rows",
    )(asked, tab4)


def query_kernel(
    heads, rel_at, tab4, shared,
    q_out, h_out, r_out, back_out, neg_acc,
    tab, rel, packed, n_hi, n_lo, t_hi, t_lo, hb, rb, sems,
):
    step = pl.program_id(0)

    @pl.when(step == 0)
    def _():
        size = N_DEV * PACK66 // PIECES
        loads = [
            pltpu.make_async_copy(shared.at[pl.ds(i * size, size)], packed.at[pl.ds(i * size, size)], sems.at[i])
            for i in range(PIECES)
        ]
        loads.append(pltpu.make_async_copy(tab4, tab, sems.at[PIECES]))
        for load in loads:
            load.start()
        neg_acc[...] = jnp.zeros_like(neg_acc)
        each = N_DEV // PIECES
        for i in range(PIECES):
            loads[i].wait()
            blocks_loop(each, 2, lambda d, i=i: unpack66(packed, (i * each + d) * PACK66, rel, (i * each + d) * PER))
        loads[PIECES].wait()

        for c in range(CHUNKS):
            lanes = slice(c * LANES, (c + 1) * LANES)

            def place(d, carry, c=c):
                rows = pl.ds(pl.multiple_of(d * NEG_DEV, NEG_DEV), NEG_DEV)
                hb[rows, :] = rel[pl.ds(d * PER + REL4 + c, NEG_DEV, stride=CHUNKS), :]
                return carry

            lax.fori_loop(0, N_DEV, place, 0)
            piece = hb[...]
            n_hi[:, lanes], n_lo[:, lanes] = split(piece)
            t_hi[lanes, :], t_lo[lanes, :] = split(piece.T)

    base = step * TILE

    def gather(i):
        hb[row(i), :] = tab[row(heads[base + i]), :]
        rb[row(i), :] = rel[row(rel_at[base + i]), :]

    rows_loop(TILE, gather)
    h = [chunk_of(hb, c, TILE) for c in range(CHUNKS)]
    r = [chunk_of(rb, c, TILE) for c in range(CHUNKS)]
    q = [h[0] * r[0] - h[2] * r[2], h[1] * r[1] - h[3] * r[3], h[0] * r[2] + h[2] * r[0], h[1] * r[3] + h[3] * r[1]]
    for c in range(CHUNKS):
        q_out[c] = q[c]
        h_out[c] = h[c]
        r_out[c] = r[c]
    q = split(jnp.concatenate(q, axis=1))
    negative = dot3(q, (t_hi[...], t_lo[...]), ((1,), (0,)))
    neg_grad = split(jax.nn.sigmoid(negative) * (1.0 / NEG))
    neg_acc[...] += dot3(neg_grad, q, ((0,), (0,)))
    back = dot3(neg_grad, (n_hi[...], n_lo[...]), ((1,), (0,)))
    for c in range(CHUNKS):
        back_out[c] = back[:, c * LANES : (c + 1) * LANES]


PLANE = jax.ShapeDtypeStruct((CHUNKS, E_DEV, LANES), f32)
BLOCK = pl.BlockSpec((CHUNKS, TILE, LANES), lambda i: (0, i, 0))


def queries(heads, rel_at, tab4, shared):
    rows = pltpu.VMEM((TILE * CHUNKS, LANES), f32)
    wide = pltpu.VMEM((NEG, CHUNKS * LANES), bf16)
    tall = pltpu.VMEM((CHUNKS * LANES, NEG), bf16)
    return pl.pallas_call(
        query_kernel,
        grid=(E_DEV // TILE,),
        out_shape=(PLANE, PLANE, PLANE, PLANE, jax.ShapeDtypeStruct((NEG, CHUNKS * LANES), f32)),
        in_specs=[SMEM, SMEM, ANY, ANY],
        out_specs=(BLOCK, BLOCK, BLOCK, BLOCK, pl.BlockSpec((NEG, CHUNKS * LANES), lambda i: (0, 0))),
        scratch_shapes=[
            pltpu.VMEM((ENT_DEV * CHUNKS, LANES), f32),
            pltpu.VMEM((N_DEV * PER, LANES), f32),
            pltpu.VMEM((N_DEV * PACK66, LANES), f32),
            wide,
            wide,
            tall,
            tall,
            rows,
            rows,
            pltpu.SemaphoreType.DMA((PIECES + 1,)),
        ],
        compiler_params=params(58),
        cost_estimate=cost(36_000_000_000, 60 << 20),
        name="queries",
    )(heads, rel_at, tab4, shared)


def tail_kernel(
    tails, tab4, fetched, q_in,
    p_out, tail_local, outgoing,
    ext, ext_grad, packed, tb, sems,
):
    step = pl.program_id(0)
    local = ENT_DEV * CHUNKS
    size = N_DEV * PACK16 // PIECES
    each = N_DEV // PIECES

    @pl.when(step == 0)
    def _():
        loads = []
        for i in range(PIECES):
            here = pl.ds(i * size, size)
            loads.append(pltpu.make_async_copy(fetched.at[here], packed.at[here], sems.at[i]))
        loads.append(pltpu.make_async_copy(tab4, ext.at[pl.ds(0, local)], sems.at[PIECES]))
        for load in loads:
            load.start()
        ext_grad[...] = jnp.zeros_like(ext_grad)
        for i in range(PIECES):
            loads[i].wait()

            def unpack(d, i=i):
                unpack16(packed, (i * each + d) * PACK16, ext, local + (i * each + d) * CAP * CHUNKS)

            blocks_loop(each, 4, unpack)
        loads[PIECES].wait()

    base = step * TAIL_TILE

    def gather(i):
        tb[row(i), :] = ext[row(tails[base + i]), :]

    rows_loop(TAIL_TILE, gather)
    t = [chunk_of(tb, c, TAIL_TILE) for c in range(CHUNKS)]
    q = [q_in[c] for c in range(CHUNKS)]
    score = (q[0] * t[0] + q[1] * t[1]) + (q[2] * t[2] + q[3] * t[3])
    pos_grad = jax.nn.sigmoid(jnp.sum(score, axis=1, keepdims=True)) - 1.0
    for c in range(CHUNKS):
        p_out[c] = pos_grad * t[c]
        tb[pl.ds(c, TAIL_TILE, stride=CHUNKS), :] = pos_grad * q[c]

    def scatter(i):
        at = row(tails[base + i])
        ext_grad[at, :] = ext_grad[at, :] + tb[row(i), :]

    rows_loop(TAIL_TILE, scatter)

    @pl.when(step == E_DEV // TAIL_TILE - 1)
    def _():
        stores = []
        for i in range(PIECES):
            here = pl.ds(i * size, size)
            stores.append(pltpu.make_async_copy(packed.at[here], outgoing.at[here], sems.at[i]))
        stores.append(pltpu.make_async_copy(ext_grad.at[pl.ds(0, local)], tail_local, sems.at[PIECES]))
        stores[PIECES].start()
        for i in range(PIECES):

            def pack(d, i=i):
                pack16(ext_grad, local + (i * each + d) * CAP * CHUNKS, packed, (i * each + d) * PACK16)

            blocks_loop(each, 4, pack)
            stores[i].start()
        for store in stores:
            store.wait()


TAIL_TILE = 512


def tail_terms(tails, tab4, fetched, q):
    block = pl.BlockSpec((CHUNKS, TAIL_TILE, LANES), lambda i: (0, i, 0))
    return pl.pallas_call(
        tail_kernel,
        grid=(E_DEV // TAIL_TILE,),
        out_shape=(
            PLANE,
            jax.ShapeDtypeStruct((ENT_DEV * CHUNKS, LANES), f32),
            jax.ShapeDtypeStruct((N_DEV * PACK16, LANES), f32),
        ),
        in_specs=[SMEM, ANY, ANY, block],
        out_specs=(block, HBM, HBM),
        scratch_shapes=[
            pltpu.VMEM(((ENT_DEV + SLOTS) * CHUNKS, LANES), f32),
            pltpu.VMEM(((ENT_DEV + SLOTS) * CHUNKS, LANES), f32),
            pltpu.VMEM((N_DEV * PACK16, LANES), f32),
            pltpu.VMEM((TAIL_TILE * CHUNKS, LANES), f32),
            pltpu.SemaphoreType.DMA((PIECES + 1,)),
        ],
        compiler_params=params(58),
        cost_estimate=cost(0, 30 << 20),
        name="tail_terms",
    )(tails, tab4, fetched, q)


def edge_kernel(
    heads, grad_at, core, tail_local, neg_acc, h_in, r_in, p_in, back_in,
    mine, other0, other1, other2, other3, head_grad,
    rel_grad, packed, hb, rb, sems,
):
    step = pl.program_id(0)

    @pl.when(step == 0)
    def _():
        start = pltpu.make_async_copy(tail_local, head_grad, sems.at[0])
        start.start()
        rel_grad[...] = jnp.zeros_like(rel_grad)
        start.wait()

    base = step * TILE
    g = [p_in[c] + back_in[c] for c in range(CHUNKS)]
    for k in range(2):
        for buf, src in ((hb, r_in), (rb, h_in)):
            buf[pl.ds(k, TILE, stride=CHUNKS), :] = g[k] * src[k] + g[k + 2] * src[k + 2]
            buf[pl.ds(k + 2, TILE, stride=CHUNKS), :] = g[k + 2] * src[k] - g[k] * src[k + 2]

    def scatter(i):
        at = row(heads[base + i])
        rel = row(grad_at[base + i])
        head_grad[at, :] = head_grad[at, :] + hb[row(i), :]
        rel_grad[rel, :] = rel_grad[rel, :] + rb[row(i), :]

    rows_loop(TILE, scatter)

    @pl.when(step == E_DEV // TILE - 1)
    def _():
        def place(d, carry):
            spot = ((d % 2) * CHIPS + d // 2) * PER + REL4
            rows = pl.ds(pl.multiple_of(d * NEG_DEV, NEG_DEV), NEG_DEV)
            for c in range(CHUNKS):
                rel_grad[pl.ds(spot + c, NEG_DEV, stride=CHUNKS), :] = neg_acc[rows, c * LANES : (c + 1) * LANES]
            return carry

        lax.fori_loop(0, N_DEV, place, 0)
        side = core[0]
        size = CHIPS * PACK66 // PIECES
        stores = [
            pltpu.make_async_copy(packed.at[pl.ds(i * size, size)], other, sems.at[i])
            for i, other in enumerate((other0, other1, other2, other3))
        ]
        stores.append(pltpu.make_async_copy(packed.at[pl.ds(PIECES * size, PIECES * size)], mine, sems.at[PIECES]))

        def pack(d, owner, first):
            pack66(rel_grad, (owner * CHIPS + d) * PER, packed, (first + d) * PACK66)

        chips = CHIPS // PIECES
        for i in range(PIECES):
            blocks_loop(chips, 2, lambda d, i=i: pack(i * chips + d, 1 - side, 0))
            stores[i].start()
        blocks_loop(CHIPS, 2, lambda d: pack(d, side, CHIPS))
        stores[PIECES].start()
        for store in stores:
            store.wait()


def gradients(heads, grad_at, core, tail_local, neg_acc, h, r, p, back):
    half = jax.ShapeDtypeStruct((CHIPS * PACK66, LANES), f32)
    piece = jax.ShapeDtypeStruct((CHIPS * PACK66 // PIECES, LANES), f32)
    whole = pl.BlockSpec((ENT_DEV * CHUNKS, LANES), lambda i: (0, 0))
    return pl.pallas_call(
        edge_kernel,
        grid=(E_DEV // TILE,),
        out_shape=(half, piece, piece, piece, piece, jax.ShapeDtypeStruct((ENT_DEV * CHUNKS, LANES), f32)),
        in_specs=[SMEM, SMEM, SMEM, ANY, pl.BlockSpec((NEG, CHUNKS * LANES), lambda i: (0, 0)), BLOCK, BLOCK, BLOCK, BLOCK],
        out_specs=(HBM,) * 5 + (whole,),
        scratch_shapes=[
            pltpu.VMEM((N_DEV * PER, LANES), f32),
            pltpu.VMEM((N_DEV * PACK66, LANES), f32),
            pltpu.VMEM((TILE * CHUNKS, LANES), f32),
            pltpu.VMEM((TILE * CHUNKS, LANES), f32),
            pltpu.SemaphoreType.DMA((PIECES + 1,)),
        ],
        compiler_params=params(58),
        cost_estimate=cost(0, 1 << 20),
        name="gradients",
    )(heads, grad_at, core, tail_local, neg_acc, h, r, p, back)


def merge_kernel(
    color, mine, got0, got1, got2, got3,
    keep, send0, send1, send2, send3, send4,
    total, came, sems, came_sems,
):
    each = CHIPS // PIECES
    loads, arrivals = [], []
    for i, got in enumerate((got0, got1, got2, got3)):
        here = pl.ds(i * each, each)
        loads.append(pltpu.make_async_copy(mine.at[here], total.at[here], sems.at[i]))
        arrivals.append(pltpu.make_async_copy(got, came.at[here], came_sems.at[i]))
        loads[i].start()
        arrivals[i].start()
    own = pl.ds(pl.multiple_of(color[0] * KEPT, 8), KEPT)
    theirs = pl.ds(pl.multiple_of((1 - color[0]) * KEPT, 8), KEPT)
    stores = [
        pltpu.make_async_copy(total.at[pl.ds(first, last - first), theirs], send, sems.at[PIECES + i])
        for i, (first, last, send) in enumerate(
            zip(GROUPS[:-1], GROUPS[1:], (send0, send1, send2, send3, send4), strict=True)
        )
    ]
    stores.append(pltpu.make_async_copy(total.at[:, own], keep, sems.at[PIECES + WAYS]))
    started = 0
    for i in range(PIECES):
        loads[i].wait()
        arrivals[i].wait()

        def add(d, carry, i=i):
            total[i * each + d] = total[i * each + d] + came[i * each + d]
            return carry

        lax.fori_loop(0, each, add, 0)
        while started < WAYS and GROUPS[started + 1] <= (i + 1) * each:
            stores[started].start()
            started += 1
    stores[WAYS].start()
    for store in stores:
        store.wait()


def merge(color, mine, got):
    def blocks(n, rows):
        return jax.ShapeDtypeStruct((n, rows, LANES), f32)

    return pl.pallas_call(
        merge_kernel,
        out_shape=(blocks(CHIPS, KEPT),) + tuple(blocks(b - a, KEPT) for a, b in zip(GROUPS[:-1], GROUPS[1:], strict=True)),
        in_specs=[SMEM, ANY] + [ANY] * PIECES,
        out_specs=(HBM,) * (WAYS + 1),
        scratch_shapes=[
            pltpu.VMEM((CHIPS, PACK66, LANES), f32),
            pltpu.VMEM((CHIPS, PACK66, LANES), f32),
            pltpu.SemaphoreType.DMA((PIECES + WAYS + 1,)),
            pltpu.SemaphoreType.DMA((PIECES,)),
        ],
        compiler_params=params(58),
        cost_estimate=cost(0, 1 << 16),
        name="merge",
    )(color, mine.reshape(CHIPS, PACK66, LANES), *[x.reshape(CHIPS // PIECES, PACK66, LANES) for x in got])


def meet_kernel(keep, got0, got1, got2, got3, got4, out, total, sems):
    spans = list(zip(GROUPS[:-1], GROUPS[1:], (got0, got1, got2, got3, got4), strict=True))
    loads, stores = [], []
    for i, (first, last, _) in enumerate(spans):
        here = pl.ds(first, last - first)
        loads.append(pltpu.make_async_copy(keep.at[here], total.at[here], sems.at[i]))
        stores.append(pltpu.make_async_copy(total.at[here], out.at[here], sems.at[WAYS + i]))
        loads[i].start()
    for i, (first, last, got) in enumerate(spans):
        loads[i].wait()

        def add(d, carry, first=first, got=got):
            total[first + d] = total[first + d] + got[d]
            return carry

        lax.fori_loop(0, last - first, add, 0)
        stores[i].start()
    for store in stores:
        store.wait()


def meet(keep, got):
    return pl.pallas_call(
        meet_kernel,
        out_shape=jax.ShapeDtypeStruct((CHIPS, KEPT, LANES), f32),
        in_specs=[ANY] + [VMEM] * WAYS,
        out_specs=HBM,
        scratch_shapes=[pltpu.VMEM((CHIPS, KEPT, LANES), f32), pltpu.SemaphoreType.DMA((2 * WAYS,))],
        compiler_params=params(16),
        cost_estimate=cost(0, 1 << 16),
        name="meet",
    )(keep, *got)


def color_of(chip):
    return (chip // 16 + chip // 4 + chip) % 2


def matching(k):
    pairs = []
    for chip in range(CHIPS):
        if color_of(chip) == 0:
            at = [chip // 16, chip // 4 % 4, chip % 4]
            at[k // 2] = (at[k // 2] + (1 if k % 2 == 0 else 3)) % 4
            mate = (at[0] * 4 + at[1]) * 4 + at[2]
            pairs += [(chip, mate), (mate, chip)]
    return pairs


def returned_kernel(asked, packed, head_grad, out, returned):
    out[...] = head_grad[...]
    unpack_slots(packed, returned, 0)

    def body(i):
        at = row(asked[i])
        out[at, :] = out[at, :] + returned[row(i), :]

    rows_loop(SLOTS, body)


def add_returned(asked, returned, head_grad):
    return pl.pallas_call(
        returned_kernel,
        out_shape=jax.ShapeDtypeStruct((ENT_DEV * CHUNKS, LANES), f32),
        in_specs=[SMEM, VMEM, VMEM],
        out_specs=VMEM,
        scratch_shapes=[pltpu.VMEM((SLOTS * CHUNKS, LANES), f32)],
        compiler_params=params(24),
        cost_estimate=cost(0, 10 << 20),
        name="add_returned",
    )(asked, returned, head_grad)


def adagrad(grad, n, table_t, state, new_table_t, new_state):
    g = [chunk_of(grad, c, n).T for c in range(CHUNKS)]
    squares = (g[0] * g[0] + g[1] * g[1]) + (g[2] * g[2] + g[3] * g[3])
    state_now = state[...] + jnp.sum(squares, axis=0, keepdims=True) * (1.0 / WIDTH)
    new_state[...] = state_now
    below = jnp.sqrt(state_now) + 1e-10
    for c, (start, size) in enumerate(SPANS):
        spot = slice(start, start + size)
        new_table_t[spot, :] = table_t[spot, :] - rate * g[c][:size] / below


def step_kernel(
    negatives, local_grad, parts, table_now, state, rel_t, rel_state,
    new_table_t, new_state, new_rel_t, new_rel_state,
    grad, came, table_t, share, packed, sems,
):
    each = CHIPS // PIECES
    loads = []
    for i in range(PIECES):
        here = pl.ds(i * each, each)
        loads.append(pltpu.make_async_copy(parts.at[here], came.at[here], sems.at[i]))
    loads.append(pltpu.make_async_copy(local_grad, grad, sems.at[PIECES]))
    loads.append(pltpu.make_async_copy(table_now, table_t, sems.at[PIECES + 1]))
    for load in loads:
        load.start()
    share[...] = jnp.zeros_like(share)
    totals = [None, None]
    for i in range(PIECES):
        loads[i].wait()
        for chip in range(i * each, (i + 1) * each):
            half = color_of(chip)
            totals[half] = came[chip] if totals[half] is None else totals[half] + came[chip]
    packed[0:KEPT, :] = totals[0]
    packed[KEPT:PACK66, :] = totals[1]
    unpack66(packed, 0, share, 0)
    adagrad(share, LANES, rel_t, rel_state, new_rel_t, new_rel_state)
    loads[PIECES].wait()
    for i in range(NEG_DEV):
        at = row(negatives[i])
        grad[at, :] = grad[at, :] + share[REL4 + CHUNKS * i : REL4 + CHUNKS * (i + 1), :]
    loads[PIECES + 1].wait()
    adagrad(grad, ENT_DEV, table_t, state, new_table_t, new_state)


def adagrad_step(negatives, local_grad, parts, table_t, state, rel_t, rel_state):
    def like(*shape):
        return jax.ShapeDtypeStruct(shape, f32)

    return pl.pallas_call(
        step_kernel,
        out_shape=(like(WIDTH, ENT_DEV), like(1, ENT_DEV), like(WIDTH, LANES), like(1, LANES)),
        in_specs=[SMEM, ANY, ANY, ANY] + [VMEM] * 3,
        out_specs=(VMEM,) * 4,
        scratch_shapes=[
            pltpu.VMEM((ENT_DEV * CHUNKS, LANES), f32),
            pltpu.VMEM((CHIPS, KEPT, LANES), f32),
            pltpu.VMEM((WIDTH, ENT_DEV), f32),
            pltpu.VMEM((CHUNKS * LANES, LANES), f32),
            pltpu.VMEM((PACK66, LANES), f32),
            pltpu.SemaphoreType.DMA((PIECES + 2,)),
        ],
        compiler_params=params(58),
        cost_estimate=cost(0, 16 << 20),
        name="adagrad_step",
    )(negatives, local_grad, parts, table_t, state, rel_t, rel_state)


def local(
    entity_table,
    entity_state,
    relation_table,
    relation_state,
    heads,
    relations,
    tails,
    pull_lists,
    negatives,
):
    table_t = entity_table.T
    rel_t = jnp.pad(relation_table, ((0, LANES - REL_DEV), (0, 0))).T
    owner, place = relations // REL_DEV, relations % REL_DEV
    rel_at = owner * (REL_DEV + NEG_DEV) + place
    grad_at = ((owner % 2) * CHIPS + owner // 2) * (REL_DEV + NEG_DEV) + place
    core = lax.axis_index("c")

    tab4, send = prep(negatives, table_t, rel_t)
    shared = lax.all_gather(send, AXES, axis=0, tiled=True)
    asked = lax.all_to_all(pull_lists, AXES, split_axis=0, concat_axis=0, tiled=True).reshape(SLOTS)
    rows_out, shared = lax.optimization_barrier((pull_rows(asked, tab4), shared))

    def exchange(rows):
        rows = rows.reshape(N_DEV, PACK16, LANES)
        return lax.all_to_all(rows, AXES, split_axis=0, concat_axis=0, tiled=True).reshape(N_DEV * PACK16, LANES)

    fetched = exchange(rows_out)
    q, h, r, back, neg_acc = queries(heads, rel_at, tab4, shared)
    p, tail_local, outgoing = tail_terms(tails, tab4, fetched, q)
    returned = exchange(outgoing)
    mine, *others, head_grad = gradients(
        heads, grad_at, core.reshape(1), tail_local, neg_acc, h, r, p, back
    )
    color = (lax.axis_index("x") + lax.axis_index("z") + lax.axis_index("y")) % 2
    got = [lax.ppermute(other, "c", [(0, 1), (1, 0)]) for other in others]
    merged = merge(color.reshape(1), mine, got)
    (keep, *sends), returned = lax.optimization_barrier((merged, returned))
    met = meet(keep, [lax.ppermute(send, AXES[:3], matching(k)) for k, send in enumerate(sends)])
    parts = lax.all_to_all(met, AXES[:3], split_axis=0, concat_axis=0, tiled=True)
    local_grad = add_returned(asked, returned, head_grad)
    new_table_t, new_state, new_rel_t, new_rel_state = adagrad_step(
        negatives,
        local_grad,
        parts,
        table_t,
        entity_state.reshape(1, ENT_DEV),
        rel_t,
        jnp.pad(relation_state, (0, LANES - REL_DEV)).reshape(1, LANES),
    )
    return (
        new_table_t.T,
        new_state.reshape(ENT_DEV),
        new_rel_t.T[:REL_DEV],
        new_rel_state.reshape(LANES)[:REL_DEV],
    )


def solution(mesh):
    grid = Mesh(mesh.devices.reshape(4, 4, 4, 2), AXES)
    rows, flat = P(AXES, None), P(AXES)
    in_specs = (rows, flat, rows, flat, flat, flat, flat, rows, flat)
    out_specs = (rows, flat, rows, flat)
    return jax.shard_map(local, mesh=grid, in_specs=in_specs, out_specs=out_specs, check_vma=False)
```

```python
import jax
import jax.numpy as jnp
from jax import lax
from jax.experimental import pallas as pl
from jax.experimental.pallas import tpu as pltpu
from jax.sharding import Mesh, PartitionSpec as P

rate = 0.1
AXES = ("x", "z", "y", "c")
WIDTH = 400
HALF = 200
LANES = 128
CHUNKS = 4
SPANS = ((0, 128), (128, 72), (200, 128), (328, 72))
ENT_DEV = 1024
REL_DEV = 58
NEG_DEV = 8
E_DEV = 2048
N_DEV = 128
CAP = 16
NEG = N_DEV * NEG_DEV
SLOTS = N_DEV * CAP
CHIPS = N_DEV // 2
PER = CHUNKS * (REL_DEV + NEG_DEV)
REL4 = CHUNKS * REL_DEV
TILE = 256
PACK16 = 56
PACK66 = 208
PIECES = 4
KEPT = PACK66 // 2
GROUPS = (0, 13, 26, 39, 52, 64)
WAYS = len(GROUPS) - 1
UNROLL = 8

f32 = jnp.float32
bf16 = jnp.bfloat16
VMEM = pl.BlockSpec(memory_space=pltpu.VMEM)
SMEM = pl.BlockSpec(memory_space=pltpu.SMEM)
ANY = pl.BlockSpec(memory_space=pl.ANY)
HBM = pl.BlockSpec(memory_space=pltpu.HBM)


def params(mib):
    return pltpu.CompilerParams(vmem_limit_bytes=mib * 1024 * 1024)


def cost(flops, moved):
    return pl.CostEstimate(flops=flops, bytes_accessed=moved, transcendentals=0)


def chunk_of(ref, c, n):
    return ref[pl.ds(c, n, stride=CHUNKS), :]


def row(i):
    return pl.ds(pl.multiple_of(i * CHUNKS, CHUNKS), CHUNKS)


def split(x):
    hi = x.astype(bf16)
    return hi, (x - hi.astype(f32)).astype(bf16)


def dot3(a, b, dims):
    (ah, al), (bh, bl) = a, b

    def one(p, q):
        return lax.dot_general(p, q, (dims, ((), ())), preferred_element_type=f32)

    return one(ah, bh) + (one(ah, bl) + one(al, bh))


def rows_loop(n, body):
    def step(s, carry):
        for u in range(UNROLL):
            body(s * UNROLL + u)
        return carry

    lax.fori_loop(0, n // UNROLL, step, 0)


def lane(n):
    return lax.broadcasted_iota(jnp.int32, (n, LANES), 1)


def join(c1, c3):
    return jnp.where(lane(c1.shape[0]) < 72, c1, pltpu.roll(c3, 72, 1))


def rest(c3, k):
    return pltpu.roll(c3, (72 + 16 * k) % LANES, 1)


def part(joined, rem, k):
    at = lane(joined.shape[0])
    c1 = jnp.where(at < 72, joined, 0.0)
    tail = jnp.where(at < 72, pltpu.roll(rem, (56 - 16 * k) % LANES, 1), 0.0)
    return c1, jnp.where(at < 56, pltpu.roll(joined, 56, 1), tail)


def four(ref, base, n):
    return [ref[pl.ds(base + c, n, stride=CHUNKS), :] for c in range(CHUNKS)]


def pack16(src, src_base, dst, dst_base):
    rem = None
    for k in range(2):
        c0, c1, c2, c3 = four(src, src_base + 32 * k, 8)
        dst[pl.ds(dst_base + 8 * k, 8), :] = c0
        dst[pl.ds(dst_base + 16 + 8 * k, 8), :] = c2
        dst[pl.ds(dst_base + 32 + 8 * k, 8), :] = join(c1, c3)
        rem = rest(c3, 0) if k == 0 else jnp.where(lane(8) < 16, rem, rest(c3, 1))
    dst[pl.ds(dst_base + 48, 8), :] = rem


def unpack16(src, src_base, dst, dst_base):
    rem = src[pl.ds(src_base + 48, 8), :]
    for k in range(2):
        c1, c3 = part(src[pl.ds(src_base + 32 + 8 * k, 8), :], rem, k)
        c0 = src[pl.ds(src_base + 8 * k, 8), :]
        c2 = src[pl.ds(src_base + 16 + 8 * k, 8), :]
        for c, piece in enumerate((c0, c1, c2, c3)):
            dst[pl.ds(dst_base + 32 * k + c, 8, stride=CHUNKS), :] = piece


def blocks_loop(n, unroll, body):
    def step(s, carry):
        for u in range(unroll):
            body(s * unroll + u)
        return carry

    lax.fori_loop(0, n // unroll, step, 0)


def pack_slots(src, src_base, dst):
    blocks_loop(N_DEV, 4, lambda d: pack16(src, src_base + d * CAP * CHUNKS, dst, d * PACK16))


def unpack_slots(src, dst, dst_base):
    blocks_loop(N_DEV, 4, lambda d: unpack16(src, d * PACK16, dst, dst_base + d * CAP * CHUNKS))


def pack66(src, src_base, dst, dst_base):
    rows = REL_DEV + NEG_DEV
    rem = None
    for k in range(9):
        n = 8 if k < 8 else 2
        c0, c1, c2, c3 = four(src, src_base + 32 * k, n)
        dst[pl.ds(dst_base + 8 * k, n), :] = c0
        dst[pl.ds(dst_base + rows + 8 * k, n), :] = c2
        dst[pl.ds(dst_base + 2 * rows + 8 * k, n), :] = join(c1, c3)
        if k == 8:
            dst[pl.ds(dst_base + 3 * rows + 8, 2), :] = rest(c3, 0)
        else:
            rem = rest(c3, k) if k == 0 else jnp.where(lane(8) < 16 * k, rem, rest(c3, k))
    dst[pl.ds(dst_base + 3 * rows, 8), :] = rem


def unpack66(src, src_base, dst, dst_base):
    rows = REL_DEV + NEG_DEV
    for k in range(9):
        n = 8 if k < 8 else 2
        rem = src[pl.ds(src_base + 3 * rows + (0 if k < 8 else 8), n), :]
        c1, c3 = part(src[pl.ds(src_base + 2 * rows + 8 * k, n), :], rem, k % 8)
        c0 = src[pl.ds(src_base + 8 * k, n), :]
        c2 = src[pl.ds(src_base + rows + 8 * k, n), :]
        for c, piece in enumerate((c0, c1, c2, c3)):
            dst[pl.ds(dst_base + 32 * k + c, n, stride=CHUNKS), :] = piece


def to_chunks(src, dst, n):
    for c, (start, size) in enumerate(SPANS):
        piece = src[start : start + size, :]
        if size < LANES:
            piece = jnp.concatenate([piece, jnp.zeros((LANES - size, n), f32)], axis=0)
        dst[pl.ds(c, n, stride=CHUNKS), :] = piece.T


def turn_relations(rel, wide, rel_t):
    wide[...] = jnp.zeros_like(wide)
    wide[0:REL_DEV, 0:WIDTH] = rel[...]
    rel_t[...] = wide[...].T


def prep_kernel(negatives, table_t, rel, tab4, send, rel4, wide, rel_t):
    turn_relations(rel, wide, rel_t)
    to_chunks(table_t, tab4, ENT_DEV)
    to_chunks(rel_t, rel4, LANES)
    for i in range(NEG_DEV):
        rel4[REL4 + CHUNKS * i : REL4 + CHUNKS * (i + 1), :] = tab4[row(negatives[i]), :]
    pack66(rel4, 0, send, 0)


def prep(negatives, table_t, rel):
    return pl.pallas_call(
        prep_kernel,
        out_shape=(
            jax.ShapeDtypeStruct((ENT_DEV * CHUNKS, LANES), f32),
            jax.ShapeDtypeStruct((PACK66, LANES), f32),
        ),
        in_specs=[SMEM, VMEM, VMEM],
        out_specs=(VMEM, VMEM),
        scratch_shapes=[
            pltpu.VMEM((LANES * CHUNKS, LANES), f32),
            pltpu.VMEM((LANES, CHUNKS * LANES), f32),
            pltpu.VMEM((CHUNKS * LANES, LANES), f32),
        ],
        compiler_params=params(58),
        cost_estimate=cost(0, 8 << 20),
        name="prep",
    )(negatives, table_t, rel)


def pull_kernel(asked, tab4, out, picked, packed, sem):
    def body(i):
        picked[row(i), :] = tab4[row(asked[i]), :]

    rows_loop(SLOTS, body)
    pack_slots(picked, 0, packed)
    store = pltpu.make_async_copy(packed, out, sem)
    store.start()
    store.wait()


def pull_rows(asked, tab4):
    return pl.pallas_call(
        pull_kernel,
        out_shape=jax.ShapeDtypeStruct((N_DEV * PACK16, LANES), f32),
        in_specs=[SMEM, VMEM],
        out_specs=HBM,
        scratch_shapes=[
            pltpu.VMEM((SLOTS * CHUNKS, LANES), f32),
            pltpu.VMEM((N_DEV * PACK16, LANES), f32),
            pltpu.SemaphoreType.DMA,
        ],
        compiler_params=params(58),
        cost_estimate=cost(0, 8 << 20),
        name="pull_rows",
    )(asked, tab4)


def query_kernel(
    heads, rel_at, tab4, shared,
    q_out, h_out, r_out, back_out, neg_acc,
    tab, rel, packed, n_hi, n_lo, t_hi, t_lo, hb, rb, sems,
):
    step = pl.program_id(0)

    @pl.when(step == 0)
    def _():
        size = N_DEV * PACK66 // PIECES
        loads = [
            pltpu.make_async_copy(shared.at[pl.ds(i * size, size)], packed.at[pl.ds(i * size, size)], sems.at[i])
            for i in range(PIECES)
        ]
        loads.append(pltpu.make_async_copy(tab4, tab, sems.at[PIECES]))
        for load in loads:
            load.start()
        neg_acc[...] = jnp.zeros_like(neg_acc)
        each = N_DEV // PIECES
        for i in range(PIECES):
            loads[i].wait()
            blocks_loop(each, 2, lambda d, i=i: unpack66(packed, (i * each + d) * PACK66, rel, (i * each + d) * PER))
        loads[PIECES].wait()

        for c in range(CHUNKS):
            lanes = slice(c * LANES, (c + 1) * LANES)

            def place(d, carry, c=c):
                rows = pl.ds(pl.multiple_of(d * NEG_DEV, NEG_DEV), NEG_DEV)
                hb[rows, :] = rel[pl.ds(d * PER + REL4 + c, NEG_DEV, stride=CHUNKS), :]
                return carry

            lax.fori_loop(0, N_DEV, place, 0)
            piece = hb[...]
            n_hi[:, lanes], n_lo[:, lanes] = split(piece)
            t_hi[lanes, :], t_lo[lanes, :] = split(piece.T)

    base = step * TILE

    def gather(i):
        hb[row(i), :] = tab[row(heads[base + i]), :]
        rb[row(i), :] = rel[row(rel_at[base + i]), :]

    rows_loop(TILE, gather)
    h = [chunk_of(hb, c, TILE) for c in range(CHUNKS)]
    r = [chunk_of(rb, c, TILE) for c in range(CHUNKS)]
    q = [h[0] * r[0] - h[2] * r[2], h[1] * r[1] - h[3] * r[3], h[0] * r[2] + h[2] * r[0], h[1] * r[3] + h[3] * r[1]]
    for c in range(CHUNKS):
        q_out[c] = q[c]
        h_out[c] = h[c]
        r_out[c] = r[c]
    q = split(jnp.concatenate(q, axis=1))
    negative = dot3(q, (t_hi[...], t_lo[...]), ((1,), (0,)))
    neg_grad = split(jax.nn.sigmoid(negative) * (1.0 / NEG))
    neg_acc[...] += dot3(neg_grad, q, ((0,), (0,)))
    back = dot3(neg_grad, (n_hi[...], n_lo[...]), ((1,), (0,)))
    for c in range(CHUNKS):
        back_out[c] = back[:, c * LANES : (c + 1) * LANES]


PLANE = jax.ShapeDtypeStruct((CHUNKS, E_DEV, LANES), f32)
BLOCK = pl.BlockSpec((CHUNKS, TILE, LANES), lambda i: (0, i, 0))


def queries(heads, rel_at, tab4, shared):
    rows = pltpu.VMEM((TILE * CHUNKS, LANES), f32)
    wide = pltpu.VMEM((NEG, CHUNKS * LANES), bf16)
    tall = pltpu.VMEM((CHUNKS * LANES, NEG), bf16)
    return pl.pallas_call(
        query_kernel,
        grid=(E_DEV // TILE,),
        out_shape=(PLANE, PLANE, PLANE, PLANE, jax.ShapeDtypeStruct((NEG, CHUNKS * LANES), f32)),
        in_specs=[SMEM, SMEM, ANY, ANY],
        out_specs=(BLOCK, BLOCK, BLOCK, BLOCK, pl.BlockSpec((NEG, CHUNKS * LANES), lambda i: (0, 0))),
        scratch_shapes=[
            pltpu.VMEM((ENT_DEV * CHUNKS, LANES), f32),
            pltpu.VMEM((N_DEV * PER, LANES), f32),
            pltpu.VMEM((N_DEV * PACK66, LANES), f32),
            wide,
            wide,
            tall,
            tall,
            rows,
            rows,
            pltpu.SemaphoreType.DMA((PIECES + 1,)),
        ],
        compiler_params=params(58),
        cost_estimate=cost(36_000_000_000, 60 << 20),
        name="queries",
    )(heads, rel_at, tab4, shared)


def tail_kernel(
    tails, tab4, fetched, q_in,
    p_out, tail_local, outgoing,
    ext, ext_grad, packed, tb, sems,
):
    step = pl.program_id(0)
    local = ENT_DEV * CHUNKS
    size = N_DEV * PACK16 // PIECES
    each = N_DEV // PIECES

    @pl.when(step == 0)
    def _():
        loads = []
        for i in range(PIECES):
            here = pl.ds(i * size, size)
            loads.append(pltpu.make_async_copy(fetched.at[here], packed.at[here], sems.at[i]))
        loads.append(pltpu.make_async_copy(tab4, ext.at[pl.ds(0, local)], sems.at[PIECES]))
        for load in loads:
            load.start()
        ext_grad[...] = jnp.zeros_like(ext_grad)
        for i in range(PIECES):
            loads[i].wait()

            def unpack(d, i=i):
                unpack16(packed, (i * each + d) * PACK16, ext, local + (i * each + d) * CAP * CHUNKS)

            blocks_loop(each, 4, unpack)
        loads[PIECES].wait()

    base = step * TAIL_TILE

    def gather(i):
        tb[row(i), :] = ext[row(tails[base + i]), :]

    rows_loop(TAIL_TILE, gather)
    t = [chunk_of(tb, c, TAIL_TILE) for c in range(CHUNKS)]
    q = [q_in[c] for c in range(CHUNKS)]
    score = (q[0] * t[0] + q[1] * t[1]) + (q[2] * t[2] + q[3] * t[3])
    pos_grad = jax.nn.sigmoid(jnp.sum(score, axis=1, keepdims=True)) - 1.0
    for c in range(CHUNKS):
        p_out[c] = pos_grad * t[c]
        tb[pl.ds(c, TAIL_TILE, stride=CHUNKS), :] = pos_grad * q[c]

    def scatter(i):
        at = row(tails[base + i])
        ext_grad[at, :] = ext_grad[at, :] + tb[row(i), :]

    rows_loop(TAIL_TILE, scatter)

    @pl.when(step == E_DEV // TAIL_TILE - 1)
    def _():
        stores = []
        for i in range(PIECES):
            here = pl.ds(i * size, size)
            stores.append(pltpu.make_async_copy(packed.at[here], outgoing.at[here], sems.at[i]))
        stores.append(pltpu.make_async_copy(ext_grad.at[pl.ds(0, local)], tail_local, sems.at[PIECES]))
        stores[PIECES].start()
        for i in range(PIECES):

            def pack(d, i=i):
                pack16(ext_grad, local + (i * each + d) * CAP * CHUNKS, packed, (i * each + d) * PACK16)

            blocks_loop(each, 4, pack)
            stores[i].start()
        for store in stores:
            store.wait()


TAIL_TILE = 512


def tail_terms(tails, tab4, fetched, q):
    block = pl.BlockSpec((CHUNKS, TAIL_TILE, LANES), lambda i: (0, i, 0))
    return pl.pallas_call(
        tail_kernel,
        grid=(E_DEV // TAIL_TILE,),
        out_shape=(
            PLANE,
            jax.ShapeDtypeStruct((ENT_DEV * CHUNKS, LANES), f32),
            jax.ShapeDtypeStruct((N_DEV * PACK16, LANES), f32),
        ),
        in_specs=[SMEM, ANY, ANY, block],
        out_specs=(block, HBM, HBM),
        scratch_shapes=[
            pltpu.VMEM(((ENT_DEV + SLOTS) * CHUNKS, LANES), f32),
            pltpu.VMEM(((ENT_DEV + SLOTS) * CHUNKS, LANES), f32),
            pltpu.VMEM((N_DEV * PACK16, LANES), f32),
            pltpu.VMEM((TAIL_TILE * CHUNKS, LANES), f32),
            pltpu.SemaphoreType.DMA((PIECES + 1,)),
        ],
        compiler_params=params(58),
        cost_estimate=cost(0, 30 << 20),
        name="tail_terms",
    )(tails, tab4, fetched, q)


def edge_kernel(
    heads, grad_at, core, tail_local, neg_acc, h_in, r_in, p_in, back_in,
    mine, other0, other1, other2, other3, head_grad,
    rel_grad, packed, hb, rb, sems,
):
    step = pl.program_id(0)

    @pl.when(step == 0)
    def _():
        start = pltpu.make_async_copy(tail_local, head_grad, sems.at[0])
        start.start()
        rel_grad[...] = jnp.zeros_like(rel_grad)
        start.wait()

    base = step * EDGE_TILE
    g = [p_in[c] + back_in[c] for c in range(CHUNKS)]
    for k in range(2):
        for buf, src in ((hb, r_in), (rb, h_in)):
            buf[pl.ds(k, EDGE_TILE, stride=CHUNKS), :] = g[k] * src[k] + g[k + 2] * src[k + 2]
            buf[pl.ds(k + 2, EDGE_TILE, stride=CHUNKS), :] = g[k + 2] * src[k] - g[k] * src[k + 2]

    def scatter(i):
        at = row(heads[base + i])
        rel = row(grad_at[base + i])
        head_grad[at, :] = head_grad[at, :] + hb[row(i), :]
        rel_grad[rel, :] = rel_grad[rel, :] + rb[row(i), :]

    rows_loop(EDGE_TILE, scatter)

    @pl.when(step == E_DEV // EDGE_TILE - 1)
    def _():
        def place(d, carry):
            spot = ((d % 2) * CHIPS + d // 2) * PER + REL4
            rows = pl.ds(pl.multiple_of(d * NEG_DEV, NEG_DEV), NEG_DEV)
            for c in range(CHUNKS):
                rel_grad[pl.ds(spot + c, NEG_DEV, stride=CHUNKS), :] = neg_acc[rows, c * LANES : (c + 1) * LANES]
            return carry

        lax.fori_loop(0, N_DEV, place, 0)
        side = core[0]
        size = CHIPS * PACK66 // PIECES
        stores = [
            pltpu.make_async_copy(packed.at[pl.ds(i * size, size)], other, sems.at[i])
            for i, other in enumerate((other0, other1, other2, other3))
        ]
        stores.append(pltpu.make_async_copy(packed.at[pl.ds(PIECES * size, PIECES * size)], mine, sems.at[PIECES]))

        def pack(d, owner, first):
            pack66(rel_grad, (owner * CHIPS + d) * PER, packed, (first + d) * PACK66)

        chips = CHIPS // PIECES
        for i in range(PIECES):
            blocks_loop(chips, 2, lambda d, i=i: pack(i * chips + d, 1 - side, 0))
            stores[i].start()
        blocks_loop(CHIPS, 2, lambda d: pack(d, side, CHIPS))
        stores[PIECES].start()
        for store in stores:
            store.wait()


EDGE_TILE = 512


def gradients(heads, grad_at, core, tail_local, neg_acc, h, r, p, back):
    half = jax.ShapeDtypeStruct((CHIPS * PACK66, LANES), f32)
    piece = jax.ShapeDtypeStruct((CHIPS * PACK66 // PIECES, LANES), f32)
    block = pl.BlockSpec((CHUNKS, EDGE_TILE, LANES), lambda i: (0, i, 0))
    whole = pl.BlockSpec((ENT_DEV * CHUNKS, LANES), lambda i: (0, 0))
    return pl.pallas_call(
        edge_kernel,
        grid=(E_DEV // EDGE_TILE,),
        out_shape=(half, piece, piece, piece, piece, jax.ShapeDtypeStruct((ENT_DEV * CHUNKS, LANES), f32)),
        in_specs=[SMEM, SMEM, SMEM, ANY, pl.BlockSpec((NEG, CHUNKS * LANES), lambda i: (0, 0)), block, block, block, block],
        out_specs=(HBM,) * 5 + (whole,),
        scratch_shapes=[
            pltpu.VMEM((N_DEV * PER, LANES), f32),
            pltpu.VMEM((N_DEV * PACK66, LANES), f32),
            pltpu.VMEM((EDGE_TILE * CHUNKS, LANES), f32),
            pltpu.VMEM((EDGE_TILE * CHUNKS, LANES), f32),
            pltpu.SemaphoreType.DMA((PIECES + 1,)),
        ],
        compiler_params=params(58),
        cost_estimate=cost(0, 1 << 20),
        name="gradients",
    )(heads, grad_at, core, tail_local, neg_acc, h, r, p, back)


def merge_kernel(
    color, mine, got0, got1, got2, got3,
    keep, send0, send1, send2, send3, send4,
    total, came, sems, came_sems,
):
    each = CHIPS // PIECES
    loads, arrivals = [], []
    for i, got in enumerate((got0, got1, got2, got3)):
        here = pl.ds(i * each, each)
        loads.append(pltpu.make_async_copy(mine.at[here], total.at[here], sems.at[i]))
        arrivals.append(pltpu.make_async_copy(got, came.at[here], came_sems.at[i]))
        loads[i].start()
        arrivals[i].start()
    own = pl.ds(pl.multiple_of(color[0] * KEPT, 8), KEPT)
    theirs = pl.ds(pl.multiple_of((1 - color[0]) * KEPT, 8), KEPT)
    stores = [
        pltpu.make_async_copy(total.at[pl.ds(first, last - first), theirs], send, sems.at[PIECES + i])
        for i, (first, last, send) in enumerate(
            zip(GROUPS[:-1], GROUPS[1:], (send0, send1, send2, send3, send4), strict=True)
        )
    ]
    stores.append(pltpu.make_async_copy(total.at[:, own], keep, sems.at[PIECES + WAYS]))
    started = 0
    for i in range(PIECES):
        loads[i].wait()
        arrivals[i].wait()

        def add(d, carry, i=i):
            total[i * each + d] = total[i * each + d] + came[i * each + d]
            return carry

        lax.fori_loop(0, each, add, 0)
        while started < WAYS and GROUPS[started + 1] <= (i + 1) * each:
            stores[started].start()
            started += 1
    stores[WAYS].start()
    for store in stores:
        store.wait()


def merge(color, mine, got):
    def blocks(n, rows):
        return jax.ShapeDtypeStruct((n, rows, LANES), f32)

    return pl.pallas_call(
        merge_kernel,
        out_shape=(blocks(CHIPS, KEPT),) + tuple(blocks(b - a, KEPT) for a, b in zip(GROUPS[:-1], GROUPS[1:], strict=True)),
        in_specs=[SMEM, ANY] + [ANY] * PIECES,
        out_specs=(HBM,) * (WAYS + 1),
        scratch_shapes=[
            pltpu.VMEM((CHIPS, PACK66, LANES), f32),
            pltpu.VMEM((CHIPS, PACK66, LANES), f32),
            pltpu.SemaphoreType.DMA((PIECES + WAYS + 1,)),
            pltpu.SemaphoreType.DMA((PIECES,)),
        ],
        compiler_params=params(58),
        cost_estimate=cost(0, 1 << 16),
        name="merge",
    )(color, mine.reshape(CHIPS, PACK66, LANES), *[x.reshape(CHIPS // PIECES, PACK66, LANES) for x in got])


def meet_kernel(keep, got0, got1, got2, got3, got4, out, total, sems):
    spans = list(zip(GROUPS[:-1], GROUPS[1:], (got0, got1, got2, got3, got4), strict=True))
    loads, stores = [], []
    for i, (first, last, _) in enumerate(spans):
        here = pl.ds(first, last - first)
        loads.append(pltpu.make_async_copy(keep.at[here], total.at[here], sems.at[i]))
        stores.append(pltpu.make_async_copy(total.at[here], out.at[here], sems.at[WAYS + i]))
        loads[i].start()
    for i, (first, last, got) in enumerate(spans):
        loads[i].wait()

        def add(d, carry, first=first, got=got):
            total[first + d] = total[first + d] + got[d]
            return carry

        lax.fori_loop(0, last - first, add, 0)
        stores[i].start()
    for store in stores:
        store.wait()


def meet(keep, got):
    return pl.pallas_call(
        meet_kernel,
        out_shape=jax.ShapeDtypeStruct((CHIPS, KEPT, LANES), f32),
        in_specs=[ANY] + [VMEM] * WAYS,
        out_specs=HBM,
        scratch_shapes=[pltpu.VMEM((CHIPS, KEPT, LANES), f32), pltpu.SemaphoreType.DMA((2 * WAYS,))],
        compiler_params=params(47),
        cost_estimate=cost(0, 1 << 16),
        name="meet",
    )(keep, *got)


def color_of(chip):
    return (chip // 16 + chip // 4 + chip) % 2


def matching(k):
    pairs = []
    for chip in range(CHIPS):
        if color_of(chip) == 0:
            at = [chip // 16, chip // 4 % 4, chip % 4]
            at[k // 2] = (at[k // 2] + (1 if k % 2 == 0 else 3)) % 4
            mate = (at[0] * 4 + at[1]) * 4 + at[2]
            pairs += [(chip, mate), (mate, chip)]
    return pairs


def returned_kernel(asked, packed, head_grad, out, returned):
    out[...] = head_grad[...]
    unpack_slots(packed, returned, 0)

    def body(i):
        at = row(asked[i])
        out[at, :] = out[at, :] + returned[row(i), :]

    rows_loop(SLOTS, body)


def add_returned(asked, returned, head_grad):
    return pl.pallas_call(
        returned_kernel,
        out_shape=jax.ShapeDtypeStruct((ENT_DEV * CHUNKS, LANES), f32),
        in_specs=[SMEM, VMEM, VMEM],
        out_specs=VMEM,
        scratch_shapes=[pltpu.VMEM((SLOTS * CHUNKS, LANES), f32)],
        compiler_params=params(24),
        cost_estimate=cost(0, 10 << 20),
        name="add_returned",
    )(asked, returned, head_grad)


def adagrad(grad, n, table_t, state, new_table_t, new_state):
    g = [chunk_of(grad, c, n).T for c in range(CHUNKS)]
    squares = (g[0] * g[0] + g[1] * g[1]) + (g[2] * g[2] + g[3] * g[3])
    state_now = state[...] + jnp.sum(squares, axis=0, keepdims=True) * (1.0 / WIDTH)
    new_state[...] = state_now
    below = jnp.sqrt(state_now) + 1e-10
    for c, (start, size) in enumerate(SPANS):
        spot = slice(start, start + size)
        new_table_t[spot, :] = table_t[spot, :] - rate * g[c][:size] / below


def step_kernel(
    negatives, local_grad, parts, table_now, state, rel, rel_state,
    new_table_t, new_state, new_rel, new_rel_state,
    grad, came, table_t, share, packed, wide, rel_t, new_rel_t, states, new_states, sems,
):
    each = CHIPS // PIECES
    loads = []
    for i in range(PIECES):
        here = pl.ds(i * each, each)
        loads.append(pltpu.make_async_copy(parts.at[here], came.at[here], sems.at[i]))
    loads.append(pltpu.make_async_copy(local_grad, grad, sems.at[PIECES]))
    loads.append(pltpu.make_async_copy(table_now, table_t, sems.at[PIECES + 1]))
    for load in loads:
        load.start()
    share[...] = jnp.zeros_like(share)
    turn_relations(rel, wide, rel_t)
    new_rel_t[...] = jnp.zeros_like(new_rel_t)
    states[...] = jnp.zeros_like(states)
    states[:, 0:REL_DEV] = rel_state[...]
    totals = [None, None]
    for i in range(PIECES):
        loads[i].wait()
        for chip in range(i * each, (i + 1) * each):
            half = color_of(chip)
            totals[half] = came[chip] if totals[half] is None else totals[half] + came[chip]
    packed[0:KEPT, :] = totals[0]
    packed[KEPT:PACK66, :] = totals[1]
    unpack66(packed, 0, share, 0)
    adagrad(share, LANES, rel_t, states, new_rel_t, new_states)
    new_rel[...] = new_rel_t[...].T[0:REL_DEV, 0:WIDTH]
    new_rel_state[...] = new_states[:, 0:REL_DEV]
    loads[PIECES].wait()
    for i in range(NEG_DEV):
        at = row(negatives[i])
        grad[at, :] = grad[at, :] + share[REL4 + CHUNKS * i : REL4 + CHUNKS * (i + 1), :]
    loads[PIECES + 1].wait()
    adagrad(grad, ENT_DEV, table_t, state, new_table_t, new_state)


def adagrad_step(negatives, local_grad, parts, table_t, state, rel, rel_state):
    def like(*shape):
        return jax.ShapeDtypeStruct(shape, f32)

    return pl.pallas_call(
        step_kernel,
        out_shape=(like(WIDTH, ENT_DEV), like(1, ENT_DEV), like(REL_DEV, WIDTH), like(1, REL_DEV)),
        in_specs=[SMEM, ANY, ANY, ANY] + [VMEM] * 3,
        out_specs=(VMEM,) * 4,
        scratch_shapes=[
            pltpu.VMEM((ENT_DEV * CHUNKS, LANES), f32),
            pltpu.VMEM((CHIPS, KEPT, LANES), f32),
            pltpu.VMEM((WIDTH, ENT_DEV), f32),
            pltpu.VMEM((CHUNKS * LANES, LANES), f32),
            pltpu.VMEM((PACK66, LANES), f32),
            pltpu.VMEM((LANES, CHUNKS * LANES), f32),
            pltpu.VMEM((CHUNKS * LANES, LANES), f32),
            pltpu.VMEM((CHUNKS * LANES, LANES), f32),
            pltpu.VMEM((1, LANES), f32),
            pltpu.VMEM((1, LANES), f32),
            pltpu.SemaphoreType.DMA((PIECES + 2,)),
        ],
        compiler_params=params(58),
        cost_estimate=cost(0, 16 << 20),
        name="adagrad_step",
    )(negatives, local_grad, parts, table_t, state, rel, rel_state)


def local(
    entity_table,
    entity_state,
    relation_table,
    relation_state,
    heads,
    relations,
    tails,
    pull_lists,
    negatives,
):
    table_t = entity_table.T
    owner, place = relations // REL_DEV, relations % REL_DEV
    rel_at = owner * (REL_DEV + NEG_DEV) + place
    grad_at = ((owner % 2) * CHIPS + owner // 2) * (REL_DEV + NEG_DEV) + place
    core = lax.axis_index("c")

    tab4, send = prep(negatives, table_t, relation_table)
    shared = lax.all_gather(send, AXES, axis=0, tiled=True)
    asked = lax.all_to_all(pull_lists, AXES, split_axis=0, concat_axis=0, tiled=True).reshape(SLOTS)
    rows_out, shared = lax.optimization_barrier((pull_rows(asked, tab4), shared))

    def exchange(rows):
        rows = rows.reshape(N_DEV, PACK16, LANES)
        return lax.all_to_all(rows, AXES, split_axis=0, concat_axis=0, tiled=True).reshape(N_DEV * PACK16, LANES)

    fetched = exchange(rows_out)
    q, h, r, back, neg_acc = queries(heads, rel_at, tab4, shared)
    p, tail_local, outgoing = tail_terms(tails, tab4, fetched, q)
    returned = exchange(outgoing)
    mine, *others, head_grad = gradients(
        heads, grad_at, core.reshape(1), tail_local, neg_acc, h, r, p, back
    )
    color = (lax.axis_index("x") + lax.axis_index("z") + lax.axis_index("y")) % 2
    got = [lax.ppermute(other, "c", [(0, 1), (1, 0)]) for other in others]
    merged = merge(color.reshape(1), mine, got)
    (keep, *sends), returned = lax.optimization_barrier((merged, returned))
    met = meet(keep, [lax.ppermute(send, AXES[:3], matching(k)) for k, send in enumerate(sends)])
    parts = lax.all_to_all(met, AXES[:3], split_axis=0, concat_axis=0, tiled=True)
    local_grad = add_returned(asked, returned, head_grad)
    new_table_t, new_state, new_rel, new_rel_state = adagrad_step(
        negatives,
        local_grad,
        parts,
        table_t,
        entity_state.reshape(1, ENT_DEV),
        relation_table,
        relation_state.reshape(1, REL_DEV),
    )
    return (
        new_table_t.T,
        new_state.reshape(ENT_DEV),
        new_rel,
        new_rel_state.reshape(REL_DEV),
    )


def solution(mesh):
    grid = Mesh(mesh.devices.reshape(4, 4, 4, 2), AXES)
    rows, flat = P(AXES, None), P(AXES)
    in_specs = (rows, flat, rows, flat, flat, flat, flat, rows, flat)
    out_specs = (rows, flat, rows, flat)
    return jax.shard_map(local, mesh=grid, in_specs=in_specs, out_specs=out_specs, check_vma=False)
```

```python
import jax
import jax.numpy as jnp
from jax import lax
from jax.experimental import pallas as pl
from jax.experimental.pallas import tpu as pltpu
from jax.sharding import Mesh, PartitionSpec as P

rate = 0.1
AXES = ("x", "z", "y", "c")
WIDTH = 400
HALF = 200
LANES = 128
CHUNKS = 4
SPANS = ((0, 128), (128, 72), (200, 128), (328, 72))
ENT_DEV = 1024
REL_DEV = 58
NEG_DEV = 8
E_DEV = 2048
N_DEV = 128
CAP = 16
NEG = N_DEV * NEG_DEV
SLOTS = N_DEV * CAP
CHIPS = N_DEV // 2
PER = CHUNKS * (REL_DEV + NEG_DEV)
REL4 = CHUNKS * REL_DEV
TILE = 256
PACK16 = 56
PACK66 = 208
PIECES = 4
KEPT = PACK66 // 2
GROUPS = (0, 13, 26, 39, 52, 64)
WAYS = len(GROUPS) - 1
UNROLL = 8

f32 = jnp.float32
bf16 = jnp.bfloat16
VMEM = pl.BlockSpec(memory_space=pltpu.VMEM)
SMEM = pl.BlockSpec(memory_space=pltpu.SMEM)
ANY = pl.BlockSpec(memory_space=pl.ANY)
HBM = pl.BlockSpec(memory_space=pltpu.HBM)


def params(mib):
    return pltpu.CompilerParams(vmem_limit_bytes=mib * 1024 * 1024)


def cost(flops, moved):
    return pl.CostEstimate(flops=flops, bytes_accessed=moved, transcendentals=0)


def chunk_of(ref, c, n):
    return ref[pl.ds(c, n, stride=CHUNKS), :]


def row(i):
    return pl.ds(pl.multiple_of(i * CHUNKS, CHUNKS), CHUNKS)


def split(x):
    hi = x.astype(bf16)
    return hi, (x - hi.astype(f32)).astype(bf16)


def dot3(a, b, dims):
    (ah, al), (bh, bl) = a, b

    def one(p, q):
        return lax.dot_general(p, q, (dims, ((), ())), preferred_element_type=f32)

    return one(ah, bh) + (one(ah, bl) + one(al, bh))


def rows_loop(n, body):
    def step(s, carry):
        for u in range(UNROLL):
            body(s * UNROLL + u)
        return carry

    lax.fori_loop(0, n // UNROLL, step, 0)


def add_two(acc, a, b, first, second):
    old_a, old_b = acc[row(a), :], acc[row(b), :]
    acc[row(a), :] = old_a + first
    acc[row(b), :] = (old_b + second) + jnp.where(a == b, first, jnp.zeros_like(first))


def lane(n):
    return lax.broadcasted_iota(jnp.int32, (n, LANES), 1)


def join(c1, c3):
    return jnp.where(lane(c1.shape[0]) < 72, c1, pltpu.roll(c3, 72, 1))


def rest(c3, k):
    return pltpu.roll(c3, (72 + 16 * k) % LANES, 1)


def part(joined, rem, k):
    at = lane(joined.shape[0])
    c1 = jnp.where(at < 72, joined, 0.0)
    tail = jnp.where(at < 72, pltpu.roll(rem, (56 - 16 * k) % LANES, 1), 0.0)
    return c1, jnp.where(at < 56, pltpu.roll(joined, 56, 1), tail)


def four(ref, base, n):
    return [ref[pl.ds(base + c, n, stride=CHUNKS), :] for c in range(CHUNKS)]


def pack16(src, src_base, dst, dst_base):
    rem = None
    for k in range(2):
        c0, c1, c2, c3 = four(src, src_base + 32 * k, 8)
        dst[pl.ds(dst_base + 8 * k, 8), :] = c0
        dst[pl.ds(dst_base + 16 + 8 * k, 8), :] = c2
        dst[pl.ds(dst_base + 32 + 8 * k, 8), :] = join(c1, c3)
        rem = rest(c3, 0) if k == 0 else jnp.where(lane(8) < 16, rem, rest(c3, 1))
    dst[pl.ds(dst_base + 48, 8), :] = rem


def unpack16(src, src_base, dst, dst_base):
    rem = src[pl.ds(src_base + 48, 8), :]
    for k in range(2):
        c1, c3 = part(src[pl.ds(src_base + 32 + 8 * k, 8), :], rem, k)
        c0 = src[pl.ds(src_base + 8 * k, 8), :]
        c2 = src[pl.ds(src_base + 16 + 8 * k, 8), :]
        for c, piece in enumerate((c0, c1, c2, c3)):
            dst[pl.ds(dst_base + 32 * k + c, 8, stride=CHUNKS), :] = piece


def blocks_loop(n, unroll, body):
    def step(s, carry):
        for u in range(unroll):
            body(s * unroll + u)
        return carry

    lax.fori_loop(0, n // unroll, step, 0)


def pack_slots(src, src_base, dst):
    blocks_loop(N_DEV, 4, lambda d: pack16(src, src_base + d * CAP * CHUNKS, dst, d * PACK16))


def unpack_slots(src, dst, dst_base):
    blocks_loop(N_DEV, 4, lambda d: unpack16(src, d * PACK16, dst, dst_base + d * CAP * CHUNKS))


def pack66(src, src_base, dst, dst_base):
    rows = REL_DEV + NEG_DEV
    rem = None
    for k in range(9):
        n = 8 if k < 8 else 2
        c0, c1, c2, c3 = four(src, src_base + 32 * k, n)
        dst[pl.ds(dst_base + 8 * k, n), :] = c0
        dst[pl.ds(dst_base + rows + 8 * k, n), :] = c2
        dst[pl.ds(dst_base + 2 * rows + 8 * k, n), :] = join(c1, c3)
        if k == 8:
            dst[pl.ds(dst_base + 3 * rows + 8, 2), :] = rest(c3, 0)
        else:
            rem = rest(c3, k) if k == 0 else jnp.where(lane(8) < 16 * k, rem, rest(c3, k))
    dst[pl.ds(dst_base + 3 * rows, 8), :] = rem


def unpack66(src, src_base, dst, dst_base):
    rows = REL_DEV + NEG_DEV
    for k in range(9):
        n = 8 if k < 8 else 2
        rem = src[pl.ds(src_base + 3 * rows + (0 if k < 8 else 8), n), :]
        c1, c3 = part(src[pl.ds(src_base + 2 * rows + 8 * k, n), :], rem, k % 8)
        c0 = src[pl.ds(src_base + 8 * k, n), :]
        c2 = src[pl.ds(src_base + rows + 8 * k, n), :]
        for c, piece in enumerate((c0, c1, c2, c3)):
            dst[pl.ds(dst_base + 32 * k + c, n, stride=CHUNKS), :] = piece


def to_chunks(src, dst, n):
    for c, (start, size) in enumerate(SPANS):
        piece = src[start : start + size, :]
        if size < LANES:
            piece = jnp.concatenate([piece, jnp.zeros((LANES - size, n), f32)], axis=0)
        dst[pl.ds(c, n, stride=CHUNKS), :] = piece.T


def turn_relations(rel, wide, rel_t):
    wide[...] = jnp.zeros_like(wide)
    wide[0:REL_DEV, 0:WIDTH] = rel[...]
    rel_t[...] = wide[...].T


def prep_kernel(negatives, table_t, rel, tab4, send, rel4, wide, rel_t):
    turn_relations(rel, wide, rel_t)
    to_chunks(table_t, tab4, ENT_DEV)
    to_chunks(rel_t, rel4, LANES)
    for i in range(NEG_DEV):
        rel4[REL4 + CHUNKS * i : REL4 + CHUNKS * (i + 1), :] = tab4[row(negatives[i]), :]
    pack66(rel4, 0, send, 0)


def prep(negatives, table_t, rel):
    return pl.pallas_call(
        prep_kernel,
        out_shape=(
            jax.ShapeDtypeStruct((ENT_DEV * CHUNKS, LANES), f32),
            jax.ShapeDtypeStruct((PACK66, LANES), f32),
        ),
        in_specs=[SMEM, VMEM, VMEM],
        out_specs=(VMEM, VMEM),
        scratch_shapes=[
            pltpu.VMEM((LANES * CHUNKS, LANES), f32),
            pltpu.VMEM((LANES, CHUNKS * LANES), f32),
            pltpu.VMEM((CHUNKS * LANES, LANES), f32),
        ],
        compiler_params=params(58),
        cost_estimate=cost(0, 8 << 20),
        name="prep",
    )(negatives, table_t, rel)


def pull_kernel(asked, tab4, out, picked, packed, sem):
    def body(i):
        picked[row(i), :] = tab4[row(asked[i]), :]

    rows_loop(SLOTS, body)
    pack_slots(picked, 0, packed)
    store = pltpu.make_async_copy(packed, out, sem)
    store.start()
    store.wait()


def pull_rows(asked, tab4):
    return pl.pallas_call(
        pull_kernel,
        out_shape=jax.ShapeDtypeStruct((N_DEV * PACK16, LANES), f32),
        in_specs=[SMEM, VMEM],
        out_specs=HBM,
        scratch_shapes=[
            pltpu.VMEM((SLOTS * CHUNKS, LANES), f32),
            pltpu.VMEM((N_DEV * PACK16, LANES), f32),
            pltpu.SemaphoreType.DMA,
        ],
        compiler_params=params(58),
        cost_estimate=cost(0, 8 << 20),
        name="pull_rows",
    )(asked, tab4)


def query_kernel(
    heads, rel_at, tab4, shared,
    q_out, h_out, r_out, back_out, neg_acc,
    tab, rel, packed, n_hi, n_lo, t_hi, t_lo, hb, rb, sems,
):
    step = pl.program_id(0)

    @pl.when(step == 0)
    def _():
        size = N_DEV * PACK66 // PIECES
        loads = [
            pltpu.make_async_copy(shared.at[pl.ds(i * size, size)], packed.at[pl.ds(i * size, size)], sems.at[i])
            for i in range(PIECES)
        ]
        loads.append(pltpu.make_async_copy(tab4, tab, sems.at[PIECES]))
        for load in loads:
            load.start()
        neg_acc[...] = jnp.zeros_like(neg_acc)
        each = N_DEV // PIECES
        for i in range(PIECES):
            loads[i].wait()
            blocks_loop(each, 2, lambda d, i=i: unpack66(packed, (i * each + d) * PACK66, rel, (i * each + d) * PER))
        loads[PIECES].wait()

        for c in range(CHUNKS):
            lanes = slice(c * LANES, (c + 1) * LANES)

            def place(d, carry, c=c):
                rows = pl.ds(pl.multiple_of(d * NEG_DEV, NEG_DEV), NEG_DEV)
                hb[rows, :] = rel[pl.ds(d * PER + REL4 + c, NEG_DEV, stride=CHUNKS), :]
                return carry

            lax.fori_loop(0, N_DEV, place, 0)
            piece = hb[...]
            n_hi[:, lanes], n_lo[:, lanes] = split(piece)
            t_hi[lanes, :], t_lo[lanes, :] = split(piece.T)

    base = step * TILE

    def gather(i):
        hb[row(i), :] = tab[row(heads[base + i]), :]
        rb[row(i), :] = rel[row(rel_at[base + i]), :]

    rows_loop(TILE, gather)
    h = [chunk_of(hb, c, TILE) for c in range(CHUNKS)]
    r = [chunk_of(rb, c, TILE) for c in range(CHUNKS)]
    q = [h[0] * r[0] - h[2] * r[2], h[1] * r[1] - h[3] * r[3], h[0] * r[2] + h[2] * r[0], h[1] * r[3] + h[3] * r[1]]
    for c in range(CHUNKS):
        q_out[c] = q[c]
        h_out[c] = h[c]
        r_out[c] = r[c]
    q = split(jnp.concatenate(q, axis=1))
    negative = dot3(q, (t_hi[...], t_lo[...]), ((1,), (0,)))
    neg_grad = split(jax.nn.sigmoid(negative) * (1.0 / NEG))
    neg_acc[...] += dot3(neg_grad, q, ((0,), (0,)))
    back = dot3(neg_grad, (n_hi[...], n_lo[...]), ((1,), (0,)))
    for c in range(CHUNKS):
        back_out[c] = back[:, c * LANES : (c + 1) * LANES]


PLANE = jax.ShapeDtypeStruct((CHUNKS, E_DEV, LANES), f32)
BLOCK = pl.BlockSpec((CHUNKS, TILE, LANES), lambda i: (0, i, 0))


def queries(heads, rel_at, tab4, shared):
    rows = pltpu.VMEM((TILE * CHUNKS, LANES), f32)
    wide = pltpu.VMEM((NEG, CHUNKS * LANES), bf16)
    tall = pltpu.VMEM((CHUNKS * LANES, NEG), bf16)
    return pl.pallas_call(
        query_kernel,
        grid=(E_DEV // TILE,),
        out_shape=(PLANE, PLANE, PLANE, PLANE, jax.ShapeDtypeStruct((NEG, CHUNKS * LANES), f32)),
        in_specs=[SMEM, SMEM, ANY, ANY],
        out_specs=(BLOCK, BLOCK, BLOCK, BLOCK, pl.BlockSpec((NEG, CHUNKS * LANES), lambda i: (0, 0))),
        scratch_shapes=[
            pltpu.VMEM((ENT_DEV * CHUNKS, LANES), f32),
            pltpu.VMEM((N_DEV * PER, LANES), f32),
            pltpu.VMEM((N_DEV * PACK66, LANES), f32),
            wide,
            wide,
            tall,
            tall,
            rows,
            rows,
            pltpu.SemaphoreType.DMA((PIECES + 1,)),
        ],
        compiler_params=params(58),
        cost_estimate=cost(36_000_000_000, 60 << 20),
        name="queries",
    )(heads, rel_at, tab4, shared)


def tail_kernel(
    tails, tab4, fetched, q_in,
    p_out, tail_local, outgoing,
    ext, ext_grad, packed, tb, sems,
):
    step = pl.program_id(0)
    local = ENT_DEV * CHUNKS
    size = N_DEV * PACK16 // PIECES
    each = N_DEV // PIECES

    @pl.when(step == 0)
    def _():
        loads = []
        for i in range(PIECES):
            here = pl.ds(i * size, size)
            loads.append(pltpu.make_async_copy(fetched.at[here], packed.at[here], sems.at[i]))
        loads.append(pltpu.make_async_copy(tab4, ext.at[pl.ds(0, local)], sems.at[PIECES]))
        for load in loads:
            load.start()
        ext_grad[...] = jnp.zeros_like(ext_grad)
        for i in range(PIECES):
            loads[i].wait()

            def unpack(d, i=i):
                unpack16(packed, (i * each + d) * PACK16, ext, local + (i * each + d) * CAP * CHUNKS)

            blocks_loop(each, 4, unpack)
        loads[PIECES].wait()

    base = step * TAIL_TILE

    def gather(i):
        tb[row(i), :] = ext[row(tails[base + i]), :]

    rows_loop(TAIL_TILE, gather)
    t = [chunk_of(tb, c, TAIL_TILE) for c in range(CHUNKS)]
    q = [q_in[c] for c in range(CHUNKS)]
    score = (q[0] * t[0] + q[1] * t[1]) + (q[2] * t[2] + q[3] * t[3])
    pos_grad = jax.nn.sigmoid(jnp.sum(score, axis=1, keepdims=True)) - 1.0
    for c in range(CHUNKS):
        p_out[c] = pos_grad * t[c]
        tb[pl.ds(c, TAIL_TILE, stride=CHUNKS), :] = pos_grad * q[c]

    def scatter(pair):
        i = pair * 2
        add_two(ext_grad, tails[base + i], tails[base + i + 1], tb[row(i), :], tb[row(i + 1), :])

    rows_loop(TAIL_TILE // 2, scatter)

    @pl.when(step == E_DEV // TAIL_TILE - 1)
    def _():
        stores = []
        for i in range(PIECES):
            here = pl.ds(i * size, size)
            stores.append(pltpu.make_async_copy(packed.at[here], outgoing.at[here], sems.at[i]))
        stores.append(pltpu.make_async_copy(ext_grad.at[pl.ds(0, local)], tail_local, sems.at[PIECES]))
        stores[PIECES].start()
        for i in range(PIECES):

            def pack(d, i=i):
                pack16(ext_grad, local + (i * each + d) * CAP * CHUNKS, packed, (i * each + d) * PACK16)

            blocks_loop(each, 4, pack)
            stores[i].start()
        for store in stores:
            store.wait()


TAIL_TILE = 512


def tail_terms(tails, tab4, fetched, q):
    block = pl.BlockSpec((CHUNKS, TAIL_TILE, LANES), lambda i: (0, i, 0))
    return pl.pallas_call(
        tail_kernel,
        grid=(E_DEV // TAIL_TILE,),
        out_shape=(
            PLANE,
            jax.ShapeDtypeStruct((ENT_DEV * CHUNKS, LANES), f32),
            jax.ShapeDtypeStruct((N_DEV * PACK16, LANES), f32),
        ),
        in_specs=[SMEM, ANY, ANY, block],
        out_specs=(block, HBM, HBM),
        scratch_shapes=[
            pltpu.VMEM(((ENT_DEV + SLOTS) * CHUNKS, LANES), f32),
            pltpu.VMEM(((ENT_DEV + SLOTS) * CHUNKS, LANES), f32),
            pltpu.VMEM((N_DEV * PACK16, LANES), f32),
            pltpu.VMEM((TAIL_TILE * CHUNKS, LANES), f32),
            pltpu.SemaphoreType.DMA((PIECES + 1,)),
        ],
        compiler_params=params(58),
        cost_estimate=cost(0, 30 << 20),
        name="tail_terms",
    )(tails, tab4, fetched, q)


def edge_kernel(
    heads, grad_at, core, tail_local, neg_acc, h_in, r_in, p_in, back_in,
    mine, other0, other1, other2, other3, head_grad,
    rel_grad, packed, hb, rb, sems,
):
    step = pl.program_id(0)

    @pl.when(step == 0)
    def _():
        start = pltpu.make_async_copy(tail_local, head_grad, sems.at[0])
        start.start()
        rel_grad[...] = jnp.zeros_like(rel_grad)
        start.wait()

    base = step * EDGE_TILE
    g = [p_in[c] + back_in[c] for c in range(CHUNKS)]
    for k in range(2):
        for buf, src in ((hb, r_in), (rb, h_in)):
            buf[pl.ds(k, EDGE_TILE, stride=CHUNKS), :] = g[k] * src[k] + g[k + 2] * src[k + 2]
            buf[pl.ds(k + 2, EDGE_TILE, stride=CHUNKS), :] = g[k + 2] * src[k] - g[k] * src[k + 2]

    def scatter(pair):
        i = pair * 2
        add_two(head_grad, heads[base + i], heads[base + i + 1], hb[row(i), :], hb[row(i + 1), :])
        add_two(rel_grad, grad_at[base + i], grad_at[base + i + 1], rb[row(i), :], rb[row(i + 1), :])

    rows_loop(EDGE_TILE // 2, scatter)

    @pl.when(step == E_DEV // EDGE_TILE - 1)
    def _():
        def place(d, carry):
            spot = ((d % 2) * CHIPS + d // 2) * PER + REL4
            rows = pl.ds(pl.multiple_of(d * NEG_DEV, NEG_DEV), NEG_DEV)
            for c in range(CHUNKS):
                rel_grad[pl.ds(spot + c, NEG_DEV, stride=CHUNKS), :] = neg_acc[rows, c * LANES : (c + 1) * LANES]
            return carry

        lax.fori_loop(0, N_DEV, place, 0)
        side = core[0]
        size = CHIPS * PACK66 // PIECES
        stores = [
            pltpu.make_async_copy(packed.at[pl.ds(i * size, size)], other, sems.at[i])
            for i, other in enumerate((other0, other1, other2, other3))
        ]
        stores.append(pltpu.make_async_copy(packed.at[pl.ds(PIECES * size, PIECES * size)], mine, sems.at[PIECES]))

        def pack(d, owner, first):
            pack66(rel_grad, (owner * CHIPS + d) * PER, packed, (first + d) * PACK66)

        chips = CHIPS // PIECES
        for i in range(PIECES):
            blocks_loop(chips, 2, lambda d, i=i: pack(i * chips + d, 1 - side, 0))
            stores[i].start()
        blocks_loop(CHIPS, 2, lambda d: pack(d, side, CHIPS))
        stores[PIECES].start()
        for store in stores:
            store.wait()


EDGE_TILE = 256


def gradients(heads, grad_at, core, tail_local, neg_acc, h, r, p, back):
    half = jax.ShapeDtypeStruct((CHIPS * PACK66, LANES), f32)
    piece = jax.ShapeDtypeStruct((CHIPS * PACK66 // PIECES, LANES), f32)
    block = pl.BlockSpec((CHUNKS, EDGE_TILE, LANES), lambda i: (0, i, 0))
    whole = pl.BlockSpec((ENT_DEV * CHUNKS, LANES), lambda i: (0, 0))
    return pl.pallas_call(
        edge_kernel,
        grid=(E_DEV // EDGE_TILE,),
        out_shape=(half, piece, piece, piece, piece, jax.ShapeDtypeStruct((ENT_DEV * CHUNKS, LANES), f32)),
        in_specs=[SMEM, SMEM, SMEM, ANY, pl.BlockSpec((NEG, CHUNKS * LANES), lambda i: (0, 0)), block, block, block, block],
        out_specs=(HBM,) * 5 + (whole,),
        scratch_shapes=[
            pltpu.VMEM((N_DEV * PER, LANES), f32),
            pltpu.VMEM((N_DEV * PACK66, LANES), f32),
            pltpu.VMEM((EDGE_TILE * CHUNKS, LANES), f32),
            pltpu.VMEM((EDGE_TILE * CHUNKS, LANES), f32),
            pltpu.SemaphoreType.DMA((PIECES + 1,)),
        ],
        compiler_params=params(58),
        cost_estimate=cost(0, 1 << 20),
        name="gradients",
    )(heads, grad_at, core, tail_local, neg_acc, h, r, p, back)


def merge_kernel(
    color, mine, got0, got1, got2, got3,
    keep, send0, send1, send2, send3, send4,
    total, came, sems, came_sems,
):
    each = CHIPS // PIECES
    loads, arrivals = [], []
    for i, got in enumerate((got0, got1, got2, got3)):
        here = pl.ds(i * each, each)
        loads.append(pltpu.make_async_copy(mine.at[here], total.at[here], sems.at[i]))
        arrivals.append(pltpu.make_async_copy(got, came.at[here], came_sems.at[i]))
        loads[i].start()
        arrivals[i].start()
    own = pl.ds(pl.multiple_of(color[0] * KEPT, 8), KEPT)
    theirs = pl.ds(pl.multiple_of((1 - color[0]) * KEPT, 8), KEPT)
    stores = [
        pltpu.make_async_copy(total.at[pl.ds(first, last - first), theirs], send, sems.at[PIECES + i])
        for i, (first, last, send) in enumerate(
            zip(GROUPS[:-1], GROUPS[1:], (send0, send1, send2, send3, send4), strict=True)
        )
    ]
    stores.append(pltpu.make_async_copy(total.at[:, own], keep, sems.at[PIECES + WAYS]))
    started = 0
    for i in range(PIECES):
        loads[i].wait()
        arrivals[i].wait()

        def add(d, carry, i=i):
            total[i * each + d] = total[i * each + d] + came[i * each + d]
            return carry

        lax.fori_loop(0, each, add, 0)
        while started < WAYS and GROUPS[started + 1] <= (i + 1) * each:
            stores[started].start()
            started += 1
    stores[WAYS].start()
    for store in stores:
        store.wait()


def merge(color, mine, got):
    def blocks(n, rows):
        return jax.ShapeDtypeStruct((n, rows, LANES), f32)

    return pl.pallas_call(
        merge_kernel,
        out_shape=(blocks(CHIPS, KEPT),) + tuple(blocks(b - a, KEPT) for a, b in zip(GROUPS[:-1], GROUPS[1:], strict=True)),
        in_specs=[SMEM, ANY] + [ANY] * PIECES,
        out_specs=(HBM,) * (WAYS + 1),
        scratch_shapes=[
            pltpu.VMEM((CHIPS, PACK66, LANES), f32),
            pltpu.VMEM((CHIPS, PACK66, LANES), f32),
            pltpu.SemaphoreType.DMA((PIECES + WAYS + 1,)),
            pltpu.SemaphoreType.DMA((PIECES,)),
        ],
        compiler_params=params(58),
        cost_estimate=cost(0, 1 << 16),
        name="merge",
    )(color, mine.reshape(CHIPS, PACK66, LANES), *[x.reshape(CHIPS // PIECES, PACK66, LANES) for x in got])


def meet_kernel(keep, got0, got1, got2, got3, got4, out, total, sems):
    spans = list(zip(GROUPS[:-1], GROUPS[1:], (got0, got1, got2, got3, got4), strict=True))
    loads, stores = [], []
    for i, (first, last, _) in enumerate(spans):
        here = pl.ds(first, last - first)
        loads.append(pltpu.make_async_copy(keep.at[here], total.at[here], sems.at[i]))
        stores.append(pltpu.make_async_copy(total.at[here], out.at[here], sems.at[WAYS + i]))
        loads[i].start()
    for i, (first, last, got) in enumerate(spans):
        loads[i].wait()

        def add(d, carry, first=first, got=got):
            total[first + d] = total[first + d] + got[d]
            return carry

        lax.fori_loop(0, last - first, add, 0)
        stores[i].start()
    for store in stores:
        store.wait()


def meet(keep, got):
    return pl.pallas_call(
        meet_kernel,
        out_shape=jax.ShapeDtypeStruct((CHIPS, KEPT, LANES), f32),
        in_specs=[ANY] + [VMEM] * WAYS,
        out_specs=HBM,
        scratch_shapes=[pltpu.VMEM((CHIPS, KEPT, LANES), f32), pltpu.SemaphoreType.DMA((2 * WAYS,))],
        compiler_params=params(47),
        cost_estimate=cost(0, 1 << 16),
        name="meet",
    )(keep, *got)


def color_of(chip):
    return (chip // 16 + chip // 4 + chip) % 2


def matching(k):
    pairs = []
    for chip in range(CHIPS):
        if color_of(chip) == 0:
            at = [chip // 16, chip // 4 % 4, chip % 4]
            at[k // 2] = (at[k // 2] + (1 if k % 2 == 0 else 3)) % 4
            mate = (at[0] * 4 + at[1]) * 4 + at[2]
            pairs += [(chip, mate), (mate, chip)]
    return pairs


def returned_kernel(asked, packed, head_grad, out, returned):
    out[...] = head_grad[...]
    unpack_slots(packed, returned, 0)

    def body(pair):
        i = pair * 2
        add_two(out, asked[i], asked[i + 1], returned[row(i), :], returned[row(i + 1), :])

    rows_loop(SLOTS // 2, body)


def add_returned(asked, returned, head_grad):
    return pl.pallas_call(
        returned_kernel,
        out_shape=jax.ShapeDtypeStruct((ENT_DEV * CHUNKS, LANES), f32),
        in_specs=[SMEM, VMEM, VMEM],
        out_specs=VMEM,
        scratch_shapes=[pltpu.VMEM((SLOTS * CHUNKS, LANES), f32)],
        compiler_params=params(24),
        cost_estimate=cost(0, 10 << 20),
        name="add_returned",
    )(asked, returned, head_grad)


def adagrad(grad, n, table_t, state, new_table_t, new_state):
    g = [chunk_of(grad, c, n).T for c in range(CHUNKS)]
    squares = (g[0] * g[0] + g[1] * g[1]) + (g[2] * g[2] + g[3] * g[3])
    state_now = state[...] + jnp.sum(squares, axis=0, keepdims=True) * (1.0 / WIDTH)
    new_state[...] = state_now
    below = jnp.sqrt(state_now) + 1e-10
    for c, (start, size) in enumerate(SPANS):
        spot = slice(start, start + size)
        new_table_t[spot, :] = table_t[spot, :] - rate * g[c][:size] / below


def step_kernel(
    negatives, local_grad, parts, table_now, state, rel, rel_state,
    new_table_t, new_state, new_rel, new_rel_state,
    grad, came, table_t, share, packed, wide, rel_t, new_rel_t, states, new_states, sems,
):
    each = CHIPS // PIECES
    loads = []
    for i in range(PIECES):
        here = pl.ds(i * each, each)
        loads.append(pltpu.make_async_copy(parts.at[here], came.at[here], sems.at[i]))
    loads.append(pltpu.make_async_copy(local_grad, grad, sems.at[PIECES]))
    loads.append(pltpu.make_async_copy(table_now, table_t, sems.at[PIECES + 1]))
    for load in loads:
        load.start()
    share[...] = jnp.zeros_like(share)
    turn_relations(rel, wide, rel_t)
    new_rel_t[...] = jnp.zeros_like(new_rel_t)
    states[...] = jnp.zeros_like(states)
    states[:, 0:REL_DEV] = rel_state[...]
    totals = [None, None]
    for i in range(PIECES):
        loads[i].wait()
        for chip in range(i * each, (i + 1) * each):
            half = color_of(chip)
            totals[half] = came[chip] if totals[half] is None else totals[half] + came[chip]
    packed[0:KEPT, :] = totals[0]
    packed[KEPT:PACK66, :] = totals[1]
    unpack66(packed, 0, share, 0)
    adagrad(share, LANES, rel_t, states, new_rel_t, new_states)
    new_rel[...] = new_rel_t[...].T[0:REL_DEV, 0:WIDTH]
    new_rel_state[...] = new_states[:, 0:REL_DEV]
    loads[PIECES].wait()
    for i in range(NEG_DEV):
        at = row(negatives[i])
        grad[at, :] = grad[at, :] + share[REL4 + CHUNKS * i : REL4 + CHUNKS * (i + 1), :]
    loads[PIECES + 1].wait()
    adagrad(grad, ENT_DEV, table_t, state, new_table_t, new_state)


def adagrad_step(negatives, local_grad, parts, table_t, state, rel, rel_state):
    def like(*shape):
        return jax.ShapeDtypeStruct(shape, f32)

    return pl.pallas_call(
        step_kernel,
        out_shape=(like(WIDTH, ENT_DEV), like(1, ENT_DEV), like(REL_DEV, WIDTH), like(1, REL_DEV)),
        in_specs=[SMEM, ANY, ANY, ANY] + [VMEM] * 3,
        out_specs=(VMEM,) * 4,
        scratch_shapes=[
            pltpu.VMEM((ENT_DEV * CHUNKS, LANES), f32),
            pltpu.VMEM((CHIPS, KEPT, LANES), f32),
            pltpu.VMEM((WIDTH, ENT_DEV), f32),
            pltpu.VMEM((CHUNKS * LANES, LANES), f32),
            pltpu.VMEM((PACK66, LANES), f32),
            pltpu.VMEM((LANES, CHUNKS * LANES), f32),
            pltpu.VMEM((CHUNKS * LANES, LANES), f32),
            pltpu.VMEM((CHUNKS * LANES, LANES), f32),
            pltpu.VMEM((1, LANES), f32),
            pltpu.VMEM((1, LANES), f32),
            pltpu.SemaphoreType.DMA((PIECES + 2,)),
        ],
        compiler_params=params(58),
        cost_estimate=cost(0, 16 << 20),
        name="adagrad_step",
    )(negatives, local_grad, parts, table_t, state, rel, rel_state)


def local(
    entity_table,
    entity_state,
    relation_table,
    relation_state,
    heads,
    relations,
    tails,
    pull_lists,
    negatives,
):
    table_t = entity_table.T
    owner, place = relations // REL_DEV, relations % REL_DEV
    rel_at = owner * (REL_DEV + NEG_DEV) + place
    grad_at = ((owner % 2) * CHIPS + owner // 2) * (REL_DEV + NEG_DEV) + place
    core = lax.axis_index("c")

    tab4, send = prep(negatives, table_t, relation_table)
    shared = lax.all_gather(send, AXES, axis=0, tiled=True)
    asked = lax.all_to_all(pull_lists, AXES, split_axis=0, concat_axis=0, tiled=True).reshape(SLOTS)
    rows_out, shared = lax.optimization_barrier((pull_rows(asked, tab4), shared))

    def exchange(rows):
        rows = rows.reshape(N_DEV, PACK16, LANES)
        return lax.all_to_all(rows, AXES, split_axis=0, concat_axis=0, tiled=True).reshape(N_DEV * PACK16, LANES)

    fetched = exchange(rows_out)
    q, h, r, back, neg_acc = queries(heads, rel_at, tab4, shared)
    p, tail_local, outgoing = tail_terms(tails, tab4, fetched, q)
    returned = exchange(outgoing)
    mine, *others, head_grad = gradients(
        heads, grad_at, core.reshape(1), tail_local, neg_acc, h, r, p, back
    )
    color = (lax.axis_index("x") + lax.axis_index("z") + lax.axis_index("y")) % 2
    got = [lax.ppermute(other, "c", [(0, 1), (1, 0)]) for other in others]
    merged = merge(color.reshape(1), mine, got)
    (keep, *sends), returned = lax.optimization_barrier((merged, returned))
    met = meet(keep, [lax.ppermute(send, AXES[:3], matching(k)) for k, send in enumerate(sends)])
    parts = lax.all_to_all(met, AXES[:3], split_axis=0, concat_axis=0, tiled=True)
    local_grad = add_returned(asked, returned, head_grad)
    new_table_t, new_state, new_rel, new_rel_state = adagrad_step(
        negatives,
        local_grad,
        parts,
        table_t,
        entity_state.reshape(1, ENT_DEV),
        relation_table,
        relation_state.reshape(1, REL_DEV),
    )
    return (
        new_table_t.T,
        new_state.reshape(ENT_DEV),
        new_rel,
        new_rel_state.reshape(REL_DEV),
    )


def solution(mesh):
    grid = Mesh(mesh.devices.reshape(4, 4, 4, 2), AXES)
    rows, flat = P(AXES, None), P(AXES)
    in_specs = (rows, flat, rows, flat, flat, flat, flat, rows, flat)
    out_specs = (rows, flat, rows, flat)
    return jax.shard_map(local, mesh=grid, in_specs=in_specs, out_specs=out_specs, check_vma=False)
```

```python
import jax
import jax.numpy as jnp
from jax import lax
from jax.experimental import pallas as pl
from jax.experimental.pallas import tpu as pltpu
from jax.sharding import Mesh, PartitionSpec as P

rate = 0.1
AXES = ("x", "z", "y", "c")
WIDTH = 400
HALF = 200
LANES = 128
CHUNKS = 4
SPANS = ((0, 128), (128, 72), (200, 128), (328, 72))
ENT_DEV = 1024
REL_DEV = 58
NEG_DEV = 8
E_DEV = 2048
N_DEV = 128
CAP = 16
NEG = N_DEV * NEG_DEV
SLOTS = N_DEV * CAP
CHIPS = N_DEV // 2
PER = CHUNKS * (REL_DEV + NEG_DEV)
REL4 = CHUNKS * REL_DEV
TILE = 256
PACK16 = 56
PACK66 = 208
PIECES = 4
KEPT = PACK66 // 2
GROUPS = (0, 13, 26, 39, 52, 64)
WAYS = len(GROUPS) - 1
UNROLL = 16

f32 = jnp.float32
bf16 = jnp.bfloat16
VMEM = pl.BlockSpec(memory_space=pltpu.VMEM)
SMEM = pl.BlockSpec(memory_space=pltpu.SMEM)
ANY = pl.BlockSpec(memory_space=pl.ANY)
HBM = pl.BlockSpec(memory_space=pltpu.HBM)


def params(mib):
    return pltpu.CompilerParams(vmem_limit_bytes=mib * 1024 * 1024)


def cost(flops, moved):
    return pl.CostEstimate(flops=flops, bytes_accessed=moved, transcendentals=0)


def chunk_of(ref, c, n):
    return ref[pl.ds(c, n, stride=CHUNKS), :]


def row(i):
    return pl.ds(pl.multiple_of(i * CHUNKS, CHUNKS), CHUNKS)


def split(x):
    hi = x.astype(bf16)
    return hi, (x - hi.astype(f32)).astype(bf16)


def dot3(a, b, dims):
    (ah, al), (bh, bl) = a, b

    def one(p, q):
        return lax.dot_general(p, q, (dims, ((), ())), preferred_element_type=f32)

    return one(ah, bh) + (one(ah, bl) + one(al, bh))


def rows_loop(n, body):
    def step(s, carry):
        for u in range(UNROLL):
            body(s * UNROLL + u)
        return carry

    lax.fori_loop(0, n // UNROLL, step, 0)


def add_two(acc, a, b, first, second):
    old_a, old_b = acc[row(a), :], acc[row(b), :]
    acc[row(a), :] = old_a + first
    acc[row(b), :] = (old_b + second) + jnp.where(a == b, first, jnp.zeros_like(first))


def lane(n):
    return lax.broadcasted_iota(jnp.int32, (n, LANES), 1)


def join(c1, c3):
    return jnp.where(lane(c1.shape[0]) < 72, c1, pltpu.roll(c3, 72, 1))


def rest(c3, k):
    return pltpu.roll(c3, (72 + 16 * k) % LANES, 1)


def part(joined, rem, k):
    at = lane(joined.shape[0])
    c1 = jnp.where(at < 72, joined, 0.0)
    tail = jnp.where(at < 72, pltpu.roll(rem, (56 - 16 * k) % LANES, 1), 0.0)
    return c1, jnp.where(at < 56, pltpu.roll(joined, 56, 1), tail)


def four(ref, base, n):
    return [ref[pl.ds(base + c, n, stride=CHUNKS), :] for c in range(CHUNKS)]


def pack16(src, src_base, dst, dst_base):
    rem = None
    for k in range(2):
        c0, c1, c2, c3 = four(src, src_base + 32 * k, 8)
        dst[pl.ds(dst_base + 8 * k, 8), :] = c0
        dst[pl.ds(dst_base + 16 + 8 * k, 8), :] = c2
        dst[pl.ds(dst_base + 32 + 8 * k, 8), :] = join(c1, c3)
        rem = rest(c3, 0) if k == 0 else jnp.where(lane(8) < 16, rem, rest(c3, 1))
    dst[pl.ds(dst_base + 48, 8), :] = rem


def unpack16(src, src_base, dst, dst_base):
    rem = src[pl.ds(src_base + 48, 8), :]
    for k in range(2):
        c1, c3 = part(src[pl.ds(src_base + 32 + 8 * k, 8), :], rem, k)
        c0 = src[pl.ds(src_base + 8 * k, 8), :]
        c2 = src[pl.ds(src_base + 16 + 8 * k, 8), :]
        for c, piece in enumerate((c0, c1, c2, c3)):
            dst[pl.ds(dst_base + 32 * k + c, 8, stride=CHUNKS), :] = piece


def blocks_loop(n, unroll, body):
    def step(s, carry):
        for u in range(unroll):
            body(s * unroll + u)
        return carry

    lax.fori_loop(0, n // unroll, step, 0)


def pack_slots(src, src_base, dst):
    blocks_loop(N_DEV, 8, lambda d: pack16(src, src_base + d * CAP * CHUNKS, dst, d * PACK16))


def unpack_slots(src, dst, dst_base):
    blocks_loop(N_DEV, 8, lambda d: unpack16(src, d * PACK16, dst, dst_base + d * CAP * CHUNKS))


def pack66(src, src_base, dst, dst_base):
    rows = REL_DEV + NEG_DEV
    rem = None
    for k in range(9):
        n = 8 if k < 8 else 2
        c0, c1, c2, c3 = four(src, src_base + 32 * k, n)
        dst[pl.ds(dst_base + 8 * k, n), :] = c0
        dst[pl.ds(dst_base + rows + 8 * k, n), :] = c2
        dst[pl.ds(dst_base + 2 * rows + 8 * k, n), :] = join(c1, c3)
        if k == 8:
            dst[pl.ds(dst_base + 3 * rows + 8, 2), :] = rest(c3, 0)
        else:
            rem = rest(c3, k) if k == 0 else jnp.where(lane(8) < 16 * k, rem, rest(c3, k))
    dst[pl.ds(dst_base + 3 * rows, 8), :] = rem


def unpack66(src, src_base, dst, dst_base):
    rows = REL_DEV + NEG_DEV
    for k in range(9):
        n = 8 if k < 8 else 2
        rem = src[pl.ds(src_base + 3 * rows + (0 if k < 8 else 8), n), :]
        c1, c3 = part(src[pl.ds(src_base + 2 * rows + 8 * k, n), :], rem, k % 8)
        c0 = src[pl.ds(src_base + 8 * k, n), :]
        c2 = src[pl.ds(src_base + rows + 8 * k, n), :]
        for c, piece in enumerate((c0, c1, c2, c3)):
            dst[pl.ds(dst_base + 32 * k + c, n, stride=CHUNKS), :] = piece


def to_chunks(src, dst, n):
    for c, (start, size) in enumerate(SPANS):
        piece = src[start : start + size, :]
        if size < LANES:
            piece = jnp.concatenate([piece, jnp.zeros((LANES - size, n), f32)], axis=0)
        dst[pl.ds(c, n, stride=CHUNKS), :] = piece.T


def turn_relations(rel, wide, rel_t):
    wide[...] = jnp.zeros_like(wide)
    wide[0:REL_DEV, 0:WIDTH] = rel[...]
    rel_t[...] = wide[...].T


def prep_kernel(negatives, table_t, rel, tab4, send, rel4, wide, rel_t):
    turn_relations(rel, wide, rel_t)
    to_chunks(table_t, tab4, ENT_DEV)
    to_chunks(rel_t, rel4, LANES)
    for i in range(NEG_DEV):
        rel4[REL4 + CHUNKS * i : REL4 + CHUNKS * (i + 1), :] = tab4[row(negatives[i]), :]
    pack66(rel4, 0, send, 0)


def prep(negatives, table_t, rel):
    return pl.pallas_call(
        prep_kernel,
        out_shape=(
            jax.ShapeDtypeStruct((ENT_DEV * CHUNKS, LANES), f32),
            jax.ShapeDtypeStruct((PACK66, LANES), f32),
        ),
        in_specs=[SMEM, VMEM, VMEM],
        out_specs=(VMEM, VMEM),
        scratch_shapes=[
            pltpu.VMEM((LANES * CHUNKS, LANES), f32),
            pltpu.VMEM((LANES, CHUNKS * LANES), f32),
            pltpu.VMEM((CHUNKS * LANES, LANES), f32),
        ],
        compiler_params=params(58),
        cost_estimate=cost(0, 8 << 20),
        name="prep",
    )(negatives, table_t, rel)


def pull_kernel(asked, tab4, out, picked, packed, sem):
    def body(i):
        picked[row(i), :] = tab4[row(asked[i]), :]

    rows_loop(SLOTS, body)
    pack_slots(picked, 0, packed)
    store = pltpu.make_async_copy(packed, out, sem)
    store.start()
    store.wait()


def pull_rows(asked, tab4):
    return pl.pallas_call(
        pull_kernel,
        out_shape=jax.ShapeDtypeStruct((N_DEV * PACK16, LANES), f32),
        in_specs=[SMEM, VMEM],
        out_specs=HBM,
        scratch_shapes=[
            pltpu.VMEM((SLOTS * CHUNKS, LANES), f32),
            pltpu.VMEM((N_DEV * PACK16, LANES), f32),
            pltpu.SemaphoreType.DMA,
        ],
        compiler_params=params(58),
        cost_estimate=cost(0, 8 << 20),
        name="pull_rows",
    )(asked, tab4)


def query_kernel(
    heads, rel_at, tab4, shared,
    q_out, h_out, r_out, back_out, neg_acc,
    tab, rel, packed, n_hi, n_lo, t_hi, t_lo, hb, rb, sems,
):
    step = pl.program_id(0)

    @pl.when(step == 0)
    def _():
        size = N_DEV * PACK66 // PIECES
        loads = [
            pltpu.make_async_copy(shared.at[pl.ds(i * size, size)], packed.at[pl.ds(i * size, size)], sems.at[i])
            for i in range(PIECES)
        ]
        loads.append(pltpu.make_async_copy(tab4, tab, sems.at[PIECES]))
        for load in loads:
            load.start()
        neg_acc[...] = jnp.zeros_like(neg_acc)
        each = N_DEV // PIECES
        for i in range(PIECES):
            loads[i].wait()
            blocks_loop(each, 2, lambda d, i=i: unpack66(packed, (i * each + d) * PACK66, rel, (i * each + d) * PER))
        loads[PIECES].wait()

        for c in range(CHUNKS):
            lanes = slice(c * LANES, (c + 1) * LANES)

            def place(d, carry, c=c):
                rows = pl.ds(pl.multiple_of(d * NEG_DEV, NEG_DEV), NEG_DEV)
                hb[rows, :] = rel[pl.ds(d * PER + REL4 + c, NEG_DEV, stride=CHUNKS), :]
                return carry

            lax.fori_loop(0, N_DEV, place, 0)
            piece = hb[...]
            n_hi[:, lanes], n_lo[:, lanes] = split(piece)
            t_hi[lanes, :], t_lo[lanes, :] = split(piece.T)

    base = step * TILE

    def gather(i):
        hb[row(i), :] = tab[row(heads[base + i]), :]
        rb[row(i), :] = rel[row(rel_at[base + i]), :]

    rows_loop(TILE, gather)
    h = [chunk_of(hb, c, TILE) for c in range(CHUNKS)]
    r = [chunk_of(rb, c, TILE) for c in range(CHUNKS)]
    q = [h[0] * r[0] - h[2] * r[2], h[1] * r[1] - h[3] * r[3], h[0] * r[2] + h[2] * r[0], h[1] * r[3] + h[3] * r[1]]
    for c in range(CHUNKS):
        q_out[c] = q[c]
        h_out[c] = h[c]
        r_out[c] = r[c]
    q = split(jnp.concatenate(q, axis=1))
    negative = dot3(q, (t_hi[...], t_lo[...]), ((1,), (0,)))
    neg_grad = split(jax.nn.sigmoid(negative) * (1.0 / NEG))
    neg_acc[...] += dot3(neg_grad, q, ((0,), (0,)))
    back = dot3(neg_grad, (n_hi[...], n_lo[...]), ((1,), (0,)))
    for c in range(CHUNKS):
        back_out[c] = back[:, c * LANES : (c + 1) * LANES]


PLANE = jax.ShapeDtypeStruct((CHUNKS, E_DEV, LANES), f32)
BLOCK = pl.BlockSpec((CHUNKS, TILE, LANES), lambda i: (0, i, 0))


def queries(heads, rel_at, tab4, shared):
    rows = pltpu.VMEM((TILE * CHUNKS, LANES), f32)
    wide = pltpu.VMEM((NEG, CHUNKS * LANES), bf16)
    tall = pltpu.VMEM((CHUNKS * LANES, NEG), bf16)
    return pl.pallas_call(
        query_kernel,
        grid=(E_DEV // TILE,),
        out_shape=(PLANE, PLANE, PLANE, PLANE, jax.ShapeDtypeStruct((NEG, CHUNKS * LANES), f32)),
        in_specs=[SMEM, SMEM, ANY, ANY],
        out_specs=(BLOCK, BLOCK, BLOCK, BLOCK, pl.BlockSpec((NEG, CHUNKS * LANES), lambda i: (0, 0))),
        scratch_shapes=[
            pltpu.VMEM((ENT_DEV * CHUNKS, LANES), f32),
            pltpu.VMEM((N_DEV * PER, LANES), f32),
            pltpu.VMEM((N_DEV * PACK66, LANES), f32),
            wide,
            wide,
            tall,
            tall,
            rows,
            rows,
            pltpu.SemaphoreType.DMA((PIECES + 1,)),
        ],
        compiler_params=params(58),
        cost_estimate=cost(36_000_000_000, 60 << 20),
        name="queries",
    )(heads, rel_at, tab4, shared)


def tail_kernel(
    tails, tab4, fetched, q_in,
    p_out, tail_local, outgoing,
    ext, ext_grad, packed, tb, sems,
):
    step = pl.program_id(0)
    local = ENT_DEV * CHUNKS
    size = N_DEV * PACK16 // PIECES
    each = N_DEV // PIECES

    @pl.when(step == 0)
    def _():
        loads = []
        for i in range(PIECES):
            here = pl.ds(i * size, size)
            loads.append(pltpu.make_async_copy(fetched.at[here], packed.at[here], sems.at[i]))
        loads.append(pltpu.make_async_copy(tab4, ext.at[pl.ds(0, local)], sems.at[PIECES]))
        for load in loads:
            load.start()
        ext_grad[...] = jnp.zeros_like(ext_grad)
        for i in range(PIECES):
            loads[i].wait()

            def unpack(d, i=i):
                unpack16(packed, (i * each + d) * PACK16, ext, local + (i * each + d) * CAP * CHUNKS)

            blocks_loop(each, 8, unpack)
        loads[PIECES].wait()

    base = step * TAIL_TILE

    def gather(i):
        tb[row(i), :] = ext[row(tails[base + i]), :]

    rows_loop(TAIL_TILE, gather)
    t = [chunk_of(tb, c, TAIL_TILE) for c in range(CHUNKS)]
    q = [q_in[c] for c in range(CHUNKS)]
    score = (q[0] * t[0] + q[1] * t[1]) + (q[2] * t[2] + q[3] * t[3])
    pos_grad = jax.nn.sigmoid(jnp.sum(score, axis=1, keepdims=True)) - 1.0
    for c in range(CHUNKS):
        p_out[c] = pos_grad * t[c]
        tb[pl.ds(c, TAIL_TILE, stride=CHUNKS), :] = pos_grad * q[c]

    def scatter(pair):
        i = pair * 2
        add_two(ext_grad, tails[base + i], tails[base + i + 1], tb[row(i), :], tb[row(i + 1), :])

    rows_loop(TAIL_TILE // 2, scatter)

    @pl.when(step == E_DEV // TAIL_TILE - 1)
    def _():
        stores = []
        for i in range(PIECES):
            here = pl.ds(i * size, size)
            stores.append(pltpu.make_async_copy(packed.at[here], outgoing.at[here], sems.at[i]))
        stores.append(pltpu.make_async_copy(ext_grad.at[pl.ds(0, local)], tail_local, sems.at[PIECES]))
        stores[PIECES].start()
        for i in range(PIECES):

            def pack(d, i=i):
                pack16(ext_grad, local + (i * each + d) * CAP * CHUNKS, packed, (i * each + d) * PACK16)

            blocks_loop(each, 8, pack)
            stores[i].start()
        for store in stores:
            store.wait()


TAIL_TILE = 512


def tail_terms(tails, tab4, fetched, q):
    block = pl.BlockSpec((CHUNKS, TAIL_TILE, LANES), lambda i: (0, i, 0))
    return pl.pallas_call(
        tail_kernel,
        grid=(E_DEV // TAIL_TILE,),
        out_shape=(
            PLANE,
            jax.ShapeDtypeStruct((ENT_DEV * CHUNKS, LANES), f32),
            jax.ShapeDtypeStruct((N_DEV * PACK16, LANES), f32),
        ),
        in_specs=[SMEM, ANY, ANY, block],
        out_specs=(block, HBM, HBM),
        scratch_shapes=[
            pltpu.VMEM(((ENT_DEV + SLOTS) * CHUNKS, LANES), f32),
            pltpu.VMEM(((ENT_DEV + SLOTS) * CHUNKS, LANES), f32),
            pltpu.VMEM((N_DEV * PACK16, LANES), f32),
            pltpu.VMEM((TAIL_TILE * CHUNKS, LANES), f32),
            pltpu.SemaphoreType.DMA((PIECES + 1,)),
        ],
        compiler_params=params(58),
        cost_estimate=cost(0, 30 << 20),
        name="tail_terms",
    )(tails, tab4, fetched, q)


def edge_kernel(
    heads, grad_at, core, tail_local, neg_acc, h_in, r_in, p_in, back_in,
    mine, other0, other1, other2, other3, head_grad,
    rel_grad, packed, hb, rb, sems,
):
    step = pl.program_id(0)

    @pl.when(step == 0)
    def _():
        start = pltpu.make_async_copy(tail_local, head_grad, sems.at[0])
        start.start()
        rel_grad[...] = jnp.zeros_like(rel_grad)
        start.wait()

    base = step * EDGE_TILE
    g = [p_in[c] + back_in[c] for c in range(CHUNKS)]
    for k in range(2):
        for buf, src in ((hb, r_in), (rb, h_in)):
            buf[pl.ds(k, EDGE_TILE, stride=CHUNKS), :] = g[k] * src[k] + g[k + 2] * src[k + 2]
            buf[pl.ds(k + 2, EDGE_TILE, stride=CHUNKS), :] = g[k + 2] * src[k] - g[k] * src[k + 2]

    def scatter(pair):
        i = pair * 2
        add_two(head_grad, heads[base + i], heads[base + i + 1], hb[row(i), :], hb[row(i + 1), :])
        add_two(rel_grad, grad_at[base + i], grad_at[base + i + 1], rb[row(i), :], rb[row(i + 1), :])

    rows_loop(EDGE_TILE // 2, scatter)

    @pl.when(step == E_DEV // EDGE_TILE - 1)
    def _():
        def place(d, carry):
            spot = ((d % 2) * CHIPS + d // 2) * PER + REL4
            rows = pl.ds(pl.multiple_of(d * NEG_DEV, NEG_DEV), NEG_DEV)
            for c in range(CHUNKS):
                rel_grad[pl.ds(spot + c, NEG_DEV, stride=CHUNKS), :] = neg_acc[rows, c * LANES : (c + 1) * LANES]
            return carry

        lax.fori_loop(0, N_DEV, place, 0)
        side = core[0]
        size = CHIPS * PACK66 // PIECES
        stores = [
            pltpu.make_async_copy(packed.at[pl.ds(i * size, size)], other, sems.at[i])
            for i, other in enumerate((other0, other1, other2, other3))
        ]
        stores.append(pltpu.make_async_copy(packed.at[pl.ds(PIECES * size, PIECES * size)], mine, sems.at[PIECES]))

        def pack(d, owner, first):
            pack66(rel_grad, (owner * CHIPS + d) * PER, packed, (first + d) * PACK66)

        chips = CHIPS // PIECES
        for i in range(PIECES):
            blocks_loop(chips, 2, lambda d, i=i: pack(i * chips + d, 1 - side, 0))
            stores[i].start()
        blocks_loop(CHIPS, 2, lambda d: pack(d, side, CHIPS))
        stores[PIECES].start()
        for store in stores:
            store.wait()


EDGE_TILE = 256


def gradients(heads, grad_at, core, tail_local, neg_acc, h, r, p, back):
    half = jax.ShapeDtypeStruct((CHIPS * PACK66, LANES), f32)
    piece = jax.ShapeDtypeStruct((CHIPS * PACK66 // PIECES, LANES), f32)
    block = pl.BlockSpec((CHUNKS, EDGE_TILE, LANES), lambda i: (0, i, 0))
    whole = pl.BlockSpec((ENT_DEV * CHUNKS, LANES), lambda i: (0, 0))
    return pl.pallas_call(
        edge_kernel,
        grid=(E_DEV // EDGE_TILE,),
        out_shape=(half, piece, piece, piece, piece, jax.ShapeDtypeStruct((ENT_DEV * CHUNKS, LANES), f32)),
        in_specs=[SMEM, SMEM, SMEM, ANY, pl.BlockSpec((NEG, CHUNKS * LANES), lambda i: (0, 0)), block, block, block, block],
        out_specs=(HBM,) * 5 + (whole,),
        scratch_shapes=[
            pltpu.VMEM((N_DEV * PER, LANES), f32),
            pltpu.VMEM((N_DEV * PACK66, LANES), f32),
            pltpu.VMEM((EDGE_TILE * CHUNKS, LANES), f32),
            pltpu.VMEM((EDGE_TILE * CHUNKS, LANES), f32),
            pltpu.SemaphoreType.DMA((PIECES + 1,)),
        ],
        compiler_params=params(58),
        cost_estimate=cost(0, 1 << 20),
        name="gradients",
    )(heads, grad_at, core, tail_local, neg_acc, h, r, p, back)


def merge_kernel(
    color, mine, got0, got1, got2, got3,
    keep, send0, send1, send2, send3, send4,
    total, came, sems, came_sems,
):
    each = CHIPS // PIECES
    loads, arrivals = [], []
    for i, got in enumerate((got0, got1, got2, got3)):
        here = pl.ds(i * each, each)
        loads.append(pltpu.make_async_copy(mine.at[here], total.at[here], sems.at[i]))
        arrivals.append(pltpu.make_async_copy(got, came.at[here], came_sems.at[i]))
        loads[i].start()
        arrivals[i].start()
    own = pl.ds(pl.multiple_of(color[0] * KEPT, 8), KEPT)
    theirs = pl.ds(pl.multiple_of((1 - color[0]) * KEPT, 8), KEPT)
    stores = [
        pltpu.make_async_copy(total.at[pl.ds(first, last - first), theirs], send, sems.at[PIECES + i])
        for i, (first, last, send) in enumerate(
            zip(GROUPS[:-1], GROUPS[1:], (send0, send1, send2, send3, send4), strict=True)
        )
    ]
    stores.append(pltpu.make_async_copy(total.at[:, own], keep, sems.at[PIECES + WAYS]))
    started = 0
    for i in range(PIECES):
        loads[i].wait()
        arrivals[i].wait()

        def add(d, carry, i=i):
            total[i * each + d] = total[i * each + d] + came[i * each + d]
            return carry

        lax.fori_loop(0, each, add, 0)
        while started < WAYS and GROUPS[started + 1] <= (i + 1) * each:
            stores[started].start()
            started += 1
    stores[WAYS].start()
    for store in stores:
        store.wait()


def merge(color, mine, got):
    def blocks(n, rows):
        return jax.ShapeDtypeStruct((n, rows, LANES), f32)

    return pl.pallas_call(
        merge_kernel,
        out_shape=(blocks(CHIPS, KEPT),) + tuple(blocks(b - a, KEPT) for a, b in zip(GROUPS[:-1], GROUPS[1:], strict=True)),
        in_specs=[SMEM, ANY] + [ANY] * PIECES,
        out_specs=(HBM,) * (WAYS + 1),
        scratch_shapes=[
            pltpu.VMEM((CHIPS, PACK66, LANES), f32),
            pltpu.VMEM((CHIPS, PACK66, LANES), f32),
            pltpu.SemaphoreType.DMA((PIECES + WAYS + 1,)),
            pltpu.SemaphoreType.DMA((PIECES,)),
        ],
        compiler_params=params(58),
        cost_estimate=cost(0, 1 << 16),
        name="merge",
    )(color, mine.reshape(CHIPS, PACK66, LANES), *[x.reshape(CHIPS // PIECES, PACK66, LANES) for x in got])


def meet_kernel(keep, got0, got1, got2, got3, got4, out, total, sems):
    spans = list(zip(GROUPS[:-1], GROUPS[1:], (got0, got1, got2, got3, got4), strict=True))
    loads, stores = [], []
    for i, (first, last, _) in enumerate(spans):
        here = pl.ds(first, last - first)
        loads.append(pltpu.make_async_copy(keep.at[here], total.at[here], sems.at[i]))
        stores.append(pltpu.make_async_copy(total.at[here], out.at[here], sems.at[WAYS + i]))
        loads[i].start()
    for i, (first, last, got) in enumerate(spans):
        loads[i].wait()

        def add(d, carry, first=first, got=got):
            total[first + d] = total[first + d] + got[d]
            return carry

        lax.fori_loop(0, last - first, add, 0)
        stores[i].start()
    for store in stores:
        store.wait()


def meet(keep, got):
    return pl.pallas_call(
        meet_kernel,
        out_shape=jax.ShapeDtypeStruct((CHIPS, KEPT, LANES), f32),
        in_specs=[ANY] + [VMEM] * WAYS,
        out_specs=HBM,
        scratch_shapes=[pltpu.VMEM((CHIPS, KEPT, LANES), f32), pltpu.SemaphoreType.DMA((2 * WAYS,))],
        compiler_params=params(47),
        cost_estimate=cost(0, 1 << 16),
        name="meet",
    )(keep, *got)


def color_of(chip):
    return (chip // 16 + chip // 4 + chip) % 2


def matching(k):
    pairs = []
    for chip in range(CHIPS):
        if color_of(chip) == 0:
            at = [chip // 16, chip // 4 % 4, chip % 4]
            at[k // 2] = (at[k // 2] + (1 if k % 2 == 0 else 3)) % 4
            mate = (at[0] * 4 + at[1]) * 4 + at[2]
            pairs += [(chip, mate), (mate, chip)]
    return pairs


def returned_kernel(asked, packed, head_grad, out, returned):
    out[...] = head_grad[...]
    unpack_slots(packed, returned, 0)

    def body(pair):
        i = pair * 2
        add_two(out, asked[i], asked[i + 1], returned[row(i), :], returned[row(i + 1), :])

    rows_loop(SLOTS // 2, body)


def add_returned(asked, returned, head_grad):
    return pl.pallas_call(
        returned_kernel,
        out_shape=jax.ShapeDtypeStruct((ENT_DEV * CHUNKS, LANES), f32),
        in_specs=[SMEM, VMEM, VMEM],
        out_specs=VMEM,
        scratch_shapes=[pltpu.VMEM((SLOTS * CHUNKS, LANES), f32)],
        compiler_params=params(24),
        cost_estimate=cost(0, 10 << 20),
        name="add_returned",
    )(asked, returned, head_grad)


def adagrad(grad, n, table_t, state, new_table_t, new_state):
    g = [chunk_of(grad, c, n).T for c in range(CHUNKS)]
    squares = (g[0] * g[0] + g[1] * g[1]) + (g[2] * g[2] + g[3] * g[3])
    state_now = state[...] + jnp.sum(squares, axis=0, keepdims=True) * (1.0 / WIDTH)
    new_state[...] = state_now
    below = jnp.sqrt(state_now) + 1e-10
    for c, (start, size) in enumerate(SPANS):
        spot = slice(start, start + size)
        new_table_t[spot, :] = table_t[spot, :] - rate * g[c][:size] / below


def step_kernel(
    negatives, local_grad, parts, table_now, state, rel, rel_state,
    new_table_t, new_state, new_rel, new_rel_state,
    grad, came, table_t, share, packed, wide, rel_t, new_rel_t, states, new_states, sems,
):
    each = CHIPS // PIECES
    loads = []
    for i in range(PIECES):
        here = pl.ds(i * each, each)
        loads.append(pltpu.make_async_copy(parts.at[here], came.at[here], sems.at[i]))
    loads.append(pltpu.make_async_copy(local_grad, grad, sems.at[PIECES]))
    loads.append(pltpu.make_async_copy(table_now, table_t, sems.at[PIECES + 1]))
    for load in loads:
        load.start()
    share[...] = jnp.zeros_like(share)
    turn_relations(rel, wide, rel_t)
    new_rel_t[...] = jnp.zeros_like(new_rel_t)
    states[...] = jnp.zeros_like(states)
    states[:, 0:REL_DEV] = rel_state[...]
    totals = [None, None]
    for i in range(PIECES):
        loads[i].wait()
        for chip in range(i * each, (i + 1) * each):
            half = color_of(chip)
            totals[half] = came[chip] if totals[half] is None else totals[half] + came[chip]
    packed[0:KEPT, :] = totals[0]
    packed[KEPT:PACK66, :] = totals[1]
    unpack66(packed, 0, share, 0)
    adagrad(share, LANES, rel_t, states, new_rel_t, new_states)
    new_rel[...] = new_rel_t[...].T[0:REL_DEV, 0:WIDTH]
    new_rel_state[...] = new_states[:, 0:REL_DEV]
    loads[PIECES].wait()
    for i in range(NEG_DEV):
        at = row(negatives[i])
        grad[at, :] = grad[at, :] + share[REL4 + CHUNKS * i : REL4 + CHUNKS * (i + 1), :]
    loads[PIECES + 1].wait()
    adagrad(grad, ENT_DEV, table_t, state, new_table_t, new_state)


def adagrad_step(negatives, local_grad, parts, table_t, state, rel, rel_state):
    def like(*shape):
        return jax.ShapeDtypeStruct(shape, f32)

    return pl.pallas_call(
        step_kernel,
        out_shape=(like(WIDTH, ENT_DEV), like(1, ENT_DEV), like(REL_DEV, WIDTH), like(1, REL_DEV)),
        in_specs=[SMEM, ANY, ANY, ANY] + [VMEM] * 3,
        out_specs=(VMEM,) * 4,
        scratch_shapes=[
            pltpu.VMEM((ENT_DEV * CHUNKS, LANES), f32),
            pltpu.VMEM((CHIPS, KEPT, LANES), f32),
            pltpu.VMEM((WIDTH, ENT_DEV), f32),
            pltpu.VMEM((CHUNKS * LANES, LANES), f32),
            pltpu.VMEM((PACK66, LANES), f32),
            pltpu.VMEM((LANES, CHUNKS * LANES), f32),
            pltpu.VMEM((CHUNKS * LANES, LANES), f32),
            pltpu.VMEM((CHUNKS * LANES, LANES), f32),
            pltpu.VMEM((1, LANES), f32),
            pltpu.VMEM((1, LANES), f32),
            pltpu.SemaphoreType.DMA((PIECES + 2,)),
        ],
        compiler_params=params(58),
        cost_estimate=cost(0, 16 << 20),
        name="adagrad_step",
    )(negatives, local_grad, parts, table_t, state, rel, rel_state)


def local(
    entity_table,
    entity_state,
    relation_table,
    relation_state,
    heads,
    relations,
    tails,
    pull_lists,
    negatives,
):
    table_t = entity_table.T
    owner, place = relations // REL_DEV, relations % REL_DEV
    rel_at = owner * (REL_DEV + NEG_DEV) + place
    grad_at = ((owner % 2) * CHIPS + owner // 2) * (REL_DEV + NEG_DEV) + place
    core = lax.axis_index("c")

    tab4, send = prep(negatives, table_t, relation_table)
    shared = lax.all_gather(send, AXES, axis=0, tiled=True)
    asked = lax.all_to_all(pull_lists, AXES, split_axis=0, concat_axis=0, tiled=True).reshape(SLOTS)
    rows_out, shared = lax.optimization_barrier((pull_rows(asked, tab4), shared))

    def exchange(rows):
        rows = rows.reshape(N_DEV, PACK16, LANES)
        return lax.all_to_all(rows, AXES, split_axis=0, concat_axis=0, tiled=True).reshape(N_DEV * PACK16, LANES)

    fetched = exchange(rows_out)
    q, h, r, back, neg_acc = queries(heads, rel_at, tab4, shared)
    p, tail_local, outgoing = tail_terms(tails, tab4, fetched, q)
    returned = exchange(outgoing)
    mine, *others, head_grad = gradients(
        heads, grad_at, core.reshape(1), tail_local, neg_acc, h, r, p, back
    )
    color = (lax.axis_index("x") + lax.axis_index("z") + lax.axis_index("y")) % 2
    got = [lax.ppermute(other, "c", [(0, 1), (1, 0)]) for other in others]
    merged = merge(color.reshape(1), mine, got)
    (keep, *sends), returned = lax.optimization_barrier((merged, returned))
    met = meet(keep, [lax.ppermute(send, AXES[:3], matching(k)) for k, send in enumerate(sends)])
    parts = lax.all_to_all(met, AXES[:3], split_axis=0, concat_axis=0, tiled=True)
    local_grad = add_returned(asked, returned, head_grad)
    new_table_t, new_state, new_rel, new_rel_state = adagrad_step(
        negatives,
        local_grad,
        parts,
        table_t,
        entity_state.reshape(1, ENT_DEV),
        relation_table,
        relation_state.reshape(1, REL_DEV),
    )
    return (
        new_table_t.T,
        new_state.reshape(ENT_DEV),
        new_rel,
        new_rel_state.reshape(REL_DEV),
    )


def solution(mesh):
    grid = Mesh(mesh.devices.reshape(4, 4, 4, 2), AXES)
    rows, flat = P(AXES, None), P(AXES)
    in_specs = (rows, flat, rows, flat, flat, flat, flat, rows, flat)
    out_specs = (rows, flat, rows, flat)
    return jax.shard_map(local, mesh=grid, in_specs=in_specs, out_specs=out_specs, check_vma=False)
```

```python
import jax
import jax.numpy as jnp
from jax import lax
from jax.experimental import pallas as pl
from jax.experimental.pallas import tpu as pltpu
from jax.sharding import Mesh, PartitionSpec as P

rate = 0.1
AXES = ("x", "z", "y", "c")
WIDTH = 400
HALF = 200
LANES = 128
CHUNKS = 4
SPANS = ((0, 128), (128, 72), (200, 128), (328, 72))
ENT_DEV = 1024
REL_DEV = 58
NEG_DEV = 8
E_DEV = 2048
N_DEV = 128
CAP = 16
NEG = N_DEV * NEG_DEV
SLOTS = N_DEV * CAP
CHIPS = N_DEV // 2
PER = CHUNKS * (REL_DEV + NEG_DEV)
REL4 = CHUNKS * REL_DEV
TILE = 256
PACK16 = 56
PACK66 = 208
PIECES = 4
KEPT = PACK66 // 2
GROUPS = (0, 13, 26, 39, 52, 64)
WAYS = len(GROUPS) - 1
UNROLL = 16

f32 = jnp.float32
bf16 = jnp.bfloat16
VMEM = pl.BlockSpec(memory_space=pltpu.VMEM)
SMEM = pl.BlockSpec(memory_space=pltpu.SMEM)
ANY = pl.BlockSpec(memory_space=pl.ANY)
HBM = pl.BlockSpec(memory_space=pltpu.HBM)


def params(mib):
    return pltpu.CompilerParams(vmem_limit_bytes=mib * 1024 * 1024)


def cost(flops, moved):
    return pl.CostEstimate(flops=flops, bytes_accessed=moved, transcendentals=0)


def chunk_of(ref, c, n):
    return ref[pl.ds(c, n, stride=CHUNKS), :]


def row(i):
    return pl.ds(pl.multiple_of(i * CHUNKS, CHUNKS), CHUNKS)


def split(x):
    hi = x.astype(bf16)
    return hi, (x - hi.astype(f32)).astype(bf16)


def dot3(a, b, dims):
    (ah, al), (bh, bl) = a, b

    def one(p, q):
        return lax.dot_general(p, q, (dims, ((), ())), preferred_element_type=f32)

    return one(ah, bh) + (one(ah, bl) + one(al, bh))


def rows_loop(n, body):
    def step(s, carry):
        for u in range(UNROLL):
            body(s * UNROLL + u)
        return carry

    lax.fori_loop(0, n // UNROLL, step, 0)


def add_two(acc, a, b, first, second):
    old_a, old_b = acc[row(a), :], acc[row(b), :]
    acc[row(a), :] = old_a + first
    acc[row(b), :] = (old_b + second) + jnp.where(a == b, first, jnp.zeros_like(first))


def add_four(acc, spots, terms):
    sums = [acc[row(spot), :] + term for spot, term in zip(spots, terms, strict=True)]
    for j in range(4):
        total = sums[j]
        for m in range(j):
            total = total + jnp.where(spots[m] == spots[j], terms[m], jnp.zeros_like(total))
        acc[row(spots[j]), :] = total


def lane(n):
    return lax.broadcasted_iota(jnp.int32, (n, LANES), 1)


def join(c1, c3):
    return jnp.where(lane(c1.shape[0]) < 72, c1, pltpu.roll(c3, 72, 1))


def rest(c3, k):
    return pltpu.roll(c3, (72 + 16 * k) % LANES, 1)


def part(joined, rem, k):
    at = lane(joined.shape[0])
    c1 = jnp.where(at < 72, joined, 0.0)
    tail = jnp.where(at < 72, pltpu.roll(rem, (56 - 16 * k) % LANES, 1), 0.0)
    return c1, jnp.where(at < 56, pltpu.roll(joined, 56, 1), tail)


def four(ref, base, n):
    return [ref[pl.ds(base + c, n, stride=CHUNKS), :] for c in range(CHUNKS)]


def pack16(src, src_base, dst, dst_base):
    rem = None
    for k in range(2):
        c0, c1, c2, c3 = four(src, src_base + 32 * k, 8)
        dst[pl.ds(dst_base + 8 * k, 8), :] = c0
        dst[pl.ds(dst_base + 16 + 8 * k, 8), :] = c2
        dst[pl.ds(dst_base + 32 + 8 * k, 8), :] = join(c1, c3)
        rem = rest(c3, 0) if k == 0 else jnp.where(lane(8) < 16, rem, rest(c3, 1))
    dst[pl.ds(dst_base + 48, 8), :] = rem


def unpack16(src, src_base, dst, dst_base):
    rem = src[pl.ds(src_base + 48, 8), :]
    for k in range(2):
        c1, c3 = part(src[pl.ds(src_base + 32 + 8 * k, 8), :], rem, k)
        c0 = src[pl.ds(src_base + 8 * k, 8), :]
        c2 = src[pl.ds(src_base + 16 + 8 * k, 8), :]
        for c, piece in enumerate((c0, c1, c2, c3)):
            dst[pl.ds(dst_base + 32 * k + c, 8, stride=CHUNKS), :] = piece


def blocks_loop(n, unroll, body):
    def step(s, carry):
        for u in range(unroll):
            body(s * unroll + u)
        return carry

    lax.fori_loop(0, n // unroll, step, 0)


def pack_slots(src, src_base, dst):
    blocks_loop(N_DEV, 8, lambda d: pack16(src, src_base + d * CAP * CHUNKS, dst, d * PACK16))


def unpack_slots(src, dst, dst_base):
    blocks_loop(N_DEV, 8, lambda d: unpack16(src, d * PACK16, dst, dst_base + d * CAP * CHUNKS))


def pack66(src, src_base, dst, dst_base):
    rows = REL_DEV + NEG_DEV
    rem = None
    for k in range(9):
        n = 8 if k < 8 else 2
        c0, c1, c2, c3 = four(src, src_base + 32 * k, n)
        dst[pl.ds(dst_base + 8 * k, n), :] = c0
        dst[pl.ds(dst_base + rows + 8 * k, n), :] = c2
        dst[pl.ds(dst_base + 2 * rows + 8 * k, n), :] = join(c1, c3)
        if k == 8:
            dst[pl.ds(dst_base + 3 * rows + 8, 2), :] = rest(c3, 0)
        else:
            rem = rest(c3, k) if k == 0 else jnp.where(lane(8) < 16 * k, rem, rest(c3, k))
    dst[pl.ds(dst_base + 3 * rows, 8), :] = rem


def unpack66(src, src_base, dst, dst_base):
    rows = REL_DEV + NEG_DEV
    for k in range(9):
        n = 8 if k < 8 else 2
        rem = src[pl.ds(src_base + 3 * rows + (0 if k < 8 else 8), n), :]
        c1, c3 = part(src[pl.ds(src_base + 2 * rows + 8 * k, n), :], rem, k % 8)
        c0 = src[pl.ds(src_base + 8 * k, n), :]
        c2 = src[pl.ds(src_base + rows + 8 * k, n), :]
        for c, piece in enumerate((c0, c1, c2, c3)):
            dst[pl.ds(dst_base + 32 * k + c, n, stride=CHUNKS), :] = piece


def to_chunks(src, dst, n):
    for c, (start, size) in enumerate(SPANS):
        piece = src[start : start + size, :]
        if size < LANES:
            piece = jnp.concatenate([piece, jnp.zeros((LANES - size, n), f32)], axis=0)
        dst[pl.ds(c, n, stride=CHUNKS), :] = piece.T


def turn_relations(rel, wide, rel_t):
    wide[...] = jnp.zeros_like(wide)
    wide[0:REL_DEV, 0:WIDTH] = rel[...]
    rel_t[...] = wide[...].T


def prep_kernel(negatives, table_t, rel, tab4, send, rel4, wide, rel_t):
    turn_relations(rel, wide, rel_t)
    to_chunks(table_t, tab4, ENT_DEV)
    to_chunks(rel_t, rel4, LANES)
    for i in range(NEG_DEV):
        rel4[REL4 + CHUNKS * i : REL4 + CHUNKS * (i + 1), :] = tab4[row(negatives[i]), :]
    pack66(rel4, 0, send, 0)


def prep(negatives, table_t, rel):
    return pl.pallas_call(
        prep_kernel,
        out_shape=(
            jax.ShapeDtypeStruct((ENT_DEV * CHUNKS, LANES), f32),
            jax.ShapeDtypeStruct((PACK66, LANES), f32),
        ),
        in_specs=[SMEM, VMEM, VMEM],
        out_specs=(VMEM, VMEM),
        scratch_shapes=[
            pltpu.VMEM((LANES * CHUNKS, LANES), f32),
            pltpu.VMEM((LANES, CHUNKS * LANES), f32),
            pltpu.VMEM((CHUNKS * LANES, LANES), f32),
        ],
        compiler_params=params(58),
        cost_estimate=cost(0, 8 << 20),
        name="prep",
    )(negatives, table_t, rel)


def pull_kernel(asked, tab4, out, picked, packed, sem):
    def body(i):
        picked[row(i), :] = tab4[row(asked[i]), :]

    rows_loop(SLOTS, body)
    pack_slots(picked, 0, packed)
    store = pltpu.make_async_copy(packed, out, sem)
    store.start()
    store.wait()


def pull_rows(asked, tab4):
    return pl.pallas_call(
        pull_kernel,
        out_shape=jax.ShapeDtypeStruct((N_DEV * PACK16, LANES), f32),
        in_specs=[SMEM, VMEM],
        out_specs=HBM,
        scratch_shapes=[
            pltpu.VMEM((SLOTS * CHUNKS, LANES), f32),
            pltpu.VMEM((N_DEV * PACK16, LANES), f32),
            pltpu.SemaphoreType.DMA,
        ],
        compiler_params=params(58),
        cost_estimate=cost(0, 8 << 20),
        name="pull_rows",
    )(asked, tab4)


def query_kernel(
    heads, rel_at, tab4, shared,
    q_out, h_out, r_out, back_out, neg_acc,
    tab, rel, packed, n_hi, n_lo, t_hi, t_lo, hb, rb, sems,
):
    step = pl.program_id(0)

    @pl.when(step == 0)
    def _():
        size = N_DEV * PACK66 // PIECES
        loads = [
            pltpu.make_async_copy(shared.at[pl.ds(i * size, size)], packed.at[pl.ds(i * size, size)], sems.at[i])
            for i in range(PIECES)
        ]
        loads.append(pltpu.make_async_copy(tab4, tab, sems.at[PIECES]))
        for load in loads:
            load.start()
        neg_acc[...] = jnp.zeros_like(neg_acc)
        each = N_DEV // PIECES
        for i in range(PIECES):
            loads[i].wait()
            blocks_loop(each, 2, lambda d, i=i: unpack66(packed, (i * each + d) * PACK66, rel, (i * each + d) * PER))
        loads[PIECES].wait()

        for c in range(CHUNKS):
            lanes = slice(c * LANES, (c + 1) * LANES)

            def place(d, carry, c=c):
                rows = pl.ds(pl.multiple_of(d * NEG_DEV, NEG_DEV), NEG_DEV)
                hb[rows, :] = rel[pl.ds(d * PER + REL4 + c, NEG_DEV, stride=CHUNKS), :]
                return carry

            lax.fori_loop(0, N_DEV, place, 0)
            piece = hb[...]
            n_hi[:, lanes], n_lo[:, lanes] = split(piece)
            t_hi[lanes, :], t_lo[lanes, :] = split(piece.T)

    base = step * TILE

    def gather(i):
        hb[row(i), :] = tab[row(heads[base + i]), :]
        rb[row(i), :] = rel[row(rel_at[base + i]), :]

    rows_loop(TILE, gather)
    h = [chunk_of(hb, c, TILE) for c in range(CHUNKS)]
    r = [chunk_of(rb, c, TILE) for c in range(CHUNKS)]
    q = [h[0] * r[0] - h[2] * r[2], h[1] * r[1] - h[3] * r[3], h[0] * r[2] + h[2] * r[0], h[1] * r[3] + h[3] * r[1]]
    for c in range(CHUNKS):
        q_out[c] = q[c]
        h_out[c] = h[c]
        r_out[c] = r[c]
    q = split(jnp.concatenate(q, axis=1))
    negative = dot3(q, (t_hi[...], t_lo[...]), ((1,), (0,)))
    neg_grad = split(jax.nn.sigmoid(negative) * (1.0 / NEG))
    neg_acc[...] += dot3(neg_grad, q, ((0,), (0,)))
    back = dot3(neg_grad, (n_hi[...], n_lo[...]), ((1,), (0,)))
    for c in range(CHUNKS):
        back_out[c] = back[:, c * LANES : (c + 1) * LANES]


PLANE = jax.ShapeDtypeStruct((CHUNKS, E_DEV, LANES), f32)
BLOCK = pl.BlockSpec((CHUNKS, TILE, LANES), lambda i: (0, i, 0))


def queries(heads, rel_at, tab4, shared):
    rows = pltpu.VMEM((TILE * CHUNKS, LANES), f32)
    wide = pltpu.VMEM((NEG, CHUNKS * LANES), bf16)
    tall = pltpu.VMEM((CHUNKS * LANES, NEG), bf16)
    return pl.pallas_call(
        query_kernel,
        grid=(E_DEV // TILE,),
        out_shape=(PLANE, PLANE, PLANE, PLANE, jax.ShapeDtypeStruct((NEG, CHUNKS * LANES), f32)),
        in_specs=[SMEM, SMEM, ANY, ANY],
        out_specs=(BLOCK, BLOCK, BLOCK, BLOCK, pl.BlockSpec((NEG, CHUNKS * LANES), lambda i: (0, 0))),
        scratch_shapes=[
            pltpu.VMEM((ENT_DEV * CHUNKS, LANES), f32),
            pltpu.VMEM((N_DEV * PER, LANES), f32),
            pltpu.VMEM((N_DEV * PACK66, LANES), f32),
            wide,
            wide,
            tall,
            tall,
            rows,
            rows,
            pltpu.SemaphoreType.DMA((PIECES + 1,)),
        ],
        compiler_params=params(58),
        cost_estimate=cost(36_000_000_000, 60 << 20),
        name="queries",
    )(heads, rel_at, tab4, shared)


def tail_kernel(
    tails, tab4, fetched, q_in,
    p_out, tail_local, outgoing,
    ext, ext_grad, packed, tb, sems,
):
    step = pl.program_id(0)
    local = ENT_DEV * CHUNKS
    size = N_DEV * PACK16 // PIECES
    each = N_DEV // PIECES

    @pl.when(step == 0)
    def _():
        loads = []
        for i in range(PIECES):
            here = pl.ds(i * size, size)
            loads.append(pltpu.make_async_copy(fetched.at[here], packed.at[here], sems.at[i]))
        loads.append(pltpu.make_async_copy(tab4, ext.at[pl.ds(0, local)], sems.at[PIECES]))
        for load in loads:
            load.start()
        ext_grad[...] = jnp.zeros_like(ext_grad)
        for i in range(PIECES):
            loads[i].wait()

            def unpack(d, i=i):
                unpack16(packed, (i * each + d) * PACK16, ext, local + (i * each + d) * CAP * CHUNKS)

            blocks_loop(each, 8, unpack)
        loads[PIECES].wait()

    base = step * TAIL_TILE

    def gather(i):
        tb[row(i), :] = ext[row(tails[base + i]), :]

    rows_loop(TAIL_TILE, gather)
    t = [chunk_of(tb, c, TAIL_TILE) for c in range(CHUNKS)]
    q = [q_in[c] for c in range(CHUNKS)]
    score = (q[0] * t[0] + q[1] * t[1]) + (q[2] * t[2] + q[3] * t[3])
    pos_grad = jax.nn.sigmoid(jnp.sum(score, axis=1, keepdims=True)) - 1.0
    for c in range(CHUNKS):
        p_out[c] = pos_grad * t[c]
        tb[pl.ds(c, TAIL_TILE, stride=CHUNKS), :] = pos_grad * q[c]

    def scatter(group):
        i = group * 4
        add_four(ext_grad, [tails[base + i + k] for k in range(4)], [tb[row(i + k), :] for k in range(4)])

    blocks_loop(TAIL_TILE // 4, 8, scatter)

    @pl.when(step == E_DEV // TAIL_TILE - 1)
    def _():
        stores = []
        for i in range(PIECES):
            here = pl.ds(i * size, size)
            stores.append(pltpu.make_async_copy(packed.at[here], outgoing.at[here], sems.at[i]))
        stores.append(pltpu.make_async_copy(ext_grad.at[pl.ds(0, local)], tail_local, sems.at[PIECES]))
        stores[PIECES].start()
        for i in range(PIECES):

            def pack(d, i=i):
                pack16(ext_grad, local + (i * each + d) * CAP * CHUNKS, packed, (i * each + d) * PACK16)

            blocks_loop(each, 8, pack)
            stores[i].start()
        for store in stores:
            store.wait()


TAIL_TILE = 512


def tail_terms(tails, tab4, fetched, q):
    block = pl.BlockSpec((CHUNKS, TAIL_TILE, LANES), lambda i: (0, i, 0))
    return pl.pallas_call(
        tail_kernel,
        grid=(E_DEV // TAIL_TILE,),
        out_shape=(
            PLANE,
            jax.ShapeDtypeStruct((ENT_DEV * CHUNKS, LANES), f32),
            jax.ShapeDtypeStruct((N_DEV * PACK16, LANES), f32),
        ),
        in_specs=[SMEM, ANY, ANY, block],
        out_specs=(block, HBM, HBM),
        scratch_shapes=[
            pltpu.VMEM(((ENT_DEV + SLOTS) * CHUNKS, LANES), f32),
            pltpu.VMEM(((ENT_DEV + SLOTS) * CHUNKS, LANES), f32),
            pltpu.VMEM((N_DEV * PACK16, LANES), f32),
            pltpu.VMEM((TAIL_TILE * CHUNKS, LANES), f32),
            pltpu.SemaphoreType.DMA((PIECES + 1,)),
        ],
        compiler_params=params(58),
        cost_estimate=cost(0, 30 << 20),
        name="tail_terms",
    )(tails, tab4, fetched, q)


def edge_kernel(
    heads, grad_at, core, tail_local, neg_acc, h_in, r_in, p_in, back_in,
    mine, other0, other1, other2, other3, head_grad,
    rel_grad, packed, hb, rb, sems,
):
    step = pl.program_id(0)

    @pl.when(step == 0)
    def _():
        start = pltpu.make_async_copy(tail_local, head_grad, sems.at[0])
        start.start()
        rel_grad[...] = jnp.zeros_like(rel_grad)
        start.wait()

    base = step * EDGE_TILE
    g = [p_in[c] + back_in[c] for c in range(CHUNKS)]
    for k in range(2):
        for buf, src in ((hb, r_in), (rb, h_in)):
            buf[pl.ds(k, EDGE_TILE, stride=CHUNKS), :] = g[k] * src[k] + g[k + 2] * src[k + 2]
            buf[pl.ds(k + 2, EDGE_TILE, stride=CHUNKS), :] = g[k + 2] * src[k] - g[k] * src[k + 2]

    def scatter(pair):
        i = pair * 2
        add_two(head_grad, heads[base + i], heads[base + i + 1], hb[row(i), :], hb[row(i + 1), :])
        add_two(rel_grad, grad_at[base + i], grad_at[base + i + 1], rb[row(i), :], rb[row(i + 1), :])

    rows_loop(EDGE_TILE // 2, scatter)

    @pl.when(step == E_DEV // EDGE_TILE - 1)
    def _():
        def place(d, carry):
            spot = ((d % 2) * CHIPS + d // 2) * PER + REL4
            rows = pl.ds(pl.multiple_of(d * NEG_DEV, NEG_DEV), NEG_DEV)
            for c in range(CHUNKS):
                rel_grad[pl.ds(spot + c, NEG_DEV, stride=CHUNKS), :] = neg_acc[rows, c * LANES : (c + 1) * LANES]
            return carry

        lax.fori_loop(0, N_DEV, place, 0)
        side = core[0]
        size = CHIPS * PACK66 // PIECES
        stores = [
            pltpu.make_async_copy(packed.at[pl.ds(i * size, size)], other, sems.at[i])
            for i, other in enumerate((other0, other1, other2, other3))
        ]
        stores.append(pltpu.make_async_copy(packed.at[pl.ds(PIECES * size, PIECES * size)], mine, sems.at[PIECES]))

        def pack(d, owner, first):
            pack66(rel_grad, (owner * CHIPS + d) * PER, packed, (first + d) * PACK66)

        chips = CHIPS // PIECES
        for i in range(PIECES):
            blocks_loop(chips, 2, lambda d, i=i: pack(i * chips + d, 1 - side, 0))
            stores[i].start()
        blocks_loop(CHIPS, 2, lambda d: pack(d, side, CHIPS))
        stores[PIECES].start()
        for store in stores:
            store.wait()


EDGE_TILE = 256


def gradients(heads, grad_at, core, tail_local, neg_acc, h, r, p, back):
    half = jax.ShapeDtypeStruct((CHIPS * PACK66, LANES), f32)
    piece = jax.ShapeDtypeStruct((CHIPS * PACK66 // PIECES, LANES), f32)
    block = pl.BlockSpec((CHUNKS, EDGE_TILE, LANES), lambda i: (0, i, 0))
    whole = pl.BlockSpec((ENT_DEV * CHUNKS, LANES), lambda i: (0, 0))
    return pl.pallas_call(
        edge_kernel,
        grid=(E_DEV // EDGE_TILE,),
        out_shape=(half, piece, piece, piece, piece, jax.ShapeDtypeStruct((ENT_DEV * CHUNKS, LANES), f32)),
        in_specs=[SMEM, SMEM, SMEM, ANY, pl.BlockSpec((NEG, CHUNKS * LANES), lambda i: (0, 0)), block, block, block, block],
        out_specs=(HBM,) * 5 + (whole,),
        scratch_shapes=[
            pltpu.VMEM((N_DEV * PER, LANES), f32),
            pltpu.VMEM((N_DEV * PACK66, LANES), f32),
            pltpu.VMEM((EDGE_TILE * CHUNKS, LANES), f32),
            pltpu.VMEM((EDGE_TILE * CHUNKS, LANES), f32),
            pltpu.SemaphoreType.DMA((PIECES + 1,)),
        ],
        compiler_params=params(58),
        cost_estimate=cost(0, 1 << 20),
        name="gradients",
    )(heads, grad_at, core, tail_local, neg_acc, h, r, p, back)


def merge_kernel(
    color, mine, got0, got1, got2, got3,
    keep, send0, send1, send2, send3, send4,
    total, came, sems, came_sems,
):
    each = CHIPS // PIECES
    loads, arrivals = [], []
    for i, got in enumerate((got0, got1, got2, got3)):
        here = pl.ds(i * each, each)
        loads.append(pltpu.make_async_copy(mine.at[here], total.at[here], sems.at[i]))
        arrivals.append(pltpu.make_async_copy(got, came.at[here], came_sems.at[i]))
        loads[i].start()
        arrivals[i].start()
    own = pl.ds(pl.multiple_of(color[0] * KEPT, 8), KEPT)
    theirs = pl.ds(pl.multiple_of((1 - color[0]) * KEPT, 8), KEPT)
    stores = [
        pltpu.make_async_copy(total.at[pl.ds(first, last - first), theirs], send, sems.at[PIECES + i])
        for i, (first, last, send) in enumerate(
            zip(GROUPS[:-1], GROUPS[1:], (send0, send1, send2, send3, send4), strict=True)
        )
    ]
    stores.append(pltpu.make_async_copy(total.at[:, own], keep, sems.at[PIECES + WAYS]))
    started = 0
    for i in range(PIECES):
        loads[i].wait()
        arrivals[i].wait()

        def add(d, carry, i=i):
            total[i * each + d] = total[i * each + d] + came[i * each + d]
            return carry

        lax.fori_loop(0, each, add, 0)
        while started < WAYS and GROUPS[started + 1] <= (i + 1) * each:
            stores[started].start()
            started += 1
    stores[WAYS].start()
    for store in stores:
        store.wait()


def merge(color, mine, got):
    def blocks(n, rows):
        return jax.ShapeDtypeStruct((n, rows, LANES), f32)

    return pl.pallas_call(
        merge_kernel,
        out_shape=(blocks(CHIPS, KEPT),) + tuple(blocks(b - a, KEPT) for a, b in zip(GROUPS[:-1], GROUPS[1:], strict=True)),
        in_specs=[SMEM, ANY] + [ANY] * PIECES,
        out_specs=(HBM,) * (WAYS + 1),
        scratch_shapes=[
            pltpu.VMEM((CHIPS, PACK66, LANES), f32),
            pltpu.VMEM((CHIPS, PACK66, LANES), f32),
            pltpu.SemaphoreType.DMA((PIECES + WAYS + 1,)),
            pltpu.SemaphoreType.DMA((PIECES,)),
        ],
        compiler_params=params(58),
        cost_estimate=cost(0, 1 << 16),
        name="merge",
    )(color, mine.reshape(CHIPS, PACK66, LANES), *[x.reshape(CHIPS // PIECES, PACK66, LANES) for x in got])


def meet_kernel(keep, got0, got1, got2, got3, got4, out, total, sems):
    spans = list(zip(GROUPS[:-1], GROUPS[1:], (got0, got1, got2, got3, got4), strict=True))
    loads, stores = [], []
    for i, (first, last, _) in enumerate(spans):
        here = pl.ds(first, last - first)
        loads.append(pltpu.make_async_copy(keep.at[here], total.at[here], sems.at[i]))
        stores.append(pltpu.make_async_copy(total.at[here], out.at[here], sems.at[WAYS + i]))
        loads[i].start()
    for i, (first, last, got) in enumerate(spans):
        loads[i].wait()

        def add(d, carry, first=first, got=got):
            total[first + d] = total[first + d] + got[d]
            return carry

        lax.fori_loop(0, last - first, add, 0)
        stores[i].start()
    for store in stores:
        store.wait()


def meet(keep, got):
    return pl.pallas_call(
        meet_kernel,
        out_shape=jax.ShapeDtypeStruct((CHIPS, KEPT, LANES), f32),
        in_specs=[ANY] + [VMEM] * WAYS,
        out_specs=HBM,
        scratch_shapes=[pltpu.VMEM((CHIPS, KEPT, LANES), f32), pltpu.SemaphoreType.DMA((2 * WAYS,))],
        compiler_params=params(47),
        cost_estimate=cost(0, 1 << 16),
        name="meet",
    )(keep, *got)


def color_of(chip):
    return (chip // 16 + chip // 4 + chip) % 2


def matching(k):
    pairs = []
    for chip in range(CHIPS):
        if color_of(chip) == 0:
            at = [chip // 16, chip // 4 % 4, chip % 4]
            at[k // 2] = (at[k // 2] + (1 if k % 2 == 0 else 3)) % 4
            mate = (at[0] * 4 + at[1]) * 4 + at[2]
            pairs += [(chip, mate), (mate, chip)]
    return pairs


def returned_kernel(asked, packed, head_grad, out, returned):
    out[...] = head_grad[...]
    unpack_slots(packed, returned, 0)

    def body(pair):
        i = pair * 2
        add_two(out, asked[i], asked[i + 1], returned[row(i), :], returned[row(i + 1), :])

    rows_loop(SLOTS // 2, body)


def add_returned(asked, returned, head_grad):
    return pl.pallas_call(
        returned_kernel,
        out_shape=jax.ShapeDtypeStruct((ENT_DEV * CHUNKS, LANES), f32),
        in_specs=[SMEM, VMEM, VMEM],
        out_specs=VMEM,
        scratch_shapes=[pltpu.VMEM((SLOTS * CHUNKS, LANES), f32)],
        compiler_params=params(24),
        cost_estimate=cost(0, 10 << 20),
        name="add_returned",
    )(asked, returned, head_grad)


def adagrad(grad, n, table_t, state, new_table_t, new_state):
    g = [chunk_of(grad, c, n).T for c in range(CHUNKS)]
    squares = (g[0] * g[0] + g[1] * g[1]) + (g[2] * g[2] + g[3] * g[3])
    state_now = state[...] + jnp.sum(squares, axis=0, keepdims=True) * (1.0 / WIDTH)
    new_state[...] = state_now
    below = jnp.sqrt(state_now) + 1e-10
    for c, (start, size) in enumerate(SPANS):
        spot = slice(start, start + size)
        new_table_t[spot, :] = table_t[spot, :] - rate * g[c][:size] / below


def step_kernel(
    negatives, local_grad, parts, table_now, state, rel, rel_state,
    new_table_t, new_state, new_rel, new_rel_state,
    grad, came, table_t, share, packed, wide, rel_t, new_rel_t, states, new_states, sems,
):
    each = CHIPS // PIECES
    loads = []
    for i in range(PIECES):
        here = pl.ds(i * each, each)
        loads.append(pltpu.make_async_copy(parts.at[here], came.at[here], sems.at[i]))
    loads.append(pltpu.make_async_copy(local_grad, grad, sems.at[PIECES]))
    loads.append(pltpu.make_async_copy(table_now, table_t, sems.at[PIECES + 1]))
    for load in loads:
        load.start()
    share[...] = jnp.zeros_like(share)
    turn_relations(rel, wide, rel_t)
    new_rel_t[...] = jnp.zeros_like(new_rel_t)
    states[...] = jnp.zeros_like(states)
    states[:, 0:REL_DEV] = rel_state[...]
    totals = [None, None]
    for i in range(PIECES):
        loads[i].wait()
        for chip in range(i * each, (i + 1) * each):
            half = color_of(chip)
            totals[half] = came[chip] if totals[half] is None else totals[half] + came[chip]
    packed[0:KEPT, :] = totals[0]
    packed[KEPT:PACK66, :] = totals[1]
    unpack66(packed, 0, share, 0)
    adagrad(share, LANES, rel_t, states, new_rel_t, new_states)
    new_rel[...] = new_rel_t[...].T[0:REL_DEV, 0:WIDTH]
    new_rel_state[...] = new_states[:, 0:REL_DEV]
    loads[PIECES].wait()
    for i in range(NEG_DEV):
        at = row(negatives[i])
        grad[at, :] = grad[at, :] + share[REL4 + CHUNKS * i : REL4 + CHUNKS * (i + 1), :]
    loads[PIECES + 1].wait()
    adagrad(grad, ENT_DEV, table_t, state, new_table_t, new_state)


def adagrad_step(negatives, local_grad, parts, table_t, state, rel, rel_state):
    def like(*shape):
        return jax.ShapeDtypeStruct(shape, f32)

    return pl.pallas_call(
        step_kernel,
        out_shape=(like(WIDTH, ENT_DEV), like(1, ENT_DEV), like(REL_DEV, WIDTH), like(1, REL_DEV)),
        in_specs=[SMEM, ANY, ANY, ANY] + [VMEM] * 3,
        out_specs=(VMEM,) * 4,
        scratch_shapes=[
            pltpu.VMEM((ENT_DEV * CHUNKS, LANES), f32),
            pltpu.VMEM((CHIPS, KEPT, LANES), f32),
            pltpu.VMEM((WIDTH, ENT_DEV), f32),
            pltpu.VMEM((CHUNKS * LANES, LANES), f32),
            pltpu.VMEM((PACK66, LANES), f32),
            pltpu.VMEM((LANES, CHUNKS * LANES), f32),
            pltpu.VMEM((CHUNKS * LANES, LANES), f32),
            pltpu.VMEM((CHUNKS * LANES, LANES), f32),
            pltpu.VMEM((1, LANES), f32),
            pltpu.VMEM((1, LANES), f32),
            pltpu.SemaphoreType.DMA((PIECES + 2,)),
        ],
        compiler_params=params(58),
        cost_estimate=cost(0, 16 << 20),
        name="adagrad_step",
    )(negatives, local_grad, parts, table_t, state, rel, rel_state)


def local(
    entity_table,
    entity_state,
    relation_table,
    relation_state,
    heads,
    relations,
    tails,
    pull_lists,
    negatives,
):
    table_t = entity_table.T
    owner, place = relations // REL_DEV, relations % REL_DEV
    rel_at = owner * (REL_DEV + NEG_DEV) + place
    grad_at = ((owner % 2) * CHIPS + owner // 2) * (REL_DEV + NEG_DEV) + place
    core = lax.axis_index("c")

    tab4, send = prep(negatives, table_t, relation_table)
    shared = lax.all_gather(send, AXES, axis=0, tiled=True)
    asked = lax.all_to_all(pull_lists, AXES, split_axis=0, concat_axis=0, tiled=True).reshape(SLOTS)
    rows_out, shared = lax.optimization_barrier((pull_rows(asked, tab4), shared))

    def exchange(rows):
        rows = rows.reshape(N_DEV, PACK16, LANES)
        return lax.all_to_all(rows, AXES, split_axis=0, concat_axis=0, tiled=True).reshape(N_DEV * PACK16, LANES)

    fetched = exchange(rows_out)
    q, h, r, back, neg_acc = queries(heads, rel_at, tab4, shared)
    p, tail_local, outgoing = tail_terms(tails, tab4, fetched, q)
    returned = exchange(outgoing)
    mine, *others, head_grad = gradients(
        heads, grad_at, core.reshape(1), tail_local, neg_acc, h, r, p, back
    )
    color = (lax.axis_index("x") + lax.axis_index("z") + lax.axis_index("y")) % 2
    got = [lax.ppermute(other, "c", [(0, 1), (1, 0)]) for other in others]
    merged = merge(color.reshape(1), mine, got)
    (keep, *sends), returned = lax.optimization_barrier((merged, returned))
    met = meet(keep, [lax.ppermute(send, AXES[:3], matching(k)) for k, send in enumerate(sends)])
    parts = lax.all_to_all(met, AXES[:3], split_axis=0, concat_axis=0, tiled=True)
    local_grad = add_returned(asked, returned, head_grad)
    new_table_t, new_state, new_rel, new_rel_state = adagrad_step(
        negatives,
        local_grad,
        parts,
        table_t,
        entity_state.reshape(1, ENT_DEV),
        relation_table,
        relation_state.reshape(1, REL_DEV),
    )
    return (
        new_table_t.T,
        new_state.reshape(ENT_DEV),
        new_rel,
        new_rel_state.reshape(REL_DEV),
    )


def solution(mesh):
    grid = Mesh(mesh.devices.reshape(4, 4, 4, 2), AXES)
    rows, flat = P(AXES, None), P(AXES)
    in_specs = (rows, flat, rows, flat, flat, flat, flat, rows, flat)
    out_specs = (rows, flat, rows, flat)
    return jax.shard_map(local, mesh=grid, in_specs=in_specs, out_specs=out_specs, check_vma=False)
```
